32 devices in a mesh: grp: 2 (over y), row: 4 (over x, core), col: 4 (over z).
Axes of the slice: x: 2, y: 2, z: 4, core: 2. Of those that a mesh axis runs over, the one named last changes fastest.
Arguments:
- video: bfloat16 [514, 32, 512], P('grp', 'row', 'col'), parts along dimension 0, may hold values from -6 to 6, as said below
- filters: float32 [4, 2, 7, 7], replicated, may hold values from -0.875 to 0.875
- start_basis: float32 [256, 64], replicated, may hold values from -6 to 6
Outputs:
- basis: float32 [512, 64], P('grp'), parts along dimension 0
- modes: float32 [16, 128, 256], P(('grp', 'row'), 'col'), parts along dimension 0
The draws below stay inside these ranges and needn't reach their ends.
There are 2 independent parts, one for each index of `grp`. The reference program is written for one: setup_inputs(seed, part) draws one part's arguments, and reference() takes and returns one part's arrays. A program takes and returns all parts, laid end to end along the dimension named above; an argument that names none is the same for every part. Nothing has to cross between parts.
Inputs may be any that keep to these rules, and one draw needn't show every extreme that they name: `video`: grey levels: a fixed texture plus a per-pixel oscillation in time.
All inputs are finite; a program needn't handle non-finite values.
Results may differ from the reference program's by a relative error of at most 0.0034.
Values may be sent and summed in bfloat16 or wider, within the bound.
No kernel may reach another device: no remote copies, remote signals or barrier semaphores. Data moves between devices by JAX's collectives and lax.ppermute only.
A program may use at most 64 MiB of HBM per device.

```python
import math
import jax
import jax.numpy as jnp
from jax import lax

FRAMES = 256
MODES = 64
ORIENT = 4
TAPS = 7
SWEEPS = 2
HEIGHT = 32
WIDTH = 512
NPIX = 4096


def draw_video(key, part):
    keys = jax.random.split(jax.random.fold_in(key, 17), 4)
    rows_pos = jnp.arange(HEIGHT, dtype=jnp.float32)[:, None]
    texture = jnp.clip(jax.random.normal(keys[0], (HEIGHT, WIDTH), jnp.float32), -3.0, 3.0)
    amplitude = jnp.exp(jax.random.uniform(keys[1], (HEIGHT, WIDTH), jnp.float32, math.log(0.2), 0.0))
    amplitude = amplitude * (1.0 + 2.0 * rows_pos / HEIGHT)
    omega = jnp.exp(jax.random.uniform(keys[2], (HEIGHT, WIDTH), jnp.float32, math.log(0.05), math.log(2.0)))
    phase = jax.random.uniform(keys[3], (HEIGHT, WIDTH), jnp.float32, -math.pi, math.pi)
    times = jnp.arange(FRAMES + 1, dtype=jnp.float32)[:, None, None]
    return (texture[None] + amplitude[None] * jnp.sin(omega[None] * times + phase[None])).astype(jnp.bfloat16)


def normal_values(key, dims, scale, bound, held_as=jnp.bfloat16):
    array = scale * jax.random.normal(key, dims, jnp.float32)
    return jnp.clip(array, min=-bound, max=bound).astype(held_as)


def setup_inputs(seed: int = 0, part: int = 0) -> dict:
    streams_of = jax.random.split(jax.random.key(seed), 4)
    part_splits = jax.random.split(jax.random.fold_in(streams_of[3], part), 4)
    return {
        "video": draw_video(jax.random.fold_in(jax.random.fold_in(streams_of[3], part), 71), part),
        "filters": normal_values(streams_of[1], (ORIENT, 2, TAPS, TAPS), (TAPS * TAPS) ** -0.5, 0.875, jnp.float32),
        "start_basis": normal_values(streams_of[2], (FRAMES, MODES), 1.0, 6.0, jnp.float32),
    }


def orthonormal(stacked):
    inner = jnp.dot(stacked.T, stacked, precision=lax.Precision.HIGHEST)
    factor = jnp.linalg.cholesky(inner)
    return lax.linalg.triangular_solve(factor, stacked, left_side=False, lower=True, transpose_a=True)

def reference(video, filters, start_basis):
    height = video.shape[1]
    width = video.shape[2]
    kernels = filters.reshape(2 * ORIENT, 1, TAPS, TAPS).astype(jnp.float32)

    def respond(frame):
        lifted = frame.astype(jnp.float32)[None, None]
        return lax.conv_general_dilated(lifted, kernels, (1, 1), ((3, 3), (3, 3)), precision=lax.Precision.HIGHEST)[0]

    def advance(previous, frame):
        current = respond(frame)
        real_now = current[0::2]
        imag_now = current[1::2]
        real_old = previous[0::2]
        imag_old = previous[1::2]
        prod_real = real_now * real_old + imag_now * imag_old
        prod_imag = imag_now * real_old - real_now * imag_old
        motion = prod_imag / jnp.sqrt(prod_real * prod_real + prod_imag * prod_imag + 1.0)
        pooled = motion.reshape(ORIENT, height // 4, 4, width // 4, 4).mean(axis=(2, 4))
        return (current, pooled.astype(jnp.bfloat16))
    unused, feats = lax.scan(advance, respond(video[0]), video[1:])
    flat = feats.reshape(FRAMES, -1)
    gram = jnp.dot(flat.astype(jnp.float32), flat.T.astype(jnp.float32), preferred_element_type=jnp.float32) / NPIX
    basis_now = start_basis.astype(jnp.float32)
    for sweep in range(SWEEPS):
        basis_now = orthonormal(jnp.dot(gram, basis_now, precision=lax.Precision.HIGHEST))
    projected = jnp.dot(basis_now.astype(jnp.bfloat16).T.astype(jnp.float32), flat.astype(jnp.float32), preferred_element_type=jnp.float32)
    fields = projected.reshape(MODES, ORIENT, height // 4, width // 4)
    modes = jnp.transpose(fields, (2, 3, 1, 0)).reshape(height // 4, width // 4, ORIENT * MODES)
    return (basis_now, modes)
```

```python
import functools

import jax
import jax.numpy as jnp
from jax import lax
from jax.experimental import pallas as pl
from jax.experimental.pallas import tpu as pltpu
from jax.sharding import PartitionSpec as P

FRAMES = 256
HALF = FRAMES // 2
MODES = 64
ORIENT = 4
TAPS = 7
REACH = 3
SWEEPS = 2
ROWS = 8
COLS = 128
BLOCKS = 16
F32 = jnp.float32
BF16 = jnp.bfloat16
HIGHEST = lax.Precision.HIGHEST
PARAMS = pltpu.CompilerParams(vmem_limit_bytes=48 * 1024 * 1024)
VMEM = pl.BlockSpec(memory_space=pltpu.VMEM)
SMEM = pl.BlockSpec(memory_space=pltpu.SMEM)


def spread(rows_ref, out_ref):
    for pair in range(ROWS // 2):
        for group in range(3):
            parts = []
            for row in (2 * pair, 2 * pair + 1):
                tile = rows_ref[pl.ds(group * ROWS + row, HALF, stride=2 * ROWS), :]
                parts.append(tile.T.reshape(BLOCKS, 8, HALF))
            both = jnp.concatenate(parts, axis=1).astype(BF16)
            out_ref[:, 16 * pair : 16 * pair + 16, HALF * group : HALF * (group + 1)] = both


def own_kernel(video_ref, taps_ref, own_ref, band_ref, rows_ref):
    rows_ref[...] = video_ref[...].astype(F32).reshape(rows_ref.shape)
    spread(rows_ref, own_ref)
    taps = taps_ref[...]
    high = taps.astype(BF16)
    low = (taps - high.astype(F32)).astype(BF16)
    parts = jnp.concatenate([high, low], axis=0)
    tap = lax.broadcasted_iota(jnp.int32, (128, 256), 0)
    lane = lax.broadcasted_iota(jnp.int32, (128, 256), 1)
    slot = (lane >> 3) & 15
    column = ((lane >> 7) << 3) | (lane & 7)
    slot_hit = slot == ((((tap >> 3) & 7) - REACH) & 15)
    ahead = column - (tap & 7) - 1 - 4 * (tap >> 6)
    for j in range(4):
        select = jnp.where(slot_hit & (ahead == j), 1.0, 0.0).astype(BF16)
        base = jnp.dot(parts, select, preferred_element_type=F32)
        for i in range(ROWS):
            start = (4 * i + j) * 16
            for side in range(2):
                rolled = base[:, 128 * side : 128 * side + 128]
                if i:
                    rolled = pltpu.roll(rolled, 8 * i, 1)
                rolled = rolled.astype(BF16)
                for part in range(2):
                    at = 256 * part + 128 * side
                    band_ref[start : start + 16, at : at + 128] = rolled[16 * part : 16 * part + 16]


def halo_kernel(parity_ref, a_ref, b_ref, own_ref, halo_ref, edge_a_ref, edge_b_ref, rows_ref):
    even = parity_ref[0] == 0
    got_a = a_ref[...].astype(F32)
    got_b = b_ref[...].astype(F32)
    below = jnp.where(even, got_a, got_b)
    above = jnp.where(even, got_b, got_a)
    none = jnp.zeros((FRAMES + 1, 2, COLS), F32)
    rows_ref[...] = jnp.concatenate([below, none, above], axis=1).reshape(rows_ref.shape)
    spread(rows_ref, halo_ref)
    block_a = (BLOCKS - 1) * (1 - parity_ref[1])
    block_b = (BLOCKS - 1) * parity_ref[1]
    edge_a_ref[0:64] = own_ref[block_a]
    edge_a_ref[64:128] = halo_ref[block_a]
    edge_b_ref[0:64] = own_ref[block_b]
    edge_b_ref[64:128] = halo_ref[block_b]


def block_feats(band_ref, window):
    pooled = []
    for cell in range(2):
        rows = slice(256 * cell, 256 * cell + 256)
        resp = jnp.dot(band_ref[rows, 0:256], window, preferred_element_type=F32)
        resp = resp + jnp.dot(band_ref[rows, 256:512], window, preferred_element_type=F32)
        total = jnp.zeros((8, FRAMES), F32)
        for pixel in range(16):
            real = resp[16 * pixel : 16 * pixel + 8]
            imag = resp[16 * pixel + 8 : 16 * pixel + 16]
            real_old, real_now = real[:, :FRAMES], real[:, HALF:]
            imag_old, imag_now = imag[:, :FRAMES], imag[:, HALF:]
            prod_real = real_now * real_old + imag_now * imag_old
            prod_imag = imag_now * real_old - real_now * imag_old
            total += prod_imag * lax.rsqrt(prod_real * prod_real + prod_imag * prod_imag + 1.0)
        pooled.append(total * (1.0 / 16.0))
    return jnp.concatenate(pooled, axis=0)


def inner_kernel(band_ref, own_ref, halo_ref, feats_ref):
    def body(block, carry):
        window = jnp.concatenate(
            [own_ref[block], halo_ref[block], own_ref[block + 1], halo_ref[block + 1]], axis=0
        )
        feats_ref[block] = block_feats(band_ref, window).astype(BF16)
        return carry

    lax.fori_loop(0, BLOCKS - 1, body, 0)


def edge_kernel(parity_ref, band_ref, own_ref, halo_ref, a_ref, b_ref, inner_ref, feats_ref, mine_ref, other_ref):
    even = parity_ref[1] == 0
    got_a = a_ref[...]
    got_b = b_ref[...]
    right = jnp.where(even, got_a, got_b)
    left = jnp.where(even, got_b, got_a)
    window_left = jnp.concatenate([left, own_ref[0], halo_ref[0]], axis=0)
    window_right = jnp.concatenate([own_ref[BLOCKS - 1], halo_ref[BLOCKS - 1], right], axis=0)
    feats_left = block_feats(band_ref, window_left)
    feats_right = block_feats(band_ref, window_right)
    second = (lax.broadcasted_iota(jnp.int32, (16, FRAMES), 0) & 4) == 4
    feats_ref[0 : BLOCKS - 1] = inner_ref[0 : BLOCKS - 1]
    feats_ref[BLOCKS - 1] = jnp.where(second, feats_left, feats_right).astype(BF16)
    flat = feats_ref[...].reshape(16 * BLOCKS, FRAMES)
    gram = lax.dot_general(flat, flat, (((0,), (0,)), ((), ())), preferred_element_type=F32)
    top, cross, low = gram[:HALF, :HALF], gram[:HALF, HALF:], gram[HALF:, HALF:]
    i = lax.broadcasted_iota(jnp.int32, (HALF, HALF), 0)
    j = lax.broadcasted_iota(jnp.int32, (HALF, HALF), 1)
    folded = jnp.where(i <= j, top, low)
    diagonal = jnp.sum(jnp.where(i == j, low, 0.0), axis=0, keepdims=True)
    first = parity_ref[0] == 0
    spare = jnp.broadcast_to(diagonal, (8, HALF))
    mine_ref[0:HALF] = jnp.where(first, cross, folded)
    mine_ref[HALF : HALF + 8] = spare
    other_ref[0:HALF] = jnp.where(first, folded, cross)
    other_ref[HALF : HALF + 8] = spare


def inverse_factor(inner):
    count = MODES // 8
    i = lax.broadcasted_iota(jnp.int32, (MODES, MODES), 0)
    j = lax.broadcasted_iota(jnp.int32, (MODES, MODES), 1)
    work = jnp.concatenate([jnp.where(i == j, 1.0, 0.0), inner], axis=1)
    work = [work[8 * v : 8 * v + 8] for v in range(count)]
    sub = lax.broadcasted_iota(jnp.int32, (8, 2 * MODES), 0)
    scale = [jnp.zeros((8, 2 * MODES), F32) for v in range(count)]
    for k in range(MODES):
        v0, s = divmod(k, 8)
        pivot_row = work[v0][s : s + 1, :]
        pivot = pivot_row[:, MODES + k : MODES + k + 1]
        scaled = pivot_row * (1.0 / pivot)
        scale[v0] = jnp.where(sub == s, lax.rsqrt(pivot), scale[v0])
        for v in range(v0, count):
            factor = work[v][:, MODES + k : MODES + k + 1]
            change = factor * scaled
            if v == v0:
                change = jnp.where(sub > s, change, 0.0)
            work[v] = work[v] - change
    return jnp.concatenate([work[v] * scale[v] for v in range(count)], axis=0)[:, :MODES]


def basis_kernel(scale, parity_ref, mine_ref, other_ref, start_ref, feats_ref, basis_ref, modes_ref, rows_ref, out_ref):
    first = parity_ref[0] == 0
    mine, other = mine_ref[...], other_ref[...]
    cross = jnp.where(first, mine, other)[:HALF]
    second = jnp.where(first, other, mine)
    folded = second[:HALF]
    i = lax.broadcasted_iota(jnp.int32, (HALF, HALF), 0)
    j = lax.broadcasted_iota(jnp.int32, (HALF, HALF), 1)
    turned = folded.T
    top = jnp.where(i <= j, folded, turned)
    low = jnp.where(i > j, folded, jnp.where(i < j, turned, second[HALF : HALF + 1]))
    gram = jnp.concatenate(
        [jnp.concatenate([top, cross], axis=1), jnp.concatenate([cross.T, low], axis=1)], axis=0
    )
    gram = gram * scale
    start = start_ref[...]
    rows_ref[...] = jnp.concatenate([start, start], axis=1)
    basis = jnp.concatenate([rows_ref[pl.ds(g, HALF, stride=2), :].T for g in range(2)], axis=1)[:MODES]
    for sweep in range(SWEEPS):
        stacked = jnp.dot(basis, gram, precision=HIGHEST, preferred_element_type=F32)
        inner = lax.dot_general(
            stacked, stacked, (((1,), (1,)), ((), ())), precision=HIGHEST, preferred_element_type=F32
        )
        basis = jnp.dot(inverse_factor(inner), stacked, precision=HIGHEST, preferred_element_type=F32)
    twice = jnp.concatenate([basis, basis], axis=0)
    for g in range(2):
        rows_ref[pl.ds(g, HALF, stride=2), :] = twice[:, HALF * g : HALF * g + HALF].T
    basis_ref[...] = rows_ref[:, :MODES]
    flat = feats_ref[...].reshape(16 * BLOCKS, FRAMES)
    rows_ref[...] = lax.dot_general(
        flat, twice.astype(BF16), (((1,), (1,)), ((), ())), preferred_element_type=F32
    )
    left = lax.broadcasted_iota(jnp.int32, (BLOCKS, 2 * MODES), 1) < MODES
    for row in range(2):
        for half in range(2):
            for cell in range(2):
                at = 8 * row + 4 * cell + 2 * half
                field = jnp.where(
                    left, rows_ref[pl.ds(at, BLOCKS, stride=16), :], rows_ref[pl.ds(at + 1, BLOCKS, stride=16), :]
                )
                if cell:
                    field = pltpu.roll(field, 1, 0)
                out_ref[pl.ds(64 * row + 32 * half + 1 - cell, BLOCKS, stride=2), :] = field
            modes_ref[row, :, 128 * half : 128 * half + 128] = out_ref[64 * row + 32 * half : 64 * row + 32 * half + 32]


def call(kernel, outs, n_smem, n_in, scratch=()):
    return pl.pallas_call(
        kernel,
        out_shape=[jax.ShapeDtypeStruct(shape, dtype) for shape, dtype in outs],
        in_specs=[SMEM] * n_smem + [VMEM] * (n_in - n_smem),
        out_specs=[VMEM] * len(outs),
        scratch_shapes=list(scratch),
        compiler_params=PARAMS,
    )


def pairs(size, start):
    swaps = []
    for i in range(start, size - 1, 2):
        swaps += [(i, i + 1), (i + 1, i)]
    return swaps


def on_device(video, filters, start_basis):
    size_row, size_col = lax.axis_size("row"), lax.axis_size("col")
    parity = jnp.stack([lax.axis_index("row") % 2, lax.axis_index("col") % 2]).astype(jnp.int32)
    even_row = parity[0] == 0

    first, last = video[:, :REACH, :], video[:, ROWS - REACH :, :]
    got_a = lax.ppermute(jnp.where(even_row, last, first), "row", pairs(size_row, 0))
    got_b = lax.ppermute(jnp.where(even_row, first, last), "row", pairs(size_row, 1))

    taps = jnp.pad(filters, ((0, 0), (0, 0), (0, 1), (0, 1))).reshape(ORIENT, 2, 64)
    taps = jnp.transpose(taps, (1, 0, 2))[:, None, :, None, :] * jnp.eye(2, dtype=F32)[None, :, None, :, None]
    taps = taps.reshape(16, 128)
    rows = pltpu.VMEM(((FRAMES + 1) * ROWS, COLS), F32)
    tile = ((BLOCKS, 64, 3 * HALF), BF16)
    edge = ((128, 3 * HALF), BF16)
    own, band = call(own_kernel, [tile, ((512, 512), BF16)], 0, 2, [rows])(video, taps)
    halo, edge_a, edge_b = call(halo_kernel, [tile, edge, edge], 1, 4, [rows])(parity, got_a, got_b, own)
    got_a = lax.ppermute(edge_a, "col", pairs(size_col, 0))
    got_b = lax.ppermute(edge_b, "col", pairs(size_col, 1))
    feats_shape = ((BLOCKS, 16, FRAMES), BF16)
    (inner,) = call(inner_kernel, [feats_shape], 0, 3)(band, own, halo)
    part = ((HALF + 8, HALF), F32)
    feats, mine, other = call(edge_kernel, [feats_shape, part, part], 1, 7)(
        parity, band, own, halo, got_a, got_b, inner
    )

    mine = mine + lax.ppermute(other, "row", pairs(size_row, 0))
    for axis, size, step in (("row", size_row, 2), ("col", size_col, 1)):
        while step < size:
            mine = mine + lax.ppermute(mine, axis, [(i, i ^ step) for i in range(size)])
            step *= 2
    other = lax.ppermute(mine, "row", pairs(size_row, 0))

    features = ORIENT * (size_row * ROWS // 4) * (size_col * COLS // 4)
    kernel = functools.partial(basis_kernel, 1.0 / features)
    return tuple(
        call(
            kernel,
            [((FRAMES, MODES), F32), ((ROWS // 4, COLS // 4, ORIENT * MODES), F32)],
            1,
            5,
            [pltpu.VMEM((FRAMES, 2 * MODES), F32), pltpu.VMEM((128, 128), F32)],
        )(parity, mine, other, start_basis, feats)
    )


def solution(mesh):
    return jax.shard_map(
        on_device,
        mesh=mesh,
        in_specs=(P("grp", "row", "col"), P(), P()),
        out_specs=(P("grp", None), P(("grp", "row"), "col", None)),
        check_vma=False,
    )
```

```python
import functools

import jax
import jax.numpy as jnp
from jax import lax
from jax.experimental import pallas as pl
from jax.experimental.pallas import tpu as pltpu
from jax.sharding import PartitionSpec as P

FRAMES = 256
HALF = FRAMES // 2
MODES = 64
ORIENT = 4
TAPS = 7
REACH = 3
SWEEPS = 2
ROWS = 8
COLS = 128
BLOCKS = 16
F32 = jnp.float32
BF16 = jnp.bfloat16
HIGHEST = lax.Precision.HIGHEST
PARAMS = pltpu.CompilerParams(vmem_limit_bytes=48 * 1024 * 1024)
VMEM = pl.BlockSpec(memory_space=pltpu.VMEM)
SMEM = pl.BlockSpec(memory_space=pltpu.SMEM)


def turned(rows_ref, row, group):
    return rows_ref[pl.ds(group * ROWS + row, HALF, stride=2 * ROWS), :].T


def blocked(upper, lower):
    both = [part.reshape(BLOCKS, 8, HALF) for part in (upper, lower)]
    return jnp.concatenate(both, axis=1).astype(BF16)


def own_kernel(parity_ref, video_ref, send_a_ref, send_b_ref, x_ref, rim_ref, rows_ref):
    even = parity_ref[0] == 0
    rows_ref[...] = video_ref[...].astype(F32).reshape(rows_ref.shape)
    for group in range(3):
        lanes = slice(HALF * group, HALF * group + HALF)
        tiles = [turned(rows_ref, row, group) for row in range(ROWS)]
        if group < 2:
            for i in range(REACH):
                first, last = tiles[i], tiles[ROWS - REACH + i]
                at = slice(COLS * i, COLS * i + COLS)
                send_a_ref[at, lanes] = jnp.where(even, last, first).astype(BF16)
                send_b_ref[at, lanes] = jnp.where(even, first, last).astype(BF16)
        for pair in range(3):
            x_ref[:, 32 + 16 * pair : 48 + 16 * pair, lanes] = blocked(tiles[2 * pair + 1], tiles[2 * pair + 2])
        rim_ref[0, :, lanes] = tiles[0]
        rim_ref[1, :, lanes] = tiles[ROWS - 1]
    final = rows_ref[FRAMES * ROWS : FRAMES * ROWS + ROWS, :]
    shifted = pltpu.roll(final, REACH, 0)
    fill = jnp.zeros((8, COLS), F32)
    for ref, chosen in ((send_a_ref, jnp.where(even, shifted, final)), (send_b_ref, jnp.where(even, final, shifted))):
        tail = jnp.concatenate([chosen, fill], axis=0).astype(BF16)
        ref[REACH * COLS : REACH * COLS + 16, 0:COLS] = tail
        ref[REACH * COLS : REACH * COLS + 16, COLS : 2 * COLS] = tail


def band_kernel(taps_ref, start_ref, band_ref, basis_ref):
    taps = taps_ref[...]
    high = taps.astype(BF16)
    low = (taps - high.astype(F32)).astype(BF16)
    parts = jnp.concatenate([high, low], axis=0)
    tap = lax.broadcasted_iota(jnp.int32, (128, 128), 0)
    lane = lax.broadcasted_iota(jnp.int32, (128, 128), 1)
    column = ((lane >> 6) << 3) | (lane & 7)
    row_hit = ((lane >> 3) & 7) == ((tap >> 3) & 7)
    ahead = column - (tap & 7) - 1 - 4 * (tap >> 6)
    for j in range(4):
        select = jnp.where(row_hit & (ahead == j), 1.0, 0.0).astype(BF16)
        base = jnp.dot(parts, select, preferred_element_type=F32)
        for i in range(2):
            start = (4 * i + j) * 16
            rolled = (pltpu.roll(base, 8, 1) if i else base).astype(BF16)
            band_ref[start : start + 16, 0:128] = rolled[:16]
            band_ref[start : start + 16, 128:256] = rolled[16:]
    basis_ref[...] = jnp.dot(start_ref[...], frame_order(0), precision=HIGHEST, preferred_element_type=F32)


def frame_order(axis):
    frame = lax.broadcasted_iota(jnp.int32, (FRAMES, FRAMES), axis)
    lane = lax.broadcasted_iota(jnp.int32, (FRAMES, FRAMES), 1 - axis)
    return jnp.where(frame == 2 * (lane & (HALF - 1)) + (lane >> 7), 1.0, 0.0).astype(F32)


def halo_kernel(parity_ref, a_ref, b_ref, x_in_ref, rim_ref, x_ref, edge_a_ref, edge_b_ref):
    even = parity_ref[0] == 0
    got_a, got_b = a_ref[...], b_ref[...]
    final = lax.broadcasted_iota(jnp.int32, (COLS, HALF), 1) == HALF - 1
    sides = []
    for got in (jnp.where(even, got_b, got_a), jnp.where(even, got_a, got_b)):
        got = got.astype(F32)
        ends = got[REACH * COLS : REACH * COLS + 8, :COLS].T
        rows = []
        for i in range(REACH):
            tile = got[COLS * i : COLS * i + COLS]
            late = jnp.where(final, ends[:, i : i + 1], pltpu.roll(tile[:, :HALF], HALF - 1, 1))
            rows.append([tile[:, :HALF], tile[:, HALF:], late])
        sides.append(rows)
    above, below = sides
    for group in range(3):
        lanes = slice(HALF * group, HALF * group + HALF)
        x_ref[:, 0:16, lanes] = blocked(above[0][group], above[1][group])
        x_ref[:, 16:32, lanes] = blocked(above[2][group], rim_ref[0, :, lanes])
        x_ref[:, 80:96, lanes] = blocked(rim_ref[1, :, lanes], below[0][group])
        x_ref[:, 96:112, lanes] = blocked(below[1][group], below[2][group])
    x_ref[:, 32:80, :] = x_in_ref[:, 32:80, :]
    edge_a_ref[...] = x_ref[(BLOCKS - 1) * (1 - parity_ref[1])]
    edge_b_ref[...] = x_ref[(BLOCKS - 1) * parity_ref[1]]


def block_feats(band_ref, left, right):
    pooled = []
    for cell in range(2):
        windows = []
        for half in range(2):
            at = 16 * (2 * cell + half)
            windows.append(jnp.concatenate([left[at : at + 64], right[at : at + 64]], axis=0))
        window = jnp.concatenate(
            [windows[0][:, :FRAMES], windows[1][:, :FRAMES], windows[0][:, FRAMES:], windows[1][:, FRAMES:]], axis=1
        )
        window = jnp.concatenate([window, window], axis=0)
        resp = jnp.dot(band_ref[...], window, preferred_element_type=F32)
        total = [None, None]
        for half in range(2):
            starts = (FRAMES * half, FRAMES * half + HALF, 2 * FRAMES + HALF * half)
            for pixel in range(8):
                at = 16 * pixel
                real = [resp[at : at + 8, s : s + HALF] for s in starts]
                imag = [resp[at + 8 : at + 16, s : s + HALF] for s in starts]
                for g in range(2):
                    prod_real = real[g + 1] * real[g] + imag[g + 1] * imag[g]
                    prod_imag = imag[g + 1] * real[g] - real[g + 1] * imag[g]
                    motion = prod_imag * lax.rsqrt(prod_real * prod_real + prod_imag * prod_imag + 1.0)
                    total[g] = motion if total[g] is None else total[g] + motion
        pooled.append(jnp.concatenate(total, axis=1) * (1.0 / 16.0))
    return jnp.concatenate(pooled, axis=0)


def inner_kernel(band_ref, x_ref, feats_ref):
    def body(step, carry):
        for i in range(3):
            block = 3 * step + i
            feats_ref[block] = block_feats(band_ref, x_ref[block], x_ref[block + 1]).astype(BF16)
        return carry

    lax.fori_loop(0, (BLOCKS - 1) // 3, body, 0)


def edge_kernel(parity_ref, band_ref, x_ref, a_ref, b_ref, inner_ref, feats_ref, mine_ref, other_ref):
    even = parity_ref[1] == 0
    got_a = a_ref[...]
    got_b = b_ref[...]
    right = jnp.where(even, got_a, got_b)
    left = jnp.where(even, got_b, got_a)
    feats_left = block_feats(band_ref, left, x_ref[0])
    feats_right = block_feats(band_ref, x_ref[BLOCKS - 1], right)
    second = (lax.broadcasted_iota(jnp.int32, (16, FRAMES), 0) & 4) == 4
    feats_ref[0 : BLOCKS - 1] = inner_ref[0 : BLOCKS - 1]
    feats_ref[BLOCKS - 1] = jnp.where(second, feats_left, feats_right).astype(BF16)
    flat = feats_ref[...].reshape(16 * BLOCKS, FRAMES)
    gram = lax.dot_general(flat, flat, (((0,), (0,)), ((), ())), preferred_element_type=F32)
    top, cross, low = gram[:HALF, :HALF], gram[:HALF, HALF:], gram[HALF:, HALF:]
    i = lax.broadcasted_iota(jnp.int32, (HALF, HALF), 0)
    j = lax.broadcasted_iota(jnp.int32, (HALF, HALF), 1)
    folded = jnp.where(i <= j, top, low)
    diagonal = jnp.sum(jnp.where(i == j, low, 0.0), axis=0, keepdims=True)
    first = parity_ref[0] == 0
    spare = jnp.broadcast_to(diagonal, (8, HALF))
    mine_ref[0:HALF] = jnp.where(first, cross, folded)
    mine_ref[HALF : HALF + 8] = spare
    other_ref[0:HALF] = jnp.where(first, folded, cross)
    other_ref[HALF : HALF + 8] = spare


def inverse_factor(inner):
    count = MODES // 8
    shape = (8, 2 * MODES)
    i = lax.broadcasted_iota(jnp.int32, (MODES, MODES), 0)
    j = lax.broadcasted_iota(jnp.int32, (MODES, MODES), 1)
    work = jnp.concatenate([jnp.where(i == j, 1.0, 0.0), inner], axis=1)
    work = [work[8 * v : 8 * v + 8] for v in range(count)]
    sub = lax.broadcasted_iota(jnp.int32, shape, 0)
    done = []
    for b in range(count):
        lane = MODES + 8 * b
        cols = [[jnp.broadcast_to(work[v][:, lane + m : lane + m + 1], shape) for v in range(b, count)] for m in range(8)]
        scale = jnp.zeros(shape, F32)
        for m in range(8):
            lead = cols[m][0]
            pivot = jnp.broadcast_to(lead[m : m + 1], shape)
            inverse = 1.0 / pivot
            scale = jnp.where(sub == m, lax.rsqrt(pivot), scale)
            row = jnp.broadcast_to(work[b][m : m + 1], shape) * inverse
            for q in range(m + 1, 8):
                times = jnp.broadcast_to(lead[q : q + 1], shape) * inverse
                cols[q] = [c - d * times for c, d in zip(cols[q], cols[m])]
            work[b] = work[b] - jnp.where(sub > m, lead, 0.0) * row
            for v in range(b + 1, count):
                work[v] = work[v] - cols[m][v - b] * row
        done.append(work[b] * scale)
    return jnp.concatenate(done, axis=0)[:, :MODES]


def basis_kernel(scale, parity_ref, mine_ref, other_ref, start_ref, feats_ref, basis_ref, modes_ref, rows_ref, out_ref):
    first = parity_ref[0] == 0
    mine, other = mine_ref[...], other_ref[...]
    cross = jnp.where(first, mine, other)[:HALF]
    second = jnp.where(first, other, mine)
    folded = second[:HALF]
    i = lax.broadcasted_iota(jnp.int32, (HALF, HALF), 0)
    j = lax.broadcasted_iota(jnp.int32, (HALF, HALF), 1)
    flipped = folded.T
    top = jnp.where(i <= j, folded, flipped)
    low = jnp.where(i > j, folded, jnp.where(i < j, flipped, second[HALF : HALF + 1]))
    gram = jnp.concatenate(
        [jnp.concatenate([top, cross], axis=1), jnp.concatenate([cross.T, low], axis=1)], axis=0
    )
    gram = gram * scale
    basis = start_ref[...]
    for sweep in range(SWEEPS):
        stacked = jnp.dot(basis, gram, precision=HIGHEST, preferred_element_type=F32)
        inner = lax.dot_general(
            stacked, stacked, (((1,), (1,)), ((), ())), precision=HIGHEST, preferred_element_type=F32
        )
        basis = jnp.dot(inverse_factor(inner), stacked, precision=HIGHEST, preferred_element_type=F32)
    basis_ref[...] = jnp.dot(basis, frame_order(1), precision=HIGHEST, preferred_element_type=F32)
    twice = jnp.concatenate([basis, basis], axis=0)
    flat = feats_ref[...].reshape(16 * BLOCKS, FRAMES)
    rows_ref[...] = lax.dot_general(
        flat, twice.astype(BF16), (((1,), (1,)), ((), ())), preferred_element_type=F32
    )
    left = lax.broadcasted_iota(jnp.int32, (BLOCKS, 2 * MODES), 1) < MODES
    for row in range(2):
        for half in range(2):
            for cell in range(2):
                at = 8 * row + 4 * cell + 2 * half
                field = jnp.where(
                    left, rows_ref[pl.ds(at, BLOCKS, stride=16), :], rows_ref[pl.ds(at + 1, BLOCKS, stride=16), :]
                )
                if cell:
                    field = pltpu.roll(field, 1, 0)
                out_ref[pl.ds(64 * row + 32 * half + 1 - cell, BLOCKS, stride=2), :] = field
            modes_ref[row, :, 128 * half : 128 * half + 128] = out_ref[64 * row + 32 * half : 64 * row + 32 * half + 32]


def call(kernel, outs, n_smem, n_in, scratch=(), aliases={}):
    return pl.pallas_call(
        kernel,
        out_shape=[jax.ShapeDtypeStruct(shape, dtype) for shape, dtype in outs],
        in_specs=[SMEM] * n_smem + [VMEM] * (n_in - n_smem),
        out_specs=[VMEM] * len(outs),
        scratch_shapes=list(scratch),
        input_output_aliases=aliases,
        compiler_params=PARAMS,
    )


def pairs(size, start):
    swaps = []
    for i in range(start, size - 1, 2):
        swaps += [(i, i + 1), (i + 1, i)]
    return swaps


def on_device(video, filters, start_basis):
    size_row, size_col = lax.axis_size("row"), lax.axis_size("col")
    parity = jnp.stack([lax.axis_index("row") & 1, lax.axis_index("col") & 1]).astype(jnp.int32)

    rows = pltpu.VMEM(((FRAMES + 1) * ROWS, COLS), F32)
    send = ((REACH * COLS + 16, FRAMES), BF16)
    tile = ((BLOCKS, 112, 3 * HALF), BF16)
    rim = ((2, COLS, 3 * HALF), F32)
    send_a, send_b, x, rim = call(own_kernel, [send, send, tile, rim], 1, 2, [rows])(parity, video)
    got_a = lax.ppermute(send_a, "row", pairs(size_row, 0))
    got_b = lax.ppermute(send_b, "row", pairs(size_row, 1))

    taps = jnp.pad(filters, ((0, 0), (0, 0), (0, 1), (0, 1))).reshape(ORIENT, 2, 64)
    taps = jnp.transpose(taps, (1, 0, 2))[:, None, :, None, :] * jnp.eye(2, dtype=F32)[None, :, None, :, None]
    band, start = call(band_kernel, [((128, 256), BF16), ((MODES, FRAMES), F32)], 0, 2)(
        taps.reshape(16, 128), start_basis.T
    )
    edge = ((112, 3 * HALF), BF16)
    x, edge_a, edge_b = call(halo_kernel, [tile, edge, edge], 1, 5)(parity, got_a, got_b, x, rim)
    got_a = lax.ppermute(edge_a, "col", pairs(size_col, 0))
    got_b = lax.ppermute(edge_b, "col", pairs(size_col, 1))
    feats_shape = ((BLOCKS, 16, FRAMES), BF16)
    (inner,) = call(inner_kernel, [feats_shape], 0, 2)(band, x)
    part = ((HALF + 8, HALF), F32)
    feats, mine, other = call(edge_kernel, [feats_shape, part, part], 1, 6)(parity, band, x, got_a, got_b, inner)

    mine = mine + lax.ppermute(other, "row", pairs(size_row, 0))
    for axis, size, step in (("row", size_row, 2), ("col", size_col, 1)):
        while step < size:
            mine = mine + lax.ppermute(mine, axis, [(i, i ^ step) for i in range(size)])
            step *= 2
    other = lax.ppermute(mine, "row", pairs(size_row, 0))

    features = ORIENT * (size_row * ROWS // 4) * (size_col * COLS // 4)
    kernel = functools.partial(basis_kernel, 1.0 / features)
    basis, modes = call(
        kernel,
        [((MODES, FRAMES), F32), ((ROWS // 4, COLS // 4, ORIENT * MODES), F32)],
        1,
        5,
        [pltpu.VMEM((FRAMES, 2 * MODES), F32), pltpu.VMEM((128, 128), F32)],
    )(parity, mine, other, start, feats)
    return basis.T, modes


def solution(mesh):
    return jax.shard_map(
        on_device,
        mesh=mesh,
        in_specs=(P("grp", "row", "col"), P(), P()),
        out_specs=(P("grp", None), P(("grp", "row"), "col", None)),
        check_vma=False,
    )
```

```python
import functools

import jax
import jax.numpy as jnp
from jax import lax
from jax.experimental import pallas as pl
from jax.experimental.pallas import tpu as pltpu
from jax.sharding import PartitionSpec as P

FRAMES = 256
HALF = FRAMES // 2
MODES = 64
ORIENT = 4
TAPS = 7
REACH = 3
SWEEPS = 2
ROWS = 8
COLS = 128
BLOCKS = 16
F32 = jnp.float32
BF16 = jnp.bfloat16
HIGHEST = lax.Precision.HIGHEST
PARAMS = pltpu.CompilerParams(vmem_limit_bytes=24 * 1024 * 1024)
VMEM = pl.BlockSpec(memory_space=pltpu.VMEM)


def turned(rows_ref, row, group):
    return rows_ref[pl.ds(group * ROWS + row, HALF, stride=2 * ROWS), :].T


def blocked(upper, lower):
    both = [part.reshape(BLOCKS, 8, HALF) for part in (upper, lower)]
    return jnp.concatenate(both, axis=1).astype(BF16)


def is_even(axis):
    return (lax.axis_index(axis) & 1) == 0


def own_kernel(video_ref, side_a_ref, side_b_ref, send_a_ref, send_b_ref, x_ref, rim_ref, rows_ref):
    even_row, even_col = is_even("row"), is_even("col")
    rows_ref[...] = video_ref[...].astype(F32).reshape(rows_ref.shape)
    for group in range(3):
        lanes = slice(HALF * group, HALF * group + HALF)
        tiles = [turned(rows_ref, row, group) for row in range(ROWS)]
        for pair in range(ROWS // 2):
            both = tiles[2 * pair : 2 * pair + 2]
            left = jnp.concatenate([tile[:8] for tile in both], axis=0)
            right = jnp.concatenate([tile[COLS - 8 :] for tile in both], axis=0)
            at = slice(16 * pair, 16 * pair + 16)
            side_a_ref[at, lanes] = jnp.where(even_col, right, left).astype(BF16)
            side_b_ref[at, lanes] = jnp.where(even_col, left, right).astype(BF16)
        if group < 2:
            for i in range(REACH):
                first, last = tiles[i], tiles[ROWS - REACH + i]
                at = slice(COLS * i, COLS * i + COLS)
                send_a_ref[at, lanes] = jnp.where(even_row, last, first).astype(BF16)
                send_b_ref[at, lanes] = jnp.where(even_row, first, last).astype(BF16)
        for pair in range(3):
            x_ref[:, 32 + 16 * pair : 48 + 16 * pair, lanes] = blocked(tiles[2 * pair + 1], tiles[2 * pair + 2])
        rim_ref[0, :, lanes] = tiles[0]
        rim_ref[1, :, lanes] = tiles[ROWS - 1]
    final = rows_ref[FRAMES * ROWS : FRAMES * ROWS + ROWS, :]
    shifted = pltpu.roll(final, REACH, 0)
    fill = jnp.zeros((8, COLS), F32)
    first, last = (jnp.concatenate([part, fill], axis=0).astype(BF16) for part in (final, shifted))
    for ref, chosen in ((send_a_ref, jnp.where(even_row, last, first)), (send_b_ref, jnp.where(even_row, first, last))):
        ref[REACH * COLS : REACH * COLS + 16, 0:COLS] = chosen
        ref[REACH * COLS : REACH * COLS + 16, COLS : 2 * COLS] = chosen


def corner_kernel(a_ref, b_ref, band_ref, send_a_ref, send_b_ref):
    even_row, even_col = is_even("row"), is_even("col")
    got_a, got_b = a_ref[...], b_ref[...]
    for side, got in enumerate((jnp.where(even_col, got_b, got_a), jnp.where(even_col, got_a, got_b))):
        got = got.astype(F32)
        first, last = got[: 8 * REACH], got[8 * (ROWS - REACH) :]
        send_a_ref[side] = jnp.where(even_row, last, first)
        send_b_ref[side] = jnp.where(even_row, first, last)


def band_kernel(taps_ref, start_ref, band_ref, basis_ref):
    taps = taps_ref[...]
    high = taps.astype(BF16)
    low = (taps - high.astype(F32)).astype(BF16)
    parts = jnp.concatenate([high, low], axis=0)
    tap = lax.broadcasted_iota(jnp.int32, (128, 128), 0)
    lane = lax.broadcasted_iota(jnp.int32, (128, 128), 1)
    column = ((lane >> 6) << 3) | (lane & 7)
    row_hit = ((lane >> 3) & 7) == ((tap >> 3) & 7)
    ahead = column - (tap & 7) - 1 - 4 * (tap >> 6)
    for j in range(4):
        select = jnp.where(row_hit & (ahead == j), 1.0, 0.0).astype(BF16)
        base = jnp.dot(parts, select, preferred_element_type=F32)
        for i in range(2):
            start = (4 * i + j) * 16
            rolled = (pltpu.roll(base, 8, 1) if i else base).astype(BF16)
            band_ref[start : start + 16, 0:128] = rolled[:16]
            band_ref[start : start + 16, 128:256] = rolled[16:]
    basis_ref[...] = jnp.dot(start_ref[...], frame_order(0), precision=HIGHEST, preferred_element_type=F32)


def frame_order(axis):
    frame = lax.broadcasted_iota(jnp.int32, (FRAMES, FRAMES), axis)
    lane = lax.broadcasted_iota(jnp.int32, (FRAMES, FRAMES), 1 - axis)
    return jnp.where(frame == 2 * (lane & (HALF - 1)) + (lane >> 7), 1.0, 0.0).astype(F32)


def halo_kernel(a_ref, b_ref, x_in_ref, rim_ref, x_ref):
    even = is_even("row")
    got_a, got_b = a_ref[...], b_ref[...]
    final = lax.broadcasted_iota(jnp.int32, (COLS, HALF), 1) == HALF - 1
    sides = []
    for got in (jnp.where(even, got_b, got_a), jnp.where(even, got_a, got_b)):
        got = got.astype(F32)
        ends = got[REACH * COLS : REACH * COLS + 8, :COLS].T
        rows = []
        for i in range(REACH):
            tile = got[COLS * i : COLS * i + COLS]
            late = jnp.where(final, ends[:, i : i + 1], pltpu.roll(tile[:, :HALF], HALF - 1, 1))
            rows.append([tile[:, :HALF], tile[:, HALF:], late])
        sides.append(rows)
    above, below = sides
    for group in range(3):
        lanes = slice(HALF * group, HALF * group + HALF)
        x_ref[:, 0:16, lanes] = blocked(above[0][group], above[1][group])
        x_ref[:, 16:32, lanes] = blocked(above[2][group], rim_ref[0, :, lanes])
        x_ref[:, 80:96, lanes] = blocked(rim_ref[1, :, lanes], below[0][group])
        x_ref[:, 96:112, lanes] = blocked(below[1][group], below[2][group])
    x_ref[:, 32:80, :] = x_in_ref[:, 32:80, :]


def block_feats(band_ref, left, right):
    pooled = []
    for cell in range(2):
        windows = []
        for half in range(2):
            at = 16 * (2 * cell + half)
            windows.append(jnp.concatenate([left[at : at + 64], right[at : at + 64]], axis=0))
        window = jnp.concatenate(
            [windows[0][:, :FRAMES], windows[1][:, :FRAMES], windows[0][:, FRAMES:], windows[1][:, FRAMES:]], axis=1
        )
        window = jnp.concatenate([window, window], axis=0)
        resp = jnp.dot(band_ref[...], window, preferred_element_type=F32)
        total = [None, None]
        for half in range(2):
            starts = (FRAMES * half, FRAMES * half + HALF, 2 * FRAMES + HALF * half)
            for pixel in range(8):
                at = 16 * pixel
                real = [resp[at : at + 8, s : s + HALF] for s in starts]
                imag = [resp[at + 8 : at + 16, s : s + HALF] for s in starts]
                for g in range(2):
                    prod_real = real[g + 1] * real[g] + imag[g + 1] * imag[g]
                    prod_imag = imag[g + 1] * real[g] - real[g + 1] * imag[g]
                    motion = prod_imag * lax.rsqrt(prod_real * prod_real + prod_imag * prod_imag + 1.0)
                    total[g] = motion if total[g] is None else total[g] + motion
        pooled.append(jnp.concatenate(total, axis=1) * (1.0 / 16.0))
    return jnp.concatenate(pooled, axis=0)


def inner_kernel(band_ref, x_ref, feats_ref):
    def body(step, carry):
        for i in range(3):
            block = 3 * step + i
            feats_ref[block] = block_feats(band_ref, x_ref[block], x_ref[block + 1]).astype(BF16)
        return carry

    lax.fori_loop(0, (BLOCKS - 1) // 3, body, 0)


def edge_kernel(band_ref, x_ref, side_a_ref, side_b_ref, a_ref, b_ref, inner_ref, feats_ref, mine_ref, other_ref):
    even_row, even_col = is_even("row"), is_even("col")
    side_a, side_b = side_a_ref[...], side_b_ref[...]
    blocks = []
    for side, got in enumerate((jnp.where(even_col, side_b, side_a), jnp.where(even_col, side_a, side_b))):
        got_a, got_b = a_ref[side], b_ref[side]
        above = jnp.where(even_row, got_b, got_a)
        below = jnp.where(even_row, got_a, got_b)
        blocks.append(jnp.concatenate([above, got.astype(F32), below], axis=0).astype(BF16))
    left, right = blocks
    feats_left = block_feats(band_ref, left, x_ref[0])
    feats_right = block_feats(band_ref, x_ref[BLOCKS - 1], right)
    second = (lax.broadcasted_iota(jnp.int32, (16, FRAMES), 0) & 4) == 4
    feats_ref[0 : BLOCKS - 1] = inner_ref[0 : BLOCKS - 1]
    feats_ref[BLOCKS - 1] = jnp.where(second, feats_left, feats_right).astype(BF16)
    flat = feats_ref[...].reshape(16 * BLOCKS, FRAMES)
    gram = lax.dot_general(flat, flat, (((0,), (0,)), ((), ())), preferred_element_type=F32)
    top, cross, low = gram[:HALF, :HALF], gram[:HALF, HALF:], gram[HALF:, HALF:]
    i = lax.broadcasted_iota(jnp.int32, (HALF, HALF), 0)
    j = lax.broadcasted_iota(jnp.int32, (HALF, HALF), 1)
    folded = jnp.where(i <= j, top, low)
    diagonal = jnp.sum(jnp.where(i == j, low, 0.0), axis=0, keepdims=True)
    first = is_even("row")
    spare = jnp.broadcast_to(diagonal, (8, HALF))
    mine_ref[0:HALF] = jnp.where(first, cross, folded)
    mine_ref[HALF : HALF + 8] = spare
    other_ref[0:HALF] = jnp.where(first, folded, cross)
    other_ref[HALF : HALF + 8] = spare


def inverse_factor(inner):
    count = MODES // 8
    shape = (8, 2 * MODES)
    i = lax.broadcasted_iota(jnp.int32, (MODES, MODES), 0)
    j = lax.broadcasted_iota(jnp.int32, (MODES, MODES), 1)
    work = jnp.concatenate([jnp.where(i == j, 1.0, 0.0), inner], axis=1)
    work = [work[8 * v : 8 * v + 8] for v in range(count)]
    sub = lax.broadcasted_iota(jnp.int32, shape, 0)
    done = []
    for b in range(count):
        lane = MODES + 8 * b
        cols = [[jnp.broadcast_to(work[v][:, lane + m : lane + m + 1], shape) for v in range(b, count)] for m in range(8)]
        scale = jnp.zeros(shape, F32)
        for m in range(8):
            lead = cols[m][0]
            pivot = jnp.broadcast_to(lead[m : m + 1], shape)
            inverse = 1.0 / pivot
            scale = jnp.where(sub == m, lax.rsqrt(pivot), scale)
            row = jnp.broadcast_to(work[b][m : m + 1], shape) * inverse
            for q in range(m + 1, 8):
                times = jnp.broadcast_to(lead[q : q + 1], shape) * inverse
                cols[q] = [c - d * times for c, d in zip(cols[q], cols[m])]
            work[b] = work[b] - jnp.where(sub > m, lead, 0.0) * row
            for v in range(b + 1, count):
                work[v] = work[v] - cols[m][v - b] * row
        done.append(work[b] * scale)
    return jnp.concatenate(done, axis=0)[:, :MODES]


def basis_kernel(scale, mine_ref, other_ref, start_ref, feats_ref, basis_ref, modes_ref, rows_ref, out_ref):
    first = is_even("row")
    mine, other = mine_ref[...], other_ref[...]
    cross = jnp.where(first, mine, other)[:HALF]
    second = jnp.where(first, other, mine)
    folded = second[:HALF]
    i = lax.broadcasted_iota(jnp.int32, (HALF, HALF), 0)
    j = lax.broadcasted_iota(jnp.int32, (HALF, HALF), 1)
    flipped = folded.T
    top = jnp.where(i <= j, folded, flipped)
    low = jnp.where(i > j, folded, jnp.where(i < j, flipped, second[HALF : HALF + 1]))
    gram = jnp.concatenate(
        [jnp.concatenate([top, cross], axis=1), jnp.concatenate([cross.T, low], axis=1)], axis=0
    )
    gram = gram * scale
    basis = start_ref[...]
    for sweep in range(SWEEPS):
        stacked = jnp.dot(basis, gram, precision=HIGHEST, preferred_element_type=F32)
        inner = lax.dot_general(
            stacked, stacked, (((1,), (1,)), ((), ())), precision=HIGHEST, preferred_element_type=F32
        )
        basis = jnp.dot(inverse_factor(inner), stacked, precision=HIGHEST, preferred_element_type=F32)
    basis_ref[...] = jnp.dot(basis, frame_order(1), precision=HIGHEST, preferred_element_type=F32)
    twice = jnp.concatenate([basis, basis], axis=0)
    flat = feats_ref[...].reshape(16 * BLOCKS, FRAMES)
    rows_ref[...] = lax.dot_general(
        flat, twice.astype(BF16), (((1,), (1,)), ((), ())), preferred_element_type=F32
    )
    left = lax.broadcasted_iota(jnp.int32, (BLOCKS, 2 * MODES), 1) < MODES
    for row in range(2):
        for half in range(2):
            for cell in range(2):
                at = 8 * row + 4 * cell + 2 * half
                field = jnp.where(
                    left, rows_ref[pl.ds(at, BLOCKS, stride=16), :], rows_ref[pl.ds(at + 1, BLOCKS, stride=16), :]
                )
                if cell:
                    field = pltpu.roll(field, 1, 0)
                out_ref[pl.ds(64 * row + 32 * half + 1 - cell, BLOCKS, stride=2), :] = field
            modes_ref[row, :, 128 * half : 128 * half + 128] = out_ref[64 * row + 32 * half : 64 * row + 32 * half + 32]


def call(kernel, outs, n_in, scratch=()):
    return pl.pallas_call(
        kernel,
        out_shape=[jax.ShapeDtypeStruct(shape, dtype) for shape, dtype in outs],
        in_specs=[VMEM] * n_in,
        out_specs=[VMEM] * len(outs),
        scratch_shapes=list(scratch),
        compiler_params=PARAMS,
    )


def pairs(size, start):
    swaps = []
    for i in range(start, size - 1, 2):
        swaps += [(i, i + 1), (i + 1, i)]
    return swaps


def swap(axis, a, b):
    size = lax.axis_size(axis)
    return lax.ppermute(a, axis, pairs(size, 0)), lax.ppermute(b, axis, pairs(size, 1))


def on_device(video, filters, start_basis):
    size_row, size_col = lax.axis_size("row"), lax.axis_size("col")
    swap_row, swap_col = (functools.partial(swap, axis) for axis in ("row", "col"))

    side = ((8 * ROWS, 3 * HALF), BF16)
    send = ((REACH * COLS + 16, FRAMES), BF16)
    tile = ((BLOCKS, 112, 3 * HALF), BF16)
    rim = ((2, COLS, 3 * HALF), F32)
    rows = pltpu.VMEM(((FRAMES + 1) * ROWS, COLS), F32)
    side_a, side_b, send_a, send_b, x, rim = call(own_kernel, [side, side, send, send, tile, rim], 1, [rows])(video)
    side_a, side_b = swap_col(side_a, side_b)
    got_a, got_b = swap_row(send_a, send_b)

    taps = jnp.pad(filters, ((0, 0), (0, 0), (0, 1), (0, 1))).reshape(ORIENT, 2, 64)
    taps = jnp.transpose(taps, (1, 0, 2))[:, None, :, None, :] * jnp.eye(2, dtype=F32)[None, :, None, :, None]
    band, start = call(band_kernel, [((128, 256), BF16), ((MODES, FRAMES), F32)], 2)(
        taps.reshape(16, 128), start_basis.T
    )
    corner = ((2, 8 * REACH, 3 * HALF), F32)
    corner_a, corner_b = swap_row(*call(corner_kernel, [corner, corner], 3)(side_a, side_b, band))
    (x,) = call(halo_kernel, [tile], 4)(got_a, got_b, x, rim)
    feats_shape = ((BLOCKS, 16, FRAMES), BF16)
    (inner,) = call(inner_kernel, [feats_shape], 2)(band, x)
    part = ((HALF + 8, HALF), F32)
    feats, mine, other = call(edge_kernel, [feats_shape, part, part], 7)(
        band, x, side_a, side_b, corner_a, corner_b, inner
    )

    mine = mine + lax.ppermute(other, "row", pairs(size_row, 0))
    for axis, size, step in (("row", size_row, 2), ("col", size_col, 1)):
        while step < size:
            mine = mine + lax.ppermute(mine, axis, [(i, i ^ step) for i in range(size)])
            step *= 2
    other = lax.ppermute(mine, "row", pairs(size_row, 0))

    features = ORIENT * (size_row * ROWS // 4) * (size_col * COLS // 4)
    kernel = functools.partial(basis_kernel, 1.0 / features)
    basis, modes = call(
        kernel,
        [((MODES, FRAMES), F32), ((ROWS // 4, COLS // 4, ORIENT * MODES), F32)],
        4,
        [pltpu.VMEM((FRAMES, 2 * MODES), F32), pltpu.VMEM((128, 128), F32)],
    )(mine, other, start, feats)
    return basis.T, modes


def solution(mesh):
    return jax.shard_map(
        on_device,
        mesh=mesh,
        in_specs=(P("grp", "row", "col"), P(), P()),
        out_specs=(P("grp", None), P(("grp", "row"), "col", None)),
        check_vma=False,
    )
```

```python
import functools

import jax
import jax.numpy as jnp
from jax import lax
from jax.experimental import pallas as pl
from jax.experimental.pallas import tpu as pltpu
from jax.sharding import PartitionSpec as P

FRAMES = 256
HALF = FRAMES // 2
MODES = 64
ORIENT = 4
TAPS = 7
REACH = 3
SWEEPS = 2
ROWS = 8
COLS = 128
SUMMED = HALF + 8
BLOCKS = 16
F32 = jnp.float32
BF16 = jnp.bfloat16
HIGHEST = lax.Precision.HIGHEST
PARAMS = pltpu.CompilerParams(vmem_limit_bytes=24 * 1024 * 1024)
VMEM = pl.BlockSpec(memory_space=pltpu.VMEM)


def turned(rows_ref, row, group):
    return rows_ref[pl.ds(group * ROWS + row, HALF, stride=2 * ROWS), :].T


def blocked(upper, lower):
    both = [part.reshape(BLOCKS, 8, HALF) for part in (upper, lower)]
    return jnp.concatenate(both, axis=1).astype(BF16)


def is_even(axis):
    return (lax.axis_index(axis) & 1) == 0


def own_kernel(video_ref, send_a_ref, send_b_ref, x_ref, rim_ref, rows_ref):
    even = is_even("row")
    rows_ref[...] = video_ref[...].astype(F32).reshape(rows_ref.shape)
    fill = jnp.zeros((8, COLS), F32)
    for group in range(3):
        lanes = slice(HALF * group, HALF * group + HALF)
        tiles = [turned(rows_ref, row, group) for row in range(ROWS)]
        if group < 2:
            for i in range(REACH):
                first, last = tiles[i], tiles[ROWS - REACH + i]
                at = slice(COLS * i, COLS * i + COLS)
                send_a_ref[at, lanes] = jnp.where(even, last, first).astype(BF16)
                send_b_ref[at, lanes] = jnp.where(even, first, last).astype(BF16)
        for pair in range(3):
            x_ref[:, 32 + 16 * pair : 48 + 16 * pair, lanes] = blocked(tiles[2 * pair + 1], tiles[2 * pair + 2])
        rim_ref[0, :, lanes] = tiles[0]
        rim_ref[1, :, lanes] = tiles[ROWS - 1]
    final = rows_ref[FRAMES * ROWS : FRAMES * ROWS + ROWS, :]
    shifted = pltpu.roll(final, REACH, 0)
    first, last = (jnp.concatenate([part, fill], axis=0).astype(BF16) for part in (final, shifted))
    for ref, chosen in ((send_a_ref, jnp.where(even, last, first)), (send_b_ref, jnp.where(even, first, last))):
        ref[REACH * COLS : REACH * COLS + 16, 0:COLS] = chosen
        ref[REACH * COLS : REACH * COLS + 16, COLS : 2 * COLS] = chosen


def band_kernel(filters_ref, band_ref, taps_ref):
    taps_ref[...] = jnp.zeros((16, 128), F32)
    for orient in range(ORIENT):
        for part in range(2):
            for i in range(TAPS):
                line = filters_ref[orient, i, part : part + 1, :]
                for cell in range(2):
                    row, lane = 8 * part + 4 * cell + orient, 64 * cell + 8 * i
                    taps_ref[row : row + 1, lane : lane + TAPS] = line
    taps = taps_ref[...]
    high = taps.astype(BF16)
    low = (taps - high.astype(F32)).astype(BF16)
    parts = jnp.concatenate([high, low], axis=0)
    tap = lax.broadcasted_iota(jnp.int32, (128, 128), 0)
    lane = lax.broadcasted_iota(jnp.int32, (128, 128), 1)
    column = ((lane >> 6) << 3) | (lane & 7)
    row_hit = ((lane >> 3) & 7) == ((tap >> 3) & 7)
    ahead = column - (tap & 7) - 1 - 4 * (tap >> 6)
    for j in range(4):
        select = jnp.where(row_hit & (ahead == j), 1.0, 0.0).astype(BF16)
        base = jnp.dot(parts, select, preferred_element_type=F32)
        for i in range(2):
            start = (4 * i + j) * 16
            rolled = (pltpu.roll(base, 8, 1) if i else base).astype(BF16)
            band_ref[start : start + 16, 0:128] = rolled[:16]
            band_ref[start : start + 16, 128:256] = rolled[16:]


def start_kernel(start_ref, basis_ref):
    basis_ref[...] = jnp.dot(start_ref[...], frame_order(0), precision=HIGHEST, preferred_element_type=F32)


def frame_order(axis):
    frame = lax.broadcasted_iota(jnp.int32, (FRAMES, FRAMES), axis)
    lane = lax.broadcasted_iota(jnp.int32, (FRAMES, FRAMES), 1 - axis)
    return jnp.where(frame == 2 * (lane & (HALF - 1)) + (lane >> 7), 1.0, 0.0).astype(F32)


def halo_kernel(a_ref, b_ref, x_in_ref, rim_ref, band_ref, x_ref, side_ref):
    even = is_even("row")
    got_a, got_b = a_ref[...], b_ref[...]
    final = lax.broadcasted_iota(jnp.int32, (COLS, HALF), 1) == HALF - 1
    sides = []
    for got in (jnp.where(even, got_b, got_a), jnp.where(even, got_a, got_b)):
        got = got.astype(F32)
        ends = got[REACH * COLS : REACH * COLS + 8, :COLS].T
        rows = []
        for i in range(REACH):
            tile = got[COLS * i : COLS * i + COLS]
            late = jnp.where(final, ends[:, i : i + 1], pltpu.roll(tile[:, :HALF], HALF - 1, 1))
            rows.append([tile[:, :HALF], tile[:, HALF:], late])
        sides.append(rows)
    above, below = sides
    for group in range(3):
        lanes = slice(HALF * group, HALF * group + HALF)
        x_ref[:, 0:16, lanes] = blocked(above[0][group], above[1][group])
        x_ref[:, 16:32, lanes] = blocked(above[2][group], rim_ref[0, :, lanes])
        x_ref[:, 80:96, lanes] = blocked(rim_ref[1, :, lanes], below[0][group])
        x_ref[:, 96:112, lanes] = blocked(below[1][group], below[2][group])
    x_ref[:, 32:80, :] = x_in_ref[:, 32:80, :]
    side_ref[...] = x_ref[0]


def block_feats(band_ref, left, right):
    pooled = []
    for cell in range(2):
        windows = []
        for half in range(2):
            at = 16 * (2 * cell + half)
            windows.append(jnp.concatenate([left[at : at + 64], right[at : at + 64]], axis=0))
        window = jnp.concatenate(
            [windows[0][:, :FRAMES], windows[1][:, :FRAMES], windows[0][:, FRAMES:], windows[1][:, FRAMES:]], axis=1
        )
        window = jnp.concatenate([window, window], axis=0)
        resp = jnp.dot(band_ref[...], window, preferred_element_type=F32)
        total = [None, None]
        for half in range(2):
            starts = (FRAMES * half, FRAMES * half + HALF, 2 * FRAMES + HALF * half)
            for pixel in range(8):
                at = 16 * pixel
                real = [resp[at : at + 8, s : s + HALF] for s in starts]
                imag = [resp[at + 8 : at + 16, s : s + HALF] for s in starts]
                for g in range(2):
                    prod_real = real[g + 1] * real[g] + imag[g + 1] * imag[g]
                    prod_imag = imag[g + 1] * real[g] - real[g + 1] * imag[g]
                    motion = prod_imag * lax.rsqrt(prod_real * prod_real + prod_imag * prod_imag + 1.0)
                    total[g] = motion if total[g] is None else total[g] + motion
        pooled.append(jnp.concatenate(total, axis=1) * (1.0 / 16.0))
    return jnp.concatenate(pooled, axis=0)


def second_cells():
    return (lax.broadcasted_iota(jnp.int32, (16, FRAMES), 0) & 4) == 4


def inner_kernel(band_ref, x_ref, feats_ref, start_ref):
    def body(step, carry):
        for i in range(3):
            block = 3 * step + i
            feats_ref[block] = block_feats(band_ref, x_ref[block], x_ref[block + 1]).astype(BF16)
        return carry

    lax.fori_loop(0, (BLOCKS - 1) // 3, body, 0)
    start = block_feats(band_ref, jnp.zeros((112, 3 * HALF), BF16), x_ref[0])
    begins = lax.axis_index("col") == 0
    start_ref[...] = jnp.where(second_cells() & begins, start, 0.0).astype(BF16)


def edge_kernel(band_ref, x_ref, side_ref, inner_ref, start_ref, feats_ref, mine_ref, other_ref):
    edge = block_feats(band_ref, x_ref[BLOCKS - 1], side_ref[...])
    ends = lax.axis_index("col") == lax.axis_size("col") - 1
    feats_ref[0 : BLOCKS - 1] = inner_ref[0 : BLOCKS - 1]
    edge = jnp.where(second_cells() & ends, 0.0, edge).astype(BF16)
    feats_ref[BLOCKS - 1] = edge
    edge = edge.astype(F32)
    flat = jnp.concatenate([feats_ref[...].reshape(16 * BLOCKS, FRAMES), start_ref[...]], axis=0)
    gram = lax.dot_general(flat, flat, (((0,), (0,)), ((), ())), preferred_element_type=F32)
    top, cross, low = gram[:HALF, :HALF], gram[:HALF, HALF:], gram[HALF:, HALF:]
    i = lax.broadcasted_iota(jnp.int32, (HALF, HALF), 0)
    j = lax.broadcasted_iota(jnp.int32, (HALF, HALF), 1)
    folded = jnp.where(i <= j, top, low)
    diagonal = jnp.sum(jnp.where(i == j, low, 0.0), axis=0, keepdims=True)
    first = is_even("row")
    spare = jnp.broadcast_to(diagonal, (8, HALF))
    mine_ref[0:HALF] = jnp.where(first, cross, folded)
    mine_ref[HALF:SUMMED] = spare
    passed = jnp.where(second_cells()[:8], edge[:8], pltpu.roll(edge[8:], 4, 0))
    mine_ref[SUMMED : SUMMED + 8] = passed[:, :HALF]
    mine_ref[SUMMED + 8 : SUMMED + 16] = passed[:, HALF:]
    other_ref[0:HALF] = jnp.where(first, folded, cross)
    other_ref[HALF:SUMMED] = spare
    other_ref[SUMMED : SUMMED + 16] = jnp.zeros((16, HALF), F32)


def inverse_factor(inner):
    count = MODES // 8
    shape = (8, 2 * MODES)
    i = lax.broadcasted_iota(jnp.int32, (MODES, MODES), 0)
    j = lax.broadcasted_iota(jnp.int32, (MODES, MODES), 1)
    work = jnp.concatenate([jnp.where(i == j, 1.0, 0.0), inner], axis=1)
    work = [work[8 * v : 8 * v + 8] for v in range(count)]
    sub = lax.broadcasted_iota(jnp.int32, shape, 0)
    done = []
    for b in range(count):
        lane = MODES + 8 * b
        cols = [[jnp.broadcast_to(work[v][:, lane + m : lane + m + 1], shape) for v in range(b, count)] for m in range(8)]
        scale = jnp.zeros(shape, F32)
        for m in range(8):
            lead = cols[m][0]
            pivot = jnp.broadcast_to(lead[m : m + 1], shape)
            inverse = 1.0 / pivot
            scale = jnp.where(sub == m, lax.rsqrt(pivot), scale)
            row = jnp.broadcast_to(work[b][m : m + 1], shape) * inverse
            for q in range(m + 1, 8):
                times = jnp.broadcast_to(lead[q : q + 1], shape) * inverse
                cols[q] = [c - d * times for c, d in zip(cols[q], cols[m])]
            work[b] = work[b] - jnp.where(sub > m, lead, 0.0) * row
            for v in range(b + 1, count):
                work[v] = work[v] - cols[m][v - b] * row
        done.append(work[b] * scale)
    return jnp.concatenate(done, axis=0)[:, :MODES]


def basis_kernel(scale, mine_ref, other_ref, start_ref, feats_ref, first_ref, before_ref, basis_ref, modes_ref, rows_ref, out_ref):
    first = is_even("row")
    mine, other = mine_ref[...], other_ref[...]
    cross = jnp.where(first, mine, other)[:HALF]
    second = jnp.where(first, other, mine)
    folded = second[:HALF]
    i = lax.broadcasted_iota(jnp.int32, (HALF, HALF), 0)
    j = lax.broadcasted_iota(jnp.int32, (HALF, HALF), 1)
    flipped = folded.T
    top = jnp.where(i <= j, folded, flipped)
    low = jnp.where(i > j, folded, jnp.where(i < j, flipped, second[HALF : HALF + 1]))
    gram = jnp.concatenate(
        [jnp.concatenate([top, cross], axis=1), jnp.concatenate([cross.T, low], axis=1)], axis=0
    )
    gram = gram * scale
    basis = start_ref[...]
    for sweep in range(SWEEPS):
        stacked = jnp.dot(basis, gram, precision=HIGHEST, preferred_element_type=F32)
        inner = lax.dot_general(
            stacked, stacked, (((1,), (1,)), ((), ())), precision=HIGHEST, preferred_element_type=F32
        )
        basis = jnp.dot(inverse_factor(inner), stacked, precision=HIGHEST, preferred_element_type=F32)
    basis_ref[...] = jnp.dot(basis, frame_order(1), precision=HIGHEST, preferred_element_type=F32)
    twice = jnp.concatenate([basis, basis], axis=0)
    before = jnp.concatenate([before_ref[:8], before_ref[8:]], axis=1)
    before = jnp.concatenate([before, pltpu.roll(before, 4, 0)], axis=0)
    before = jnp.where(lax.axis_index("col") == 0, first_ref[...].astype(F32), before)
    cell = jnp.where(second_cells(), before, feats_ref[BLOCKS - 1].astype(F32)).astype(BF16)
    flat = jnp.concatenate([feats_ref[0 : BLOCKS - 1].reshape(16 * BLOCKS - 16, FRAMES), cell], axis=0)
    rows_ref[...] = lax.dot_general(
        flat, twice.astype(BF16), (((1,), (1,)), ((), ())), preferred_element_type=F32
    )
    left = lax.broadcasted_iota(jnp.int32, (BLOCKS, 2 * MODES), 1) < MODES
    for row in range(2):
        for half in range(2):
            for cell in range(2):
                at = 8 * row + 4 * cell + 2 * half
                field = jnp.where(
                    left, rows_ref[pl.ds(at, BLOCKS, stride=16), :], rows_ref[pl.ds(at + 1, BLOCKS, stride=16), :]
                )
                if cell:
                    field = pltpu.roll(field, 1, 0)
                out_ref[pl.ds(64 * row + 32 * half + 1 - cell, BLOCKS, stride=2), :] = field
            modes_ref[row, :, 128 * half : 128 * half + 128] = out_ref[64 * row + 32 * half : 64 * row + 32 * half + 32]


def call(kernel, outs, n_in, scratch=()):
    return pl.pallas_call(
        kernel,
        out_shape=[jax.ShapeDtypeStruct(shape, dtype) for shape, dtype in outs],
        in_specs=[VMEM] * n_in,
        out_specs=[VMEM] * len(outs),
        scratch_shapes=list(scratch),
        compiler_params=PARAMS,
    )


def pairs(size, start):
    swaps = []
    for i in range(start, size - 1, 2):
        swaps += [(i, i + 1), (i + 1, i)]
    return swaps


def on_device(video, filters, start_basis):
    size_row, size_col = lax.axis_size("row"), lax.axis_size("col")
    near, far = pairs(size_row, 0), pairs(size_row, 1)
    to_left = [(i + 1, i) for i in range(size_col - 1)]

    send = ((REACH * COLS + 16, FRAMES), BF16)
    tile = ((BLOCKS, 112, 3 * HALF), BF16)
    rim = ((2, COLS, 3 * HALF), F32)
    rows = pltpu.VMEM(((FRAMES + 1) * ROWS, COLS), F32)
    send_a, send_b, x, rim = call(own_kernel, [send, send, tile, rim], 1, [rows])(video)
    got_a = lax.ppermute(send_a, "row", near)
    got_b = lax.ppermute(send_b, "row", far)

    (band,) = call(band_kernel, [((128, 256), BF16)], 1, [pltpu.VMEM((16, 128), F32)])(
        jnp.transpose(filters, (0, 2, 1, 3))
    )
    x, side = call(halo_kernel, [tile, ((112, 3 * HALF), BF16)], 5)(got_a, got_b, x, rim, band)
    side = lax.ppermute(side, "col", to_left)
    feats_shape = ((BLOCKS, 16, FRAMES), BF16)
    inner, first = call(inner_kernel, [feats_shape, ((16, FRAMES), BF16)], 2)(band, x)
    part = ((SUMMED + 16, HALF), F32)
    feats, mine, other = call(edge_kernel, [feats_shape, part, part], 5)(band, x, side, inner, first)

    mine = mine + lax.ppermute(other, "row", near)
    summed = lax.broadcasted_iota(jnp.int32, mine.shape, 0) < SUMMED
    step = 2
    while step < size_row:
        got = lax.ppermute(mine, "row", [(i, i ^ step) for i in range(size_row)])
        mine = jnp.where(summed, mine + got, mine)
        step *= 2
    step = 1
    col = lax.axis_index("col")
    before = jnp.zeros((16, HALF), F32)
    start = start_basis.T
    while step < size_col:
        if 2 * step >= size_col:
            mine, start = lax.optimization_barrier((mine, start))
            (start,) = call(start_kernel, [((MODES, FRAMES), F32)], 1)(start)
        got = lax.ppermute(mine, "col", [(i, i ^ step) for i in range(size_col)])
        mine = jnp.where(summed, mine + got, got)
        before = jnp.where((col & (2 * step - 1)) == step, got[SUMMED:], before)
        step *= 2
    other = lax.ppermute(mine, "row", near)

    features = ORIENT * (size_row * ROWS // 4) * (size_col * COLS // 4)
    kernel = functools.partial(basis_kernel, 1.0 / features)
    basis, modes = call(
        kernel,
        [((MODES, FRAMES), F32), ((ROWS // 4, COLS // 4, ORIENT * MODES), F32)],
        6,
        [pltpu.VMEM((FRAMES, 2 * MODES), F32), pltpu.VMEM((128, 128), F32)],
    )(mine, other, start, feats, first, before)
    return basis.T, modes


def solution(mesh):
    return jax.shard_map(
        on_device,
        mesh=mesh,
        in_specs=(P("grp", "row", "col"), P(), P()),
        out_specs=(P("grp", None), P(("grp", "row"), "col", None)),
        check_vma=False,
    )
```

```python
import functools

import jax
import jax.numpy as jnp
from jax import lax
from jax.experimental import pallas as pl
from jax.experimental.pallas import tpu as pltpu
from jax.sharding import PartitionSpec as P

FRAMES = 256
HALF = FRAMES // 2
MODES = 64
ORIENT = 4
TAPS = 7
REACH = 3
SWEEPS = 2
ROWS = 8
COLS = 128
SUMMED = HALF + 8
BLOCKS = 16
F32 = jnp.float32
BF16 = jnp.bfloat16
HIGHEST = lax.Precision.HIGHEST
PARAMS = pltpu.CompilerParams(vmem_limit_bytes=24 * 1024 * 1024)
VMEM = pl.BlockSpec(memory_space=pltpu.VMEM)


def turned(rows_ref, row, group):
    return rows_ref[pl.ds(group * ROWS + row, HALF, stride=2 * ROWS), :].T


def blocked(upper, lower):
    both = [part.reshape(BLOCKS, 8, HALF) for part in (upper, lower)]
    return jnp.concatenate(both, axis=1).astype(BF16)


def is_even(axis):
    return (lax.axis_index(axis) & 1) == 0


def send_kernel(video_ref, rows_ref, send_a_ref, send_b_ref):
    even = is_even("row")
    rows_ref[...] = video_ref[...].astype(F32).reshape(rows_ref.shape)
    for group in range(2):
        lanes = slice(HALF * group, HALF * group + HALF)
        for i in range(REACH):
            first, last = turned(rows_ref, i, group), turned(rows_ref, ROWS - REACH + i, group)
            at = slice(COLS * i, COLS * i + COLS)
            send_a_ref[at, lanes] = jnp.where(even, last, first).astype(BF16)
            send_b_ref[at, lanes] = jnp.where(even, first, last).astype(BF16)
    fill = jnp.zeros((8, COLS), F32)
    final = rows_ref[FRAMES * ROWS : FRAMES * ROWS + ROWS, :]
    shifted = pltpu.roll(final, REACH, 0)
    first, last = (jnp.concatenate([part, fill], axis=0).astype(BF16) for part in (final, shifted))
    for ref, chosen in ((send_a_ref, jnp.where(even, last, first)), (send_b_ref, jnp.where(even, first, last))):
        ref[REACH * COLS : REACH * COLS + 16, 0:COLS] = chosen
        ref[REACH * COLS : REACH * COLS + 16, COLS : 2 * COLS] = chosen


def own_kernel(rows_ref, a_ref, x_ref, rim_ref, side_ref, diag_ref):
    even = is_even("row")
    fill = jnp.zeros((8, HALF), F32)
    near = expanded(a_ref[...].astype(F32), 8)
    for group in range(3):
        lanes = slice(HALF * group, HALF * group + HALF)
        tiles = [turned(rows_ref, row, group) for row in range(ROWS)]
        for pair in range(3):
            x_ref[:, 32 + 16 * pair : 48 + 16 * pair, lanes] = blocked(tiles[2 * pair + 1], tiles[2 * pair + 2])
        rim_ref[0, :, lanes] = tiles[0]
        rim_ref[1, :, lanes] = tiles[ROWS - 1]
        heads = [tile[:8] for tile in tiles]
        sent = heads + [row[group] for row in near] + [fill]
        side_ref[:, lanes] = jnp.concatenate(sent, axis=0).astype(BF16)
        chosen = [jnp.where(even, heads[i], heads[ROWS - REACH + i]) for i in range(REACH)] + [fill]
        diag_ref[:, lanes] = jnp.concatenate(chosen, axis=0).astype(BF16)


def expanded(got, count):
    final = lax.broadcasted_iota(jnp.int32, (count, HALF), 1) == HALF - 1
    ends = got[REACH * COLS : REACH * COLS + 8, :COLS].T
    rows = []
    for i in range(REACH):
        tile = got[COLS * i : COLS * i + count]
        late = jnp.where(final, ends[:count, i : i + 1], pltpu.roll(tile[:, :HALF], HALF - 1, 1))
        rows.append([tile[:, :HALF], tile[:, HALF:], late])
    return rows


def band_kernel(filters_ref, band_ref, taps_ref):
    taps_ref[...] = jnp.zeros((16, 128), F32)
    for orient in range(ORIENT):
        for part in range(2):
            for i in range(TAPS):
                line = filters_ref[orient, i, part : part + 1, :]
                for cell in range(2):
                    row, lane = 8 * part + 4 * cell + orient, 64 * cell + 8 * i
                    taps_ref[row : row + 1, lane : lane + TAPS] = line
    taps = taps_ref[...]
    high = taps.astype(BF16)
    low = (taps - high.astype(F32)).astype(BF16)
    parts = jnp.concatenate([high, low], axis=0)
    tap = lax.broadcasted_iota(jnp.int32, (128, 128), 0)
    lane = lax.broadcasted_iota(jnp.int32, (128, 128), 1)
    column = ((lane >> 6) << 3) | (lane & 7)
    row_hit = ((lane >> 3) & 7) == ((tap >> 3) & 7)
    ahead = column - (tap & 7) - 1 - 4 * (tap >> 6)
    for j in range(4):
        select = jnp.where(row_hit & (ahead == j), 1.0, 0.0).astype(BF16)
        base = jnp.dot(parts, select, preferred_element_type=F32)
        for i in range(2):
            start = (4 * i + j) * 16
            rolled = (pltpu.roll(base, 8, 1) if i else base).astype(BF16)
            band_ref[start : start + 16, 0:128] = rolled[:16]
            band_ref[start : start + 16, 128:256] = rolled[16:]


def start_kernel(start_ref, basis_ref):
    basis_ref[...] = jnp.dot(start_ref[...], frame_order(0), precision=HIGHEST, preferred_element_type=F32)


def frame_order(axis):
    frame = lax.broadcasted_iota(jnp.int32, (FRAMES, FRAMES), axis)
    lane = lax.broadcasted_iota(jnp.int32, (FRAMES, FRAMES), 1 - axis)
    return jnp.where(frame == 2 * (lane & (HALF - 1)) + (lane >> 7), 1.0, 0.0).astype(F32)


def halo_kernel(a_ref, b_ref, x_in_ref, rim_ref, band_ref, x_ref):
    even = is_even("row")
    got_a, got_b = a_ref[...], b_ref[...]
    above = expanded(jnp.where(even, got_b, got_a).astype(F32), COLS)
    below = expanded(jnp.where(even, got_a, got_b).astype(F32), COLS)
    for group in range(3):
        lanes = slice(HALF * group, HALF * group + HALF)
        x_ref[:, 0:16, lanes] = blocked(above[0][group], above[1][group])
        x_ref[:, 16:32, lanes] = blocked(above[2][group], rim_ref[0, :, lanes])
        x_ref[:, 80:96, lanes] = blocked(rim_ref[1, :, lanes], below[0][group])
        x_ref[:, 96:112, lanes] = blocked(below[1][group], below[2][group])
    x_ref[:, 32:80, :] = x_in_ref[:, 32:80, :]


def block_feats(band_ref, left, right):
    pooled = []
    for cell in range(2):
        windows = []
        for half in range(2):
            at = 16 * (2 * cell + half)
            windows.append(jnp.concatenate([left[at : at + 64], right[at : at + 64]], axis=0))
        window = jnp.concatenate(
            [windows[0][:, :FRAMES], windows[1][:, :FRAMES], windows[0][:, FRAMES:], windows[1][:, FRAMES:]], axis=1
        )
        window = jnp.concatenate([window, window], axis=0)
        resp = jnp.dot(band_ref[...], window, preferred_element_type=F32)
        total = [None, None]
        for half in range(2):
            starts = (FRAMES * half, FRAMES * half + HALF, 2 * FRAMES + HALF * half)
            for pixel in range(8):
                at = 16 * pixel
                real = [resp[at : at + 8, s : s + HALF] for s in starts]
                imag = [resp[at + 8 : at + 16, s : s + HALF] for s in starts]
                for g in range(2):
                    prod_real = real[g + 1] * real[g] + imag[g + 1] * imag[g]
                    prod_imag = imag[g + 1] * real[g] - real[g + 1] * imag[g]
                    motion = prod_imag * lax.rsqrt(prod_real * prod_real + prod_imag * prod_imag + 1.0)
                    total[g] = motion if total[g] is None else total[g] + motion
        pooled.append(jnp.concatenate(total, axis=1) * (1.0 / 16.0))
    return jnp.concatenate(pooled, axis=0)


def second_cells():
    return (lax.broadcasted_iota(jnp.int32, (16, FRAMES), 0) & 4) == 4


def inner_kernel(band_ref, x_ref, feats_ref, start_ref):
    def body(step, carry):
        for i in range(3):
            block = 3 * step + i
            feats_ref[block] = block_feats(band_ref, x_ref[block], x_ref[block + 1]).astype(BF16)
        return carry

    lax.fori_loop(0, (BLOCKS - 1) // 3, body, 0)
    start = block_feats(band_ref, jnp.zeros((112, 3 * HALF), BF16), x_ref[0])
    begins = lax.axis_index("col") == 0
    start_ref[...] = jnp.where(second_cells() & begins, start, 0.0).astype(BF16)


def edge_kernel(band_ref, x_ref, side_ref, diag_ref, inner_ref, start_ref, feats_ref, mine_ref, other_ref):
    even = is_even("row")
    side = side_ref[...].astype(F32)
    near, far = side[8 * ROWS : 8 * ROWS + 8 * REACH], diag_ref[...].astype(F32)[: 8 * REACH]
    rows = [jnp.where(even, far, near), side[: 8 * ROWS], jnp.where(even, near, far)]
    edge = block_feats(band_ref, x_ref[BLOCKS - 1], jnp.concatenate(rows, axis=0).astype(BF16))
    ends = lax.axis_index("col") == lax.axis_size("col") - 1
    feats_ref[0 : BLOCKS - 1] = inner_ref[0 : BLOCKS - 1]
    edge = jnp.where(second_cells() & ends, 0.0, edge).astype(BF16)
    feats_ref[BLOCKS - 1] = edge
    edge = edge.astype(F32)
    flat = jnp.concatenate([feats_ref[...].reshape(16 * BLOCKS, FRAMES), start_ref[...]], axis=0)
    gram = lax.dot_general(flat, flat, (((0,), (0,)), ((), ())), preferred_element_type=F32)
    top, cross, low = gram[:HALF, :HALF], gram[:HALF, HALF:], gram[HALF:, HALF:]
    i = lax.broadcasted_iota(jnp.int32, (HALF, HALF), 0)
    j = lax.broadcasted_iota(jnp.int32, (HALF, HALF), 1)
    folded = jnp.where(i <= j, top, low)
    diagonal = jnp.sum(jnp.where(i == j, low, 0.0), axis=0, keepdims=True)
    first = is_even("row")
    spare = jnp.broadcast_to(diagonal, (8, HALF))
    mine_ref[0:HALF] = jnp.where(first, cross, folded)
    mine_ref[HALF:SUMMED] = spare
    passed = jnp.where(second_cells()[:8], edge[:8], pltpu.roll(edge[8:], 4, 0))
    mine_ref[SUMMED : SUMMED + 8] = passed[:, :HALF]
    mine_ref[SUMMED + 8 : SUMMED + 16] = passed[:, HALF:]
    other_ref[0:HALF] = jnp.where(first, folded, cross)
    other_ref[HALF:SUMMED] = spare
    other_ref[SUMMED : SUMMED + 16] = jnp.zeros((16, HALF), F32)


def inverse_factor(inner):
    count = MODES // 8
    shape = (8, 2 * MODES)
    i = lax.broadcasted_iota(jnp.int32, (MODES, MODES), 0)
    j = lax.broadcasted_iota(jnp.int32, (MODES, MODES), 1)
    work = jnp.concatenate([jnp.where(i == j, 1.0, 0.0), inner], axis=1)
    work = [work[8 * v : 8 * v + 8] for v in range(count)]
    sub = lax.broadcasted_iota(jnp.int32, shape, 0)
    done = []
    for b in range(count):
        lane = MODES + 8 * b
        cols = [[jnp.broadcast_to(work[v][:, lane + m : lane + m + 1], shape) for v in range(b, count)] for m in range(8)]
        scale = jnp.zeros(shape, F32)
        for m in range(8):
            lead = cols[m][0]
            pivot = jnp.broadcast_to(lead[m : m + 1], shape)
            inverse = 1.0 / pivot
            scale = jnp.where(sub == m, lax.rsqrt(pivot), scale)
            row = jnp.broadcast_to(work[b][m : m + 1], shape) * inverse
            for q in range(m + 1, 8):
                times = jnp.broadcast_to(lead[q : q + 1], shape) * inverse
                cols[q] = [c - d * times for c, d in zip(cols[q], cols[m])]
            work[b] = work[b] - jnp.where(sub > m, lead, 0.0) * row
            for v in range(b + 1, count):
                work[v] = work[v] - cols[m][v - b] * row
        done.append(work[b] * scale)
    return jnp.concatenate(done, axis=0)[:, :MODES]


def basis_kernel(scale, mine_ref, other_ref, start_ref, feats_ref, first_ref, before_ref, basis_ref, modes_ref, rows_ref, out_ref):
    first = is_even("row")
    mine, other = mine_ref[...], other_ref[...]
    cross = jnp.where(first, mine, other)[:HALF]
    second = jnp.where(first, other, mine)
    folded = second[:HALF]
    i = lax.broadcasted_iota(jnp.int32, (HALF, HALF), 0)
    j = lax.broadcasted_iota(jnp.int32, (HALF, HALF), 1)
    flipped = folded.T
    top = jnp.where(i <= j, folded, flipped)
    low = jnp.where(i > j, folded, jnp.where(i < j, flipped, second[HALF : HALF + 1]))
    gram = jnp.concatenate(
        [jnp.concatenate([top, cross], axis=1), jnp.concatenate([cross.T, low], axis=1)], axis=0
    )
    gram = gram * scale
    basis = start_ref[...]
    for sweep in range(SWEEPS):
        stacked = jnp.dot(basis, gram, precision=HIGHEST, preferred_element_type=F32)
        inner = lax.dot_general(
            stacked, stacked, (((1,), (1,)), ((), ())), precision=HIGHEST, preferred_element_type=F32
        )
        basis = jnp.dot(inverse_factor(inner), stacked, precision=HIGHEST, preferred_element_type=F32)
    basis_ref[...] = jnp.dot(basis, frame_order(1), precision=HIGHEST, preferred_element_type=F32)
    twice = jnp.concatenate([basis, basis], axis=0)
    before = jnp.concatenate([before_ref[:8], before_ref[8:]], axis=1)
    before = jnp.concatenate([before, pltpu.roll(before, 4, 0)], axis=0)
    before = jnp.where(lax.axis_index("col") == 0, first_ref[...].astype(F32), before)
    cell = jnp.where(second_cells(), before, feats_ref[BLOCKS - 1].astype(F32)).astype(BF16)
    flat = jnp.concatenate([feats_ref[0 : BLOCKS - 1].reshape(16 * BLOCKS - 16, FRAMES), cell], axis=0)
    rows_ref[...] = lax.dot_general(
        flat, twice.astype(BF16), (((1,), (1,)), ((), ())), preferred_element_type=F32
    )
    left = lax.broadcasted_iota(jnp.int32, (BLOCKS, 2 * MODES), 1) < MODES
    for row in range(2):
        for half in range(2):
            for cell in range(2):
                at = 8 * row + 4 * cell + 2 * half
                field = jnp.where(
                    left, rows_ref[pl.ds(at, BLOCKS, stride=16), :], rows_ref[pl.ds(at + 1, BLOCKS, stride=16), :]
                )
                if cell:
                    field = pltpu.roll(field, 1, 0)
                out_ref[pl.ds(64 * row + 32 * half + 1 - cell, BLOCKS, stride=2), :] = field
            modes_ref[row, :, 128 * half : 128 * half + 128] = out_ref[64 * row + 32 * half : 64 * row + 32 * half + 32]


def call(kernel, outs, n_in, scratch=()):
    return pl.pallas_call(
        kernel,
        out_shape=[jax.ShapeDtypeStruct(shape, dtype) for shape, dtype in outs],
        in_specs=[VMEM] * n_in,
        out_specs=[VMEM] * len(outs),
        scratch_shapes=list(scratch),
        compiler_params=PARAMS,
    )


def pairs(size, start):
    swaps = []
    for i in range(start, size - 1, 2):
        swaps += [(i, i + 1), (i + 1, i)]
    return swaps


def on_device(video, filters, start_basis):
    size_row, size_col = lax.axis_size("row"), lax.axis_size("col")
    near, far = pairs(size_row, 0), pairs(size_row, 1)
    to_left = [(i + 1, i) for i in range(size_col - 1)]

    across = [(a * size_col + i, b * size_col + j) for a, b in far for i, j in to_left]
    send = ((REACH * COLS + 16, FRAMES), BF16)
    tile = ((BLOCKS, 112, 3 * HALF), BF16)
    rim = ((2, COLS, 3 * HALF), F32)
    rows = (((FRAMES + 1) * ROWS, COLS), F32)
    rows, send_a, send_b = call(send_kernel, [rows, send, send], 1)(video)
    got_a = lax.ppermute(send_a, "row", near)
    got_b = lax.ppermute(send_b, "row", far)
    outs = [tile, rim, ((96, 3 * HALF), BF16), ((32, 3 * HALF), BF16)]
    x, rim, side, diag = call(own_kernel, outs, 2)(rows, got_a)
    side = lax.ppermute(side, "col", to_left)
    diag = lax.ppermute(diag, ("row", "col"), across)

    (band,) = call(band_kernel, [((128, 256), BF16)], 1, [pltpu.VMEM((16, 128), F32)])(
        jnp.transpose(filters, (0, 2, 1, 3))
    )
    (x,) = call(halo_kernel, [tile], 5)(got_a, got_b, x, rim, band)
    feats_shape = ((BLOCKS, 16, FRAMES), BF16)
    inner, first = call(inner_kernel, [feats_shape, ((16, FRAMES), BF16)], 2)(band, x)
    part = ((SUMMED + 16, HALF), F32)
    feats, mine, other = call(edge_kernel, [feats_shape, part, part], 6)(band, x, side, diag, inner, first)

    mine = mine + lax.ppermute(other, "row", near)
    summed = lax.broadcasted_iota(jnp.int32, mine.shape, 0) < SUMMED
    step = 2
    while step < size_row:
        got = lax.ppermute(mine, "row", [(i, i ^ step) for i in range(size_row)])
        mine = jnp.where(summed, mine + got, mine)
        step *= 2
    step = 1
    col = lax.axis_index("col")
    before = jnp.zeros((16, HALF), F32)
    start = start_basis.T
    while step < size_col:
        if 2 * step >= size_col:
            mine, start = lax.optimization_barrier((mine, start))
            (start,) = call(start_kernel, [((MODES, FRAMES), F32)], 1)(start)
        got = lax.ppermute(mine, "col", [(i, i ^ step) for i in range(size_col)])
        mine = jnp.where(summed, mine + got, got)
        before = jnp.where((col & (2 * step - 1)) == step, got[SUMMED:], before)
        step *= 2
    other = lax.ppermute(mine, "row", near)

    features = ORIENT * (size_row * ROWS // 4) * (size_col * COLS // 4)
    kernel = functools.partial(basis_kernel, 1.0 / features)
    basis, modes = call(
        kernel,
        [((MODES, FRAMES), F32), ((ROWS // 4, COLS // 4, ORIENT * MODES), F32)],
        6,
        [pltpu.VMEM((FRAMES, 2 * MODES), F32), pltpu.VMEM((128, 128), F32)],
    )(mine, other, start, feats, first, before)
    return basis.T, modes


def solution(mesh):
    return jax.shard_map(
        on_device,
        mesh=mesh,
        in_specs=(P("grp", "row", "col"), P(), P()),
        out_specs=(P("grp", None), P(("grp", "row"), "col", None)),
        check_vma=False,
    )
```

```python
import functools

import jax
import jax.numpy as jnp
from jax import lax
from jax.experimental import pallas as pl
from jax.experimental.pallas import tpu as pltpu
from jax.sharding import PartitionSpec as P

FRAMES = 256
HALF = FRAMES // 2
MODES = 64
ORIENT = 4
TAPS = 7
REACH = 3
SWEEPS = 2
ROWS = 8
COLS = 128
SUMMED = HALF + 8
BLOCKS = 16
UNROLL = 4
F32 = jnp.float32
BF16 = jnp.bfloat16
HIGHEST = lax.Precision.HIGHEST
PARAMS = pltpu.CompilerParams(vmem_limit_bytes=24 * 1024 * 1024)
VMEM = pl.BlockSpec(memory_space=pltpu.VMEM)


def turned(rows_ref, row, group):
    return rows_ref[pl.ds(group * ROWS + row, HALF, stride=2 * ROWS), :].T


def blocked(upper, lower):
    both = [part.reshape(BLOCKS, 8, HALF) for part in (upper, lower)]
    return jnp.concatenate(both, axis=1).astype(BF16)


def is_even(axis):
    return (lax.axis_index(axis) & 1) == 0


def send_kernel(video_ref, rows_ref, send_a_ref, send_b_ref):
    even = is_even("row")
    rows_ref[...] = video_ref[...].astype(F32).reshape(rows_ref.shape)
    for group in range(2):
        lanes = slice(HALF * group, HALF * group + HALF)
        for i in range(REACH):
            first, last = turned(rows_ref, i, group), turned(rows_ref, ROWS - REACH + i, group)
            at = slice(COLS * i, COLS * i + COLS)
            send_a_ref[at, lanes] = jnp.where(even, last, first).astype(BF16)
            send_b_ref[at, lanes] = jnp.where(even, first, last).astype(BF16)
    fill = jnp.zeros((8, COLS), F32)
    final = rows_ref[FRAMES * ROWS : FRAMES * ROWS + ROWS, :]
    shifted = pltpu.roll(final, REACH, 0)
    first, last = (jnp.concatenate([part, fill], axis=0).astype(BF16) for part in (final, shifted))
    for ref, chosen in ((send_a_ref, jnp.where(even, last, first)), (send_b_ref, jnp.where(even, first, last))):
        ref[REACH * COLS : REACH * COLS + 16, 0:COLS] = chosen
        ref[REACH * COLS : REACH * COLS + 16, COLS : 2 * COLS] = chosen


def own_kernel(rows_ref, a_ref, x_ref, rim_ref, side_ref, diag_ref):
    even = is_even("row")
    fill = jnp.zeros((8, HALF), F32)
    near = expanded(a_ref[...].astype(F32), 8)
    for group in range(3):
        lanes = slice(HALF * group, HALF * group + HALF)
        tiles = [turned(rows_ref, row, group) for row in range(ROWS)]
        for pair in range(3):
            x_ref[:, 32 + 16 * pair : 48 + 16 * pair, lanes] = blocked(tiles[2 * pair + 1], tiles[2 * pair + 2])
        rim_ref[0, :, lanes] = tiles[0]
        rim_ref[1, :, lanes] = tiles[ROWS - 1]
        heads = [tile[:8] for tile in tiles]
        sent = heads + [row[group] for row in near] + [fill]
        side_ref[:, lanes] = jnp.concatenate(sent, axis=0).astype(BF16)
        chosen = [jnp.where(even, heads[i], heads[ROWS - REACH + i]) for i in range(REACH)] + [fill]
        diag_ref[:, lanes] = jnp.concatenate(chosen, axis=0).astype(BF16)


def expanded(got, count):
    final = lax.broadcasted_iota(jnp.int32, (count, HALF), 1) == HALF - 1
    ends = got[REACH * COLS : REACH * COLS + 8, :COLS].T
    rows = []
    for i in range(REACH):
        tile = got[COLS * i : COLS * i + count]
        late = jnp.where(final, ends[:count, i : i + 1], pltpu.roll(tile[:, :HALF], HALF - 1, 1))
        rows.append([tile[:, :HALF], tile[:, HALF:], late])
    return rows


def band_kernel(filters_ref, band_ref, taps_ref):
    taps_ref[...] = jnp.zeros((16, 128), F32)
    for orient in range(ORIENT):
        for part in range(2):
            for i in range(TAPS):
                line = filters_ref[orient, i, part : part + 1, :]
                for cell in range(2):
                    row, lane = 8 * part + 4 * cell + orient, 64 * cell + 8 * i
                    taps_ref[row : row + 1, lane : lane + TAPS] = line
    taps = taps_ref[...]
    high = taps.astype(BF16)
    low = (taps - high.astype(F32)).astype(BF16)
    parts = jnp.concatenate([high, low], axis=0)
    tap = lax.broadcasted_iota(jnp.int32, (128, 128), 0)
    lane = lax.broadcasted_iota(jnp.int32, (128, 128), 1)
    column = ((lane >> 6) << 3) | (lane & 7)
    row_hit = ((lane >> 3) & 7) == ((tap >> 3) & 7)
    ahead = column - (tap & 7) - 1 - 4 * (tap >> 6)
    for j in range(4):
        select = jnp.where(row_hit & (ahead == j), 1.0, 0.0).astype(BF16)
        base = jnp.dot(parts, select, preferred_element_type=F32)
        for i in range(2):
            start = (4 * i + j) * 16
            rolled = (pltpu.roll(base, 8, 1) if i else base).astype(BF16)
            band_ref[start : start + 16, 0:128] = rolled[:16]
            band_ref[start : start + 16, 128:256] = rolled[16:]


def start_kernel(start_ref, basis_ref):
    basis_ref[...] = jnp.dot(start_ref[...], frame_order(0), precision=HIGHEST, preferred_element_type=F32)


def frame_order(axis):
    frame = lax.broadcasted_iota(jnp.int32, (FRAMES, FRAMES), axis)
    lane = lax.broadcasted_iota(jnp.int32, (FRAMES, FRAMES), 1 - axis)
    return jnp.where(frame == 2 * (lane & (HALF - 1)) + (lane >> 7), 1.0, 0.0).astype(F32)


def place_halo(a_ref, b_ref, x_in_ref, rim_ref, x_ref):
    even = is_even("row")
    got_a, got_b = a_ref[...], b_ref[...]
    above = expanded(jnp.where(even, got_b, got_a).astype(F32), COLS)
    below = expanded(jnp.where(even, got_a, got_b).astype(F32), COLS)
    for group in range(3):
        lanes = slice(HALF * group, HALF * group + HALF)
        x_ref[1:, 0:16, lanes] = blocked(above[0][group], above[1][group])
        x_ref[1:, 16:32, lanes] = blocked(above[2][group], rim_ref[0, :, lanes])
        x_ref[1:, 80:96, lanes] = blocked(rim_ref[1, :, lanes], below[0][group])
        x_ref[1:, 96:112, lanes] = blocked(below[1][group], below[2][group])
    x_ref[1:, 32:80, :] = x_in_ref[:, 32:80, :]
    x_ref[0] = jnp.zeros((112, 3 * HALF), BF16)


def block_feats(band_ref, left, right):
    pooled = []
    for cell in range(2):
        windows = []
        for half in range(2):
            at = 16 * (2 * cell + half)
            windows.append(jnp.concatenate([left[at : at + 64], right[at : at + 64]], axis=0))
        window = jnp.concatenate(
            [windows[0][:, :FRAMES], windows[1][:, :FRAMES], windows[0][:, FRAMES:], windows[1][:, FRAMES:]], axis=1
        )
        window = jnp.concatenate([window, window], axis=0)
        resp = jnp.dot(band_ref[...], window, preferred_element_type=F32)
        total = [None, None]
        for half in range(2):
            starts = (FRAMES * half, FRAMES * half + HALF, 2 * FRAMES + HALF * half)
            for pixel in range(8):
                at = 16 * pixel
                real = [resp[at : at + 8, s : s + HALF] for s in starts]
                imag = [resp[at + 8 : at + 16, s : s + HALF] for s in starts]
                for g in range(2):
                    prod_real = real[g + 1] * real[g] + imag[g + 1] * imag[g]
                    prod_imag = imag[g + 1] * real[g] - real[g + 1] * imag[g]
                    motion = prod_imag * lax.rsqrt(prod_real * prod_real + prod_imag * prod_imag + 1.0)
                    total[g] = motion if total[g] is None else total[g] + motion
        pooled.append(jnp.concatenate(total, axis=1) * (1.0 / 16.0))
    return jnp.concatenate(pooled, axis=0)


def second_cells():
    return (lax.broadcasted_iota(jnp.int32, (16, FRAMES), 0) & 4) == 4


def inner_kernel(a_ref, b_ref, x_in_ref, rim_ref, band_ref, feats_ref, x_ref):
    place_halo(a_ref, b_ref, x_in_ref, rim_ref, x_ref)

    def body(step, carry):
        for i in range(UNROLL):
            block = UNROLL * step + i
            feats_ref[block] = block_feats(band_ref, x_ref[block], x_ref[block + 1]).astype(BF16)
        return carry

    lax.fori_loop(0, BLOCKS // UNROLL, body, 0)
    begins = lax.axis_index("col") == 0
    feats_ref[0] = jnp.where(second_cells() & begins, feats_ref[0].astype(F32), 0.0).astype(BF16)


def edge_kernel(band_ref, x_ref, side_ref, diag_ref, inner_ref, edge_ref, mine_ref, other_ref, passed_ref):
    even = is_even("row")
    side = side_ref[...].astype(F32)
    near, far = side[8 * ROWS : 8 * ROWS + 8 * REACH], diag_ref[...].astype(F32)[: 8 * REACH]
    rows = [jnp.where(even, far, near), side[: 8 * ROWS], jnp.where(even, near, far)]
    edge = block_feats(band_ref, x_ref[BLOCKS], jnp.concatenate(rows, axis=0).astype(BF16))
    ends = lax.axis_index("col") == lax.axis_size("col") - 1
    edge = jnp.where(second_cells() & ends, 0.0, edge).astype(BF16)
    edge_ref[...] = edge
    flat = jnp.concatenate([inner_ref[...].reshape(16 * BLOCKS, FRAMES), edge], axis=0)
    gram = lax.dot_general(flat, flat, (((0,), (0,)), ((), ())), preferred_element_type=F32)
    top, cross, low = gram[:HALF, :HALF], gram[:HALF, HALF:], gram[HALF:, HALF:]
    i = lax.broadcasted_iota(jnp.int32, (HALF, HALF), 0)
    j = lax.broadcasted_iota(jnp.int32, (HALF, HALF), 1)
    folded = jnp.where(i <= j, top, low)
    diagonal = jnp.sum(jnp.where(i == j, low, 0.0), axis=0, keepdims=True)
    first = is_even("row")
    spare = jnp.broadcast_to(diagonal, (8, HALF))
    mine_ref[0:HALF] = jnp.where(first, cross, folded)
    mine_ref[HALF:SUMMED] = spare
    other_ref[0:HALF] = jnp.where(first, folded, cross)
    other_ref[HALF:SUMMED] = spare
    edge = edge.astype(F32)
    passed = jnp.where(second_cells()[:8], edge[:8], pltpu.roll(edge[8:], 4, 0))
    passed_ref[0:8] = passed[:, :HALF]
    passed_ref[8:16] = passed[:, HALF:]


def inverse_factor(inner):
    count = MODES // 8
    shape = (8, 2 * MODES)
    i = lax.broadcasted_iota(jnp.int32, (MODES, MODES), 0)
    j = lax.broadcasted_iota(jnp.int32, (MODES, MODES), 1)
    work = jnp.concatenate([jnp.where(i == j, 1.0, 0.0), inner], axis=1)
    work = [work[8 * v : 8 * v + 8] for v in range(count)]
    sub = lax.broadcasted_iota(jnp.int32, shape, 0)

    def columns(b):
        lanes = [MODES + 8 * b + m for m in range(8)]
        return {v: [jnp.broadcast_to(work[v][:, k : k + 1], shape) for k in lanes] for v in range(b, count)}

    def spread(tile, row):
        return jnp.broadcast_to(tile[row : row + 1], shape)

    cols = columns(0)
    done = []
    for b in range(count):
        ahead = columns(b + 1)
        scale = jnp.zeros(shape, F32)
        for m in range(8):
            lead = cols[b][m]
            pivot = spread(lead, m)
            inverse = 1.0 / pivot
            scale = jnp.where(sub == m, lax.rsqrt(pivot), scale)
            row = spread(work[b], m) * inverse
            for q in range(m + 1, 8):
                times = spread(lead, q) * inverse
                for v in cols:
                    cols[v][q] = cols[v][q] - cols[v][m] * times
            for q in range(8 if ahead else 0):
                times = spread(cols[b + 1][m], q) * inverse
                for v in ahead:
                    ahead[v][q] = ahead[v][q] - cols[v][m] * times
            work[b] = work[b] - jnp.where(sub > m, lead, 0.0) * row
            for v in range(b + 1, count):
                work[v] = work[v] - cols[v][m] * row
        done.append(work[b] * scale)
        cols = ahead
    return jnp.concatenate(done, axis=0)[:, :MODES]


def basis_kernel(scale, mine_ref, other_ref, start_ref, inner_ref, edge_ref, before_ref, basis_ref, modes_ref, rows_ref, out_ref):
    first = is_even("row")
    mine, other = mine_ref[...], other_ref[...]
    cross = jnp.where(first, mine, other)[:HALF]
    second = jnp.where(first, other, mine)
    folded = second[:HALF]
    i = lax.broadcasted_iota(jnp.int32, (HALF, HALF), 0)
    j = lax.broadcasted_iota(jnp.int32, (HALF, HALF), 1)
    flipped = folded.T
    top = jnp.where(i <= j, folded, flipped)
    low = jnp.where(i > j, folded, jnp.where(i < j, flipped, second[HALF : HALF + 1]))
    gram = jnp.concatenate(
        [jnp.concatenate([top, cross], axis=1), jnp.concatenate([cross.T, low], axis=1)], axis=0
    )
    gram = gram * scale
    basis = start_ref[...]
    for sweep in range(SWEEPS):
        stacked = jnp.dot(basis, gram, precision=HIGHEST, preferred_element_type=F32)
        inner = lax.dot_general(
            stacked, stacked, (((1,), (1,)), ((), ())), precision=HIGHEST, preferred_element_type=F32
        )
        basis = jnp.dot(inverse_factor(inner), stacked, precision=HIGHEST, preferred_element_type=F32)
    basis_ref[...] = jnp.dot(basis, frame_order(1), precision=HIGHEST, preferred_element_type=F32)
    twice = jnp.concatenate([basis, basis], axis=0)
    before = jnp.concatenate([before_ref[:8], before_ref[8:]], axis=1)
    before = jnp.concatenate([before, pltpu.roll(before, 4, 0)], axis=0)
    before = jnp.where(lax.axis_index("col") == 0, inner_ref[0].astype(F32), before)
    cell = jnp.where(second_cells(), before, edge_ref[...].astype(F32)).astype(BF16)
    flat = jnp.concatenate([inner_ref[1:].reshape(16 * BLOCKS - 16, FRAMES), cell], axis=0)
    rows_ref[...] = lax.dot_general(
        flat, twice.astype(BF16), (((1,), (1,)), ((), ())), preferred_element_type=F32
    )
    left = lax.broadcasted_iota(jnp.int32, (BLOCKS, 2 * MODES), 1) < MODES
    for row in range(2):
        for half in range(2):
            for cell in range(2):
                at = 8 * row + 4 * cell + 2 * half
                field = jnp.where(
                    left, rows_ref[pl.ds(at, BLOCKS, stride=16), :], rows_ref[pl.ds(at + 1, BLOCKS, stride=16), :]
                )
                if cell:
                    field = pltpu.roll(field, 1, 0)
                out_ref[pl.ds(64 * row + 32 * half + 1 - cell, BLOCKS, stride=2), :] = field
            modes_ref[row, :, 128 * half : 128 * half + 128] = out_ref[64 * row + 32 * half : 64 * row + 32 * half + 32]


def call(kernel, outs, n_in, scratch=()):
    return pl.pallas_call(
        kernel,
        out_shape=[jax.ShapeDtypeStruct(shape, dtype) for shape, dtype in outs],
        in_specs=[VMEM] * n_in,
        out_specs=[VMEM] * len(outs),
        scratch_shapes=list(scratch),
        compiler_params=PARAMS,
    )


def pairs(size, start):
    swaps = []
    for i in range(start, size - 1, 2):
        swaps += [(i, i + 1), (i + 1, i)]
    return swaps


def on_device(video, filters, start_basis):
    size_row, size_col = lax.axis_size("row"), lax.axis_size("col")
    near, far = pairs(size_row, 0), pairs(size_row, 1)
    to_left = [(i + 1, i) for i in range(size_col - 1)]

    across = [(a * size_col + i, b * size_col + j) for a, b in far for i, j in to_left]
    send = ((REACH * COLS + 16, FRAMES), BF16)
    tile = ((BLOCKS, 112, 3 * HALF), BF16)
    tiles = ((BLOCKS + 1, 112, 3 * HALF), BF16)
    rim = ((2, COLS, 3 * HALF), F32)
    rows = (((FRAMES + 1) * ROWS, COLS), F32)
    rows, send_a, send_b = call(send_kernel, [rows, send, send], 1)(video)
    got_a = lax.ppermute(send_a, "row", near)
    got_b = lax.ppermute(send_b, "row", far)
    outs = [tile, rim, ((96, 3 * HALF), BF16), ((32, 3 * HALF), BF16)]
    x, rim, side, diag = call(own_kernel, outs, 2)(rows, got_a)
    side = lax.ppermute(side, "col", to_left)
    diag = lax.ppermute(diag, ("row", "col"), across)

    (band,) = call(band_kernel, [((128, 256), BF16)], 1, [pltpu.VMEM((16, 128), F32)])(
        jnp.transpose(filters, (0, 2, 1, 3))
    )
    inner, x = call(inner_kernel, [((BLOCKS, 16, FRAMES), BF16), tiles], 5)(got_a, got_b, x, rim, band)
    part, passed = ((SUMMED, HALF), F32), ((16, HALF), F32)
    edge, mine, other, passed = call(edge_kernel, [((16, FRAMES), BF16), part, part, passed], 5)(
        band, x, side, diag, inner
    )

    mine = mine + lax.ppermute(other, "row", near)
    step = 2
    while step < size_row:
        mine = mine + lax.ppermute(mine, "row", [(i, i ^ step) for i in range(size_row)])
        step *= 2
    mine = jnp.concatenate([mine, passed], axis=0)
    summed = lax.broadcasted_iota(jnp.int32, mine.shape, 0) < SUMMED
    step = 1
    col = lax.axis_index("col")
    before = jnp.zeros((16, HALF), F32)
    start = start_basis.T
    while step < size_col:
        if 2 * step >= size_col:
            mine, start = lax.optimization_barrier((mine, start))
            (start,) = call(start_kernel, [((MODES, FRAMES), F32)], 1)(start)
        got = lax.ppermute(mine, "col", [(i, i ^ step) for i in range(size_col)])
        mine = jnp.where(summed, mine + got, got)
        before = jnp.where((col & (2 * step - 1)) == step, got[SUMMED:], before)
        step *= 2
    mine = mine[:SUMMED]
    other = lax.ppermute(mine, "row", near)

    features = ORIENT * (size_row * ROWS // 4) * (size_col * COLS // 4)
    kernel = functools.partial(basis_kernel, 1.0 / features)
    basis, modes = call(
        kernel,
        [((MODES, FRAMES), F32), ((ROWS // 4, COLS // 4, ORIENT * MODES), F32)],
        6,
        [pltpu.VMEM((FRAMES, 2 * MODES), F32), pltpu.VMEM((128, 128), F32)],
    )(mine, other, start, inner, edge, before)
    return basis.T, modes


def solution(mesh):
    return jax.shard_map(
        on_device,
        mesh=mesh,
        in_specs=(P("grp", "row", "col"), P(), P()),
        out_specs=(P("grp", None), P(("grp", "row"), "col", None)),
        check_vma=False,
    )
```

```python
import functools

import jax
import jax.numpy as jnp
from jax import lax
from jax.experimental import pallas as pl
from jax.experimental.pallas import tpu as pltpu
from jax.sharding import PartitionSpec as P

FRAMES = 256
HALF = FRAMES // 2
MODES = 64
ORIENT = 4
TAPS = 7
REACH = 3
SWEEPS = 2
ROWS = 8
COLS = 128
SUMMED = HALF + 8
BLOCKS = 16
UNROLL = 4
AHEAD = 3
F32 = jnp.float32
BF16 = jnp.bfloat16
HIGHEST = lax.Precision.HIGHEST
PARAMS = pltpu.CompilerParams(vmem_limit_bytes=24 * 1024 * 1024)
VMEM = pl.BlockSpec(memory_space=pltpu.VMEM)


def turned(rows_ref, row, group):
    return rows_ref[pl.ds(group * ROWS + row, HALF, stride=2 * ROWS), :].T


def blocked(upper, lower):
    both = [part.reshape(BLOCKS, 8, HALF) for part in (upper, lower)]
    return jnp.concatenate(both, axis=1).astype(BF16)


def is_even(axis):
    return (lax.axis_index(axis) & 1) == 0


def send_kernel(video_ref, rows_ref, send_a_ref, send_b_ref, heads_ref):
    even = is_even("row")
    rows_ref[...] = video_ref[...].astype(F32).reshape(rows_ref.shape)
    for group in range(2):
        lanes = slice(HALF * group, HALF * group + HALF)
        tiles = [turned(rows_ref, row, group) for row in range(ROWS)]
        heads_ref[:, lanes] = jnp.concatenate([tile[:8] for tile in tiles], axis=0)
        for i in range(REACH):
            first, last = tiles[i], tiles[ROWS - REACH + i]
            at = slice(COLS * i, COLS * i + COLS)
            send_a_ref[at, lanes] = jnp.where(even, last, first).astype(BF16)
            send_b_ref[at, lanes] = jnp.where(even, first, last).astype(BF16)
    fill = jnp.zeros((8, COLS), F32)
    final = rows_ref[FRAMES * ROWS : FRAMES * ROWS + ROWS, :]
    shifted = pltpu.roll(final, REACH, 0)
    first, last = (jnp.concatenate([part, fill], axis=0).astype(BF16) for part in (final, shifted))
    for ref, chosen in ((send_a_ref, jnp.where(even, last, first)), (send_b_ref, jnp.where(even, first, last))):
        ref[REACH * COLS : REACH * COLS + 16, 0:COLS] = chosen
        ref[REACH * COLS : REACH * COLS + 16, COLS : 2 * COLS] = chosen


def side_kernel(rows_ref, heads_ref, a_ref, side_ref, diag_ref):
    even = is_even("row")
    fill = jnp.zeros((8, HALF), F32)
    ends = rows_ref[FRAMES * ROWS : FRAMES * ROWS + ROWS, :]
    heads = in_groups([heads_ref[8 * i : 8 * i + 8] for i in range(ROWS)], ends)
    near = expanded(a_ref[...].astype(F32), 8)
    for group in range(3):
        lanes = slice(HALF * group, HALF * group + HALF)
        sent = [row[group] for row in heads + near] + [fill]
        side_ref[:, lanes] = jnp.concatenate(sent, axis=0).astype(BF16)
        chosen = [jnp.where(even, heads[i][group], heads[ROWS - REACH + i][group]) for i in range(REACH)]
        diag_ref[:, lanes] = jnp.concatenate(chosen + [fill], axis=0).astype(BF16)


def in_groups(tiles, ends):
    count = tiles[0].shape[0]
    final = lax.broadcasted_iota(jnp.int32, (count, HALF), 1) == HALF - 1
    ends = ends.T
    rows = []
    for i, tile in enumerate(tiles):
        late = jnp.where(final, ends[:count, i : i + 1], pltpu.roll(tile[:, :HALF], HALF - 1, 1))
        rows.append([tile[:, :HALF], tile[:, HALF:], late])
    return rows


def expanded(got, count):
    tiles = [got[COLS * i : COLS * i + count] for i in range(REACH)]
    return in_groups(tiles, got[REACH * COLS : REACH * COLS + 8, :COLS])


def band_kernel(filters_ref, band_ref, taps_ref):
    taps_ref[...] = jnp.zeros((16, 128), F32)
    for orient in range(ORIENT):
        for part in range(2):
            for i in range(TAPS):
                line = filters_ref[orient, i, part : part + 1, :]
                for cell in range(2):
                    row, lane = 8 * part + 4 * cell + orient, 64 * cell + 8 * i
                    taps_ref[row : row + 1, lane : lane + TAPS] = line
    taps = taps_ref[...]
    high = taps.astype(BF16)
    low = (taps - high.astype(F32)).astype(BF16)
    parts = jnp.concatenate([high, low], axis=0)
    tap = lax.broadcasted_iota(jnp.int32, (128, 128), 0)
    lane = lax.broadcasted_iota(jnp.int32, (128, 128), 1)
    column = ((lane >> 6) << 3) | (lane & 7)
    row_hit = ((lane >> 3) & 7) == ((tap >> 3) & 7)
    ahead = column - (tap & 7) - 1 - 4 * (tap >> 6)
    for j in range(4):
        select = jnp.where(row_hit & (ahead == j), 1.0, 0.0).astype(BF16)
        base = jnp.dot(parts, select, preferred_element_type=F32)
        for i in range(2):
            start = (4 * i + j) * 16
            rolled = (pltpu.roll(base, 8, 1) if i else base).astype(BF16)
            band_ref[start : start + 16, 0:128] = rolled[:16]
            band_ref[start : start + 16, 128:256] = rolled[16:]


def dot(a, b):
    return jnp.dot(a, b, precision=HIGHEST, preferred_element_type=F32)


def start_kernel(start_ref, basis_ref):
    basis_ref[...] = dot(start_ref[...], frame_order(0))


def frame_order(axis):
    frame = lax.broadcasted_iota(jnp.int32, (FRAMES, FRAMES), axis)
    lane = lax.broadcasted_iota(jnp.int32, (FRAMES, FRAMES), 1 - axis)
    return jnp.where(frame == 2 * (lane & (HALF - 1)) + (lane >> 7), 1.0, 0.0).astype(F32)


def place_rows(a_ref, b_ref, rows_ref, x_ref):
    even = is_even("row")
    got_a, got_b = a_ref[...], b_ref[...]
    above = expanded(jnp.where(even, got_b, got_a).astype(F32), COLS)
    below = expanded(jnp.where(even, got_a, got_b).astype(F32), COLS)
    x_ref[0] = jnp.zeros((112, 3 * HALF), BF16)
    for group in range(3):
        own = [turned(rows_ref, row, group) for row in range(ROWS)]
        tiles = [row[group] for row in above] + own + [row[group] for row in below]
        for pair in range(len(tiles) // 2):
            at = slice(16 * pair, 16 * pair + 16)
            x_ref[1:, at, HALF * group : HALF * group + HALF] = blocked(tiles[2 * pair], tiles[2 * pair + 1])


def block_feats(band_ref, left, right):
    pooled = []
    for cell in range(2):
        windows = []
        for half in range(2):
            at = 16 * (2 * cell + half)
            windows.append(jnp.concatenate([left[at : at + 64], right[at : at + 64]], axis=0))
        window = jnp.concatenate(
            [windows[0][:, :FRAMES], windows[1][:, :FRAMES], windows[0][:, FRAMES:], windows[1][:, FRAMES:]], axis=1
        )
        window = jnp.concatenate([window, window], axis=0)
        resp = jnp.dot(band_ref[...], window, preferred_element_type=F32)
        total = [None, None]
        for half in range(2):
            starts = (FRAMES * half, FRAMES * half + HALF, 2 * FRAMES + HALF * half)
            for pixel in range(8):
                at = 16 * pixel
                real = [resp[at : at + 8, s : s + HALF] for s in starts]
                imag = [resp[at + 8 : at + 16, s : s + HALF] for s in starts]
                for g in range(2):
                    prod_real = real[g + 1] * real[g] + imag[g + 1] * imag[g]
                    prod_imag = imag[g + 1] * real[g] - real[g + 1] * imag[g]
                    motion = prod_imag * lax.rsqrt(prod_real * prod_real + prod_imag * prod_imag + 1.0)
                    total[g] = motion if total[g] is None else total[g] + motion
        pooled.append(jnp.concatenate(total, axis=1) * (1.0 / 16.0))
    return jnp.concatenate(pooled, axis=0)


def second_cells():
    return (lax.broadcasted_iota(jnp.int32, (16, FRAMES), 0) & 4) == 4


def inner_kernel(a_ref, b_ref, rows_ref, band_ref, feats_ref, x_ref):
    place_rows(a_ref, b_ref, rows_ref, x_ref)

    def body(step, carry):
        for i in range(UNROLL):
            block = UNROLL * step + i
            feats_ref[block] = block_feats(band_ref, x_ref[block], x_ref[block + 1]).astype(BF16)
        return carry

    lax.fori_loop(0, BLOCKS // UNROLL, body, 0)
    begins = lax.axis_index("col") == 0
    feats_ref[0] = jnp.where(second_cells() & begins, feats_ref[0].astype(F32), 0.0).astype(BF16)


def edge_kernel(band_ref, x_ref, side_ref, diag_ref, inner_ref, edge_ref, mine_ref, other_ref, passed_ref):
    even = is_even("row")
    side = side_ref[...].astype(F32)
    near, far = side[8 * ROWS : 8 * ROWS + 8 * REACH], diag_ref[...].astype(F32)[: 8 * REACH]
    rows = [jnp.where(even, far, near), side[: 8 * ROWS], jnp.where(even, near, far)]
    edge = block_feats(band_ref, x_ref[BLOCKS], jnp.concatenate(rows, axis=0).astype(BF16))
    ends = lax.axis_index("col") == lax.axis_size("col") - 1
    edge = jnp.where(second_cells() & ends, 0.0, edge).astype(BF16)
    edge_ref[...] = edge
    flat = jnp.concatenate([inner_ref[...].reshape(16 * BLOCKS, FRAMES), edge], axis=0)
    gram = lax.dot_general(flat, flat, (((0,), (0,)), ((), ())), preferred_element_type=F32)
    top, cross, low = gram[:HALF, :HALF], gram[:HALF, HALF:], gram[HALF:, HALF:]
    i = lax.broadcasted_iota(jnp.int32, (HALF, HALF), 0)
    j = lax.broadcasted_iota(jnp.int32, (HALF, HALF), 1)
    folded = jnp.where(i <= j, top, low)
    diagonal = jnp.sum(jnp.where(i == j, low, 0.0), axis=0, keepdims=True)
    first = is_even("row")
    spare = jnp.broadcast_to(diagonal, (8, HALF))
    mine_ref[0:HALF] = jnp.where(first, cross, folded)
    mine_ref[HALF:SUMMED] = spare
    other_ref[0:HALF] = jnp.where(first, folded, cross)
    other_ref[HALF:SUMMED] = spare
    edge = edge.astype(F32)
    passed = jnp.where(second_cells()[:8], edge[:8], pltpu.roll(edge[8:], 4, 0))
    passed_ref[0:8] = passed[:, :HALF]
    passed_ref[8:16] = passed[:, HALF:]


def inverse_factor(inner):
    count = MODES // 8
    shape = (8, 2 * MODES)
    i = lax.broadcasted_iota(jnp.int32, (MODES, MODES), 0)
    j = lax.broadcasted_iota(jnp.int32, (MODES, MODES), 1)
    work = jnp.concatenate([jnp.where(i == j, 1.0, 0.0), inner], axis=1)
    work = [work[8 * v : 8 * v + 8] for v in range(count)]
    sub = lax.broadcasted_iota(jnp.int32, shape, 0)

    def columns(b, first, last):
        lanes = [MODES + 8 * b + m for m in range(8)]
        return {v: [jnp.broadcast_to(work[v][:, k : k + 1], shape) for k in lanes] for v in range(first, last)}

    def spread(tile, row):
        return jnp.broadcast_to(tile[row : row + 1], shape)

    cols = columns(0, 0, count)
    done = []
    for b in range(count):
        near = min(count, b + 1 + AHEAD)
        ahead = columns(b + 1, b + 1, near)
        scale = jnp.ones(shape, F32)
        for m in range(8):
            lead = cols[b][m]
            pivot = spread(lead, m)
            inverse = 1.0 / pivot
            scale = jnp.where(sub == m, pivot, scale)
            row = spread(work[b], m) * inverse
            for q in range(m + 1, 8):
                times = spread(lead, q) * inverse
                for v in cols:
                    cols[v][q] = cols[v][q] - cols[v][m] * times
            for q in range(8 if ahead else 0):
                times = spread(cols[b + 1][m], q) * inverse
                for v in ahead:
                    ahead[v][q] = ahead[v][q] - cols[v][m] * times
            work[b] = work[b] - jnp.where(sub > m, lead, 0.0) * row
            for v in range(b + 1, count):
                work[v] = work[v] - cols[v][m] * row
        done.append(work[b] * lax.rsqrt(scale))
        cols = {**ahead, **columns(b + 1, near, count)}
    return jnp.concatenate(done, axis=0)[:, :MODES]


def basis_kernel(scale, mine_ref, other_ref, start_ref, inner_ref, edge_ref, before_ref, basis_ref, modes_ref, rows_ref, out_ref):
    first = is_even("row")
    mine, other = mine_ref[...], other_ref[...]
    cross = jnp.where(first, mine, other)[:HALF]
    second = jnp.where(first, other, mine)
    folded = second[:HALF]
    i = lax.broadcasted_iota(jnp.int32, (HALF, HALF), 0)
    j = lax.broadcasted_iota(jnp.int32, (HALF, HALF), 1)
    flipped = folded.T
    top = jnp.where(i <= j, folded, flipped)
    low = jnp.where(i > j, folded, jnp.where(i < j, flipped, second[HALF : HALF + 1]))
    gram = jnp.concatenate(
        [jnp.concatenate([top, cross], axis=1), jnp.concatenate([cross.T, low], axis=1)], axis=0
    )
    gram = gram * scale
    stacked = dot(start_ref[...], gram)
    for sweep in range(SWEEPS):
        inner = lax.dot_general(
            stacked, stacked, (((1,), (1,)), ((), ())), precision=HIGHEST, preferred_element_type=F32
        )
        if sweep < SWEEPS - 1:
            beside = dot(stacked, gram)
        else:
            beside = jnp.concatenate([stacked, dot(stacked, frame_order(1))], axis=1)
        stacked = dot(inverse_factor(inner), beside)
    basis = stacked[:, :FRAMES]
    basis_ref[...] = stacked[:, FRAMES:]
    twice = jnp.concatenate([basis, basis], axis=0)
    before = jnp.concatenate([before_ref[:8], before_ref[8:]], axis=1)
    before = jnp.concatenate([before, pltpu.roll(before, 4, 0)], axis=0)
    before = jnp.where(lax.axis_index("col") == 0, inner_ref[0].astype(F32), before)
    cell = jnp.where(second_cells(), before, edge_ref[...].astype(F32)).astype(BF16)
    flat = jnp.concatenate([inner_ref[1:].reshape(16 * BLOCKS - 16, FRAMES), cell], axis=0)
    rows_ref[...] = lax.dot_general(
        flat, twice.astype(BF16), (((1,), (1,)), ((), ())), preferred_element_type=F32
    )
    left = lax.broadcasted_iota(jnp.int32, (BLOCKS, 2 * MODES), 1) < MODES
    for row in range(2):
        for half in range(2):
            for cell in range(2):
                at = 8 * row + 4 * cell + 2 * half
                field = jnp.where(
                    left, rows_ref[pl.ds(at, BLOCKS, stride=16), :], rows_ref[pl.ds(at + 1, BLOCKS, stride=16), :]
                )
                if cell:
                    field = pltpu.roll(field, 1, 0)
                out_ref[pl.ds(64 * row + 32 * half + 1 - cell, BLOCKS, stride=2), :] = field
            modes_ref[row, :, 128 * half : 128 * half + 128] = out_ref[64 * row + 32 * half : 64 * row + 32 * half + 32]


def call(kernel, outs, n_in, scratch=()):
    return pl.pallas_call(
        kernel,
        out_shape=[jax.ShapeDtypeStruct(shape, dtype) for shape, dtype in outs],
        in_specs=[VMEM] * n_in,
        out_specs=[VMEM] * len(outs),
        scratch_shapes=list(scratch),
        compiler_params=PARAMS,
    )


def pairs(size, start):
    swaps = []
    for i in range(start, size - 1, 2):
        swaps += [(i, i + 1), (i + 1, i)]
    return swaps


def on_device(video, filters, start_basis):
    size_row, size_col = lax.axis_size("row"), lax.axis_size("col")
    near, far = pairs(size_row, 0), pairs(size_row, 1)
    to_left = [(i + 1, i) for i in range(size_col - 1)]

    across = [(a * size_col + i, b * size_col + j) for a, b in far for i, j in to_left]
    send = ((REACH * COLS + 16, FRAMES), BF16)
    tiles = ((BLOCKS + 1, 112, 3 * HALF), BF16)
    rows = (((FRAMES + 1) * ROWS, COLS), F32)
    rows, send_a, send_b, heads = call(send_kernel, [rows, send, send, ((8 * ROWS, FRAMES), F32)], 1)(video)
    got_a = lax.ppermute(send_a, "row", near)
    got_b = lax.ppermute(send_b, "row", far)
    outs = [((96, 3 * HALF), BF16), ((32, 3 * HALF), BF16)]
    side, diag = call(side_kernel, outs, 3)(rows, heads, got_a)
    side = lax.ppermute(side, "col", to_left)
    diag = lax.ppermute(diag, ("row", "col"), across)

    (band,) = call(band_kernel, [((128, 256), BF16)], 1, [pltpu.VMEM((16, 128), F32)])(
        jnp.transpose(filters, (0, 2, 1, 3))
    )
    inner, x = call(inner_kernel, [((BLOCKS, 16, FRAMES), BF16), tiles], 4)(got_a, got_b, rows, band)
    part, passed = ((SUMMED, HALF), F32), ((16, HALF), F32)
    edge, mine, other, passed = call(edge_kernel, [((16, FRAMES), BF16), part, part, passed], 5)(
        band, x, side, diag, inner
    )

    mine = mine + lax.ppermute(other, "row", near)
    step = 2
    while step < size_row:
        mine = mine + lax.ppermute(mine, "row", [(i, i ^ step) for i in range(size_row)])
        step *= 2
    mine = jnp.concatenate([mine, passed], axis=0)
    summed = lax.broadcasted_iota(jnp.int32, mine.shape, 0) < SUMMED
    step = 1
    col = lax.axis_index("col")
    before = jnp.zeros((16, HALF), F32)
    start = start_basis.T
    while step < size_col:
        if 2 * step >= size_col:
            mine, start = lax.optimization_barrier((mine, start))
            (start,) = call(start_kernel, [((MODES, FRAMES), F32)], 1)(start)
        got = lax.ppermute(mine, "col", [(i, i ^ step) for i in range(size_col)])
        mine = jnp.where(summed, mine + got, got)
        before = jnp.where((col & (2 * step - 1)) == step, got[SUMMED:], before)
        step *= 2
    mine = mine[:SUMMED]
    other = lax.ppermute(mine, "row", near)

    features = ORIENT * (size_row * ROWS // 4) * (size_col * COLS // 4)
    kernel = functools.partial(basis_kernel, 1.0 / features)
    basis, modes = call(
        kernel,
        [((MODES, FRAMES), F32), ((ROWS // 4, COLS // 4, ORIENT * MODES), F32)],
        6,
        [pltpu.VMEM((FRAMES, 2 * MODES), F32), pltpu.VMEM((128, 128), F32)],
    )(mine, other, start, inner, edge, before)
    return basis.T, modes


def solution(mesh):
    return jax.shard_map(
        on_device,
        mesh=mesh,
        in_specs=(P("grp", "row", "col"), P(), P()),
        out_specs=(P("grp", None), P(("grp", "row"), "col", None)),
        check_vma=False,
    )
```

```python
import functools

import jax
import jax.numpy as jnp
from jax import lax
from jax.experimental import pallas as pl
from jax.experimental.pallas import tpu as pltpu
from jax.sharding import PartitionSpec as P

FRAMES = 256
HALF = FRAMES // 2
MODES = 64
ORIENT = 4
TAPS = 7
REACH = 3
SWEEPS = 2
ROWS = 8
COLS = 128
SUMMED = HALF + 8
BLOCKS = 16
UNROLL = 8
AHEAD = 3
F32 = jnp.float32
BF16 = jnp.bfloat16
HIGHEST = lax.Precision.HIGHEST
PARAMS = pltpu.CompilerParams(vmem_limit_bytes=24 * 1024 * 1024)
VMEM = pl.BlockSpec(memory_space=pltpu.VMEM)


def turned(rows_ref, row, group):
    return rows_ref[pl.ds(group * ROWS + row, HALF, stride=2 * ROWS), :].T


def blocked(upper, lower):
    both = [part.reshape(BLOCKS, 8, HALF) for part in (upper, lower)]
    return jnp.concatenate(both, axis=1).astype(BF16)


def is_even(axis):
    return (lax.axis_index(axis) & 1) == 0


def send_kernel(video_ref, rows_ref, send_a_ref, send_b_ref, heads_ref):
    even = is_even("row")
    rows_ref[...] = video_ref[...].astype(F32).reshape(rows_ref.shape)
    for group in range(2):
        lanes = slice(HALF * group, HALF * group + HALF)
        tiles = [turned(rows_ref, row, group) for row in range(ROWS)]
        heads_ref[:, lanes] = jnp.concatenate([tile[:8] for tile in tiles], axis=0)
        for i in range(REACH):
            first, last = tiles[i], tiles[ROWS - REACH + i]
            at = slice(COLS * i, COLS * i + COLS)
            send_a_ref[at, lanes] = jnp.where(even, last, first).astype(BF16)
            send_b_ref[at, lanes] = jnp.where(even, first, last).astype(BF16)
    fill = jnp.zeros((8, COLS), F32)
    final = rows_ref[FRAMES * ROWS : FRAMES * ROWS + ROWS, :]
    shifted = pltpu.roll(final, REACH, 0)
    first, last = (jnp.concatenate([part, fill], axis=0).astype(BF16) for part in (final, shifted))
    for ref, chosen in ((send_a_ref, jnp.where(even, last, first)), (send_b_ref, jnp.where(even, first, last))):
        ref[REACH * COLS : REACH * COLS + 16, 0:COLS] = chosen
        ref[REACH * COLS : REACH * COLS + 16, COLS : 2 * COLS] = chosen


def side_kernel(rows_ref, heads_ref, a_ref, side_ref, diag_ref):
    even = is_even("row")
    fill = jnp.zeros((8, HALF), F32)
    ends = rows_ref[FRAMES * ROWS : FRAMES * ROWS + ROWS, :]
    heads = in_groups([heads_ref[8 * i : 8 * i + 8] for i in range(ROWS)], ends)
    near = expanded(a_ref[...].astype(F32), 8)
    for group in range(3):
        lanes = slice(HALF * group, HALF * group + HALF)
        sent = [row[group] for row in heads + near] + [fill]
        side_ref[:, lanes] = jnp.concatenate(sent, axis=0).astype(BF16)
        chosen = [jnp.where(even, heads[i][group], heads[ROWS - REACH + i][group]) for i in range(REACH)]
        diag_ref[:, lanes] = jnp.concatenate(chosen + [fill], axis=0).astype(BF16)


def in_groups(tiles, ends):
    count = tiles[0].shape[0]
    final = lax.broadcasted_iota(jnp.int32, (count, HALF), 1) == HALF - 1
    ends = ends.T
    rows = []
    for i, tile in enumerate(tiles):
        late = jnp.where(final, ends[:count, i : i + 1], pltpu.roll(tile[:, :HALF], HALF - 1, 1))
        rows.append([tile[:, :HALF], tile[:, HALF:], late])
    return rows


def expanded(got, count):
    tiles = [got[COLS * i : COLS * i + count] for i in range(REACH)]
    return in_groups(tiles, got[REACH * COLS : REACH * COLS + 8, :COLS])


def make_band(filters_ref, band_ref, taps_ref):
    taps_ref[...] = jnp.zeros((16, 128), F32)
    for orient in range(ORIENT):
        for part in range(2):
            for i in range(TAPS):
                line = filters_ref[orient, i, part : part + 1, :]
                for cell in range(2):
                    row, lane = 8 * part + 4 * cell + orient, 64 * cell + 8 * i
                    taps_ref[row : row + 1, lane : lane + TAPS] = line
    taps = taps_ref[...]
    high = taps.astype(BF16)
    low = (taps - high.astype(F32)).astype(BF16)
    parts = jnp.concatenate([high, low], axis=0)
    tap = lax.broadcasted_iota(jnp.int32, (128, 128), 0)
    lane = lax.broadcasted_iota(jnp.int32, (128, 128), 1)
    column = ((lane >> 6) << 3) | (lane & 7)
    row_hit = ((lane >> 3) & 7) == ((tap >> 3) & 7)
    ahead = column - (tap & 7) - 1 - 4 * (tap >> 6)
    for j in range(4):
        select = jnp.where(row_hit & (ahead == j), 1.0, 0.0).astype(BF16)
        base = jnp.dot(parts, select, preferred_element_type=F32)
        for i in range(2):
            start = (4 * i + j) * 16
            rolled = (pltpu.roll(base, 8, 1) if i else base).astype(BF16)
            band_ref[start : start + 16, 0:128] = rolled[:16]
            band_ref[start : start + 16, 128:256] = rolled[16:]


def dot(a, b):
    return jnp.dot(a, b, precision=HIGHEST, preferred_element_type=F32)


def start_kernel(start_ref, basis_ref):
    basis_ref[...] = dot(start_ref[...], frame_order(0))


def frame_order(axis):
    frame = lax.broadcasted_iota(jnp.int32, (FRAMES, FRAMES), axis)
    lane = lax.broadcasted_iota(jnp.int32, (FRAMES, FRAMES), 1 - axis)
    return jnp.where(frame == 2 * (lane & (HALF - 1)) + (lane >> 7), 1.0, 0.0).astype(F32)


def place_rows(a_ref, b_ref, rows_ref, x_ref):
    even = is_even("row")
    got_a, got_b = a_ref[...], b_ref[...]
    above = expanded(jnp.where(even, got_b, got_a).astype(F32), COLS)
    below = expanded(jnp.where(even, got_a, got_b).astype(F32), COLS)
    x_ref[0] = jnp.zeros((112, 3 * HALF), BF16)
    for group in range(3):
        own = [turned(rows_ref, row, group) for row in range(ROWS)]
        tiles = [row[group] for row in above] + own + [row[group] for row in below]
        for pair in range(len(tiles) // 2):
            at = slice(16 * pair, 16 * pair + 16)
            x_ref[1:, at, HALF * group : HALF * group + HALF] = blocked(tiles[2 * pair], tiles[2 * pair + 1])


def block_feats(band_ref, left, right):
    pooled = []
    for cell in range(2):
        windows = []
        for half in range(2):
            at = 16 * (2 * cell + half)
            windows.append(jnp.concatenate([left[at : at + 64], right[at : at + 64]], axis=0))
        window = jnp.concatenate(
            [windows[0][:, :FRAMES], windows[1][:, :FRAMES], windows[0][:, FRAMES:], windows[1][:, FRAMES:]], axis=1
        )
        window = jnp.concatenate([window, window], axis=0)
        resp = jnp.dot(band_ref[...], window, preferred_element_type=F32)
        total = [None, None]
        for half in range(2):
            starts = (FRAMES * half, FRAMES * half + HALF, 2 * FRAMES + HALF * half)
            for pixel in range(8):
                at = 16 * pixel
                real = [resp[at : at + 8, s : s + HALF] for s in starts]
                imag = [resp[at + 8 : at + 16, s : s + HALF] for s in starts]
                for g in range(2):
                    prod_real = real[g + 1] * real[g] + imag[g + 1] * imag[g]
                    prod_imag = imag[g + 1] * real[g] - real[g + 1] * imag[g]
                    motion = prod_imag * lax.rsqrt(prod_real * prod_real + prod_imag * prod_imag + 1.0)
                    total[g] = motion if total[g] is None else total[g] + motion
        pooled.append(jnp.concatenate(total, axis=1) * (1.0 / 16.0))
    return jnp.concatenate(pooled, axis=0)


def second_cells():
    return (lax.broadcasted_iota(jnp.int32, (16, FRAMES), 0) & 4) == 4


def inner_kernel(a_ref, b_ref, rows_ref, filters_ref, feats_ref, x_ref, band_ref, taps_ref):
    make_band(filters_ref, band_ref, taps_ref)
    place_rows(a_ref, b_ref, rows_ref, x_ref)

    def body(step, carry):
        for i in range(UNROLL):
            block = UNROLL * step + i
            feats_ref[block] = block_feats(band_ref, x_ref[block], x_ref[block + 1]).astype(BF16)
        return carry

    lax.fori_loop(0, BLOCKS // UNROLL, body, 0)
    begins = lax.axis_index("col") == 0
    feats_ref[0] = jnp.where(second_cells() & begins, feats_ref[0].astype(F32), 0.0).astype(BF16)


def edge_kernel(band_ref, x_ref, side_ref, diag_ref, inner_ref, edge_ref, mine_ref, other_ref, passed_ref):
    even = is_even("row")
    side = side_ref[...].astype(F32)
    near, far = side[8 * ROWS : 8 * ROWS + 8 * REACH], diag_ref[...].astype(F32)[: 8 * REACH]
    rows = [jnp.where(even, far, near), side[: 8 * ROWS], jnp.where(even, near, far)]
    edge = block_feats(band_ref, x_ref[BLOCKS], jnp.concatenate(rows, axis=0).astype(BF16))
    ends = lax.axis_index("col") == lax.axis_size("col") - 1
    edge = jnp.where(second_cells() & ends, 0.0, edge).astype(BF16)
    edge_ref[...] = edge
    flat = jnp.concatenate([inner_ref[...].reshape(16 * BLOCKS, FRAMES), edge], axis=0)
    gram = lax.dot_general(flat, flat, (((0,), (0,)), ((), ())), preferred_element_type=F32)
    top, cross, low = gram[:HALF, :HALF], gram[:HALF, HALF:], gram[HALF:, HALF:]
    i = lax.broadcasted_iota(jnp.int32, (HALF, HALF), 0)
    j = lax.broadcasted_iota(jnp.int32, (HALF, HALF), 1)
    folded = jnp.where(i <= j, top, low)
    diagonal = jnp.sum(jnp.where(i == j, low, 0.0), axis=0, keepdims=True)
    first = is_even("row")
    spare = jnp.broadcast_to(diagonal, (8, HALF))
    mine_ref[0:HALF] = jnp.where(first, cross, folded)
    mine_ref[HALF:SUMMED] = spare
    other_ref[0:HALF] = jnp.where(first, folded, cross)
    other_ref[HALF:SUMMED] = spare
    edge = edge.astype(F32)
    passed = jnp.where(second_cells()[:8], edge[:8], pltpu.roll(edge[8:], 4, 0))
    passed_ref[0:8] = passed[:, :HALF]
    passed_ref[8:16] = passed[:, HALF:]


def inverse_factor(inner):
    count = MODES // 8
    shape = (8, 2 * MODES)
    i = lax.broadcasted_iota(jnp.int32, (MODES, MODES), 0)
    j = lax.broadcasted_iota(jnp.int32, (MODES, MODES), 1)
    work = jnp.concatenate([jnp.where(i == j, 1.0, 0.0), inner], axis=1)
    work = [work[8 * v : 8 * v + 8] for v in range(count)]
    sub = lax.broadcasted_iota(jnp.int32, shape, 0)

    def columns(b, first, last):
        lanes = [MODES + 8 * b + m for m in range(8)]
        return {v: [jnp.broadcast_to(work[v][:, k : k + 1], shape) for k in lanes] for v in range(first, last)}

    def spread(tile, row):
        return jnp.broadcast_to(tile[row : row + 1], shape)

    cols = columns(0, 0, count)
    done = []
    for b in range(count):
        near = min(count, b + 1 + AHEAD)
        ahead = columns(b + 1, b + 1, near)
        scale = jnp.ones(shape, F32)
        for m in range(8):
            lead = cols[b][m]
            pivot = spread(lead, m)
            inverse = 1.0 / pivot
            scale = jnp.where(sub == m, pivot, scale)
            row = spread(work[b], m) * inverse
            for q in range(m + 1, 8):
                times = spread(lead, q) * inverse
                for v in cols:
                    cols[v][q] = cols[v][q] - cols[v][m] * times
            for q in range(8 if ahead else 0):
                times = spread(cols[b + 1][m], q) * inverse
                for v in ahead:
                    ahead[v][q] = ahead[v][q] - cols[v][m] * times
            work[b] = work[b] - jnp.where(sub > m, lead, 0.0) * row
            for v in range(b + 1, count):
                work[v] = work[v] - cols[v][m] * row
        done.append(work[b] * lax.rsqrt(scale))
        cols = {**ahead, **columns(b + 1, near, count)}
    return jnp.concatenate(done, axis=0)[:, :MODES]


def basis_kernel(scale, mine_ref, other_ref, start_ref, inner_ref, edge_ref, before_ref, basis_ref, modes_ref, rows_ref, out_ref):
    first = is_even("row")
    mine, other = mine_ref[...], other_ref[...]
    cross = jnp.where(first, mine, other)[:HALF]
    second = jnp.where(first, other, mine)
    folded = second[:HALF]
    i = lax.broadcasted_iota(jnp.int32, (HALF, HALF), 0)
    j = lax.broadcasted_iota(jnp.int32, (HALF, HALF), 1)
    flipped = folded.T
    top = jnp.where(i <= j, folded, flipped)
    low = jnp.where(i > j, folded, jnp.where(i < j, flipped, second[HALF : HALF + 1]))
    gram = jnp.concatenate(
        [jnp.concatenate([top, cross], axis=1), jnp.concatenate([cross.T, low], axis=1)], axis=0
    )
    gram = gram * scale
    stacked = dot(start_ref[...], gram)
    for sweep in range(SWEEPS):
        inner = lax.dot_general(
            stacked, stacked, (((1,), (1,)), ((), ())), precision=HIGHEST, preferred_element_type=F32
        )
        if sweep < SWEEPS - 1:
            beside = dot(stacked, gram)
        else:
            beside = jnp.concatenate([stacked, dot(stacked, frame_order(1))], axis=1)
        stacked = dot(inverse_factor(inner), beside)
    basis = stacked[:, :FRAMES]
    basis_ref[...] = stacked[:, FRAMES:]
    twice = jnp.concatenate([basis, basis], axis=0)
    before = jnp.concatenate([before_ref[:8], before_ref[8:]], axis=1)
    before = jnp.concatenate([before, pltpu.roll(before, 4, 0)], axis=0)
    before = jnp.where(lax.axis_index("col") == 0, inner_ref[0].astype(F32), before)
    cell = jnp.where(second_cells(), before, edge_ref[...].astype(F32)).astype(BF16)
    flat = jnp.concatenate([inner_ref[1:].reshape(16 * BLOCKS - 16, FRAMES), cell], axis=0)
    rows_ref[...] = lax.dot_general(
        flat, twice.astype(BF16), (((1,), (1,)), ((), ())), preferred_element_type=F32
    )
    left = lax.broadcasted_iota(jnp.int32, (BLOCKS, 2 * MODES), 1) < MODES
    for row in range(2):
        for half in range(2):
            for cell in range(2):
                at = 8 * row + 4 * cell + 2 * half
                field = jnp.where(
                    left, rows_ref[pl.ds(at, BLOCKS, stride=16), :], rows_ref[pl.ds(at + 1, BLOCKS, stride=16), :]
                )
                if cell:
                    field = pltpu.roll(field, 1, 0)
                out_ref[pl.ds(64 * row + 32 * half + 1 - cell, BLOCKS, stride=2), :] = field
            modes_ref[row, :, 128 * half : 128 * half + 128] = out_ref[64 * row + 32 * half : 64 * row + 32 * half + 32]


def call(kernel, outs, n_in, scratch=()):
    return pl.pallas_call(
        kernel,
        out_shape=[jax.ShapeDtypeStruct(shape, dtype) for shape, dtype in outs],
        in_specs=[VMEM] * n_in,
        out_specs=[VMEM] * len(outs),
        scratch_shapes=list(scratch),
        compiler_params=PARAMS,
    )


def pairs(size, start):
    swaps = []
    for i in range(start, size - 1, 2):
        swaps += [(i, i + 1), (i + 1, i)]
    return swaps


def on_device(video, filters, start_basis):
    size_row, size_col = lax.axis_size("row"), lax.axis_size("col")
    near, far = pairs(size_row, 0), pairs(size_row, 1)
    to_left = [(i + 1, i) for i in range(size_col - 1)]

    across = [(a * size_col + i, b * size_col + j) for a, b in far for i, j in to_left]
    send = ((REACH * COLS + 16, FRAMES), BF16)
    tiles = ((BLOCKS + 1, 112, 3 * HALF), BF16)
    rows = (((FRAMES + 1) * ROWS, COLS), F32)
    rows, send_a, send_b, heads = call(send_kernel, [rows, send, send, ((8 * ROWS, FRAMES), F32)], 1)(video)
    got_a = lax.ppermute(send_a, "row", near)
    got_b = lax.ppermute(send_b, "row", far)
    outs = [((96, 3 * HALF), BF16), ((32, 3 * HALF), BF16)]
    side, diag = call(side_kernel, outs, 3)(rows, heads, got_a)
    side = lax.ppermute(side, "col", to_left)
    diag = lax.ppermute(diag, ("row", "col"), across)

    outs = [((BLOCKS, 16, FRAMES), BF16), tiles, ((128, 256), BF16)]
    inner, x, band = call(inner_kernel, outs, 4, [pltpu.VMEM((16, 128), F32)])(
        got_a, got_b, rows, jnp.transpose(filters, (0, 2, 1, 3))
    )
    part, passed = ((SUMMED, HALF), F32), ((16, HALF), F32)
    edge, mine, other, passed = call(edge_kernel, [((16, FRAMES), BF16), part, part, passed], 5)(
        band, x, side, diag, inner
    )

    mine = mine + lax.ppermute(other, "row", near)
    step = 2
    while step < size_row:
        mine = mine + lax.ppermute(mine, "row", [(i, i ^ step) for i in range(size_row)])
        step *= 2
    mine = jnp.concatenate([mine, passed], axis=0)
    summed = lax.broadcasted_iota(jnp.int32, mine.shape, 0) < SUMMED
    step = 1
    col = lax.axis_index("col")
    before = jnp.zeros((16, HALF), F32)
    start = start_basis.T
    while step < size_col:
        if 2 * step >= size_col:
            mine, start = lax.optimization_barrier((mine, start))
            (start,) = call(start_kernel, [((MODES, FRAMES), F32)], 1)(start)
        got = lax.ppermute(mine, "col", [(i, i ^ step) for i in range(size_col)])
        mine = jnp.where(summed, mine + got, got)
        before = jnp.where((col & (2 * step - 1)) == step, got[SUMMED:], before)
        step *= 2
    mine = mine[:SUMMED]
    other = lax.ppermute(mine, "row", near)

    features = ORIENT * (size_row * ROWS // 4) * (size_col * COLS // 4)
    kernel = functools.partial(basis_kernel, 1.0 / features)
    basis, modes = call(
        kernel,
        [((MODES, FRAMES), F32), ((ROWS // 4, COLS // 4, ORIENT * MODES), F32)],
        6,
        [pltpu.VMEM((FRAMES, 2 * MODES), F32), pltpu.VMEM((128, 128), F32)],
    )(mine, other, start, inner, edge, before)
    return basis.T, modes


def solution(mesh):
    return jax.shard_map(
        on_device,
        mesh=mesh,
        in_specs=(P("grp", "row", "col"), P(), P()),
        out_specs=(P("grp", None), P(("grp", "row"), "col", None)),
        check_vma=False,
    )
```

```python
import functools

import jax
import jax.numpy as jnp
from jax import lax
from jax.experimental import pallas as pl
from jax.experimental.pallas import tpu as pltpu
from jax.sharding import PartitionSpec as P

FRAMES = 256
HALF = FRAMES // 2
MODES = 64
ORIENT = 4
TAPS = 7
REACH = 3
SWEEPS = 2
ROWS = 8
COLS = 128
SUMMED = HALF + 8
BLOCKS = 16
UNROLL = 16
AHEAD = 3
F32 = jnp.float32
BF16 = jnp.bfloat16
HIGHEST = lax.Precision.HIGHEST
PARAMS = pltpu.CompilerParams(vmem_limit_bytes=24 * 1024 * 1024)
VMEM = pl.BlockSpec(memory_space=pltpu.VMEM)


def turned(rows_ref, row, group):
    return rows_ref[pl.ds(group * ROWS + row, HALF, stride=2 * ROWS), :].T


def blocked(upper, lower):
    both = [part.reshape(BLOCKS, 8, HALF) for part in (upper, lower)]
    return jnp.concatenate(both, axis=1).astype(BF16)


def is_even(axis):
    return (lax.axis_index(axis) & 1) == 0


def send_kernel(video_ref, rows_ref, send_a_ref, send_b_ref, heads_ref):
    even = is_even("row")
    rows_ref[...] = video_ref[...].astype(F32).reshape(rows_ref.shape)
    for group in range(2):
        lanes = slice(HALF * group, HALF * group + HALF)
        tiles = [turned(rows_ref, row, group) for row in range(ROWS)]
        heads_ref[:, lanes] = jnp.concatenate([tile[:8] for tile in tiles], axis=0)
        for i in range(REACH):
            first, last = tiles[i], tiles[ROWS - REACH + i]
            at = slice(COLS * i, COLS * i + COLS)
            send_a_ref[at, lanes] = jnp.where(even, last, first).astype(BF16)
            send_b_ref[at, lanes] = jnp.where(even, first, last).astype(BF16)
    fill = jnp.zeros((8, COLS), F32)
    final = rows_ref[FRAMES * ROWS : FRAMES * ROWS + ROWS, :]
    shifted = pltpu.roll(final, REACH, 0)
    first, last = (jnp.concatenate([part, fill], axis=0).astype(BF16) for part in (final, shifted))
    for ref, chosen in ((send_a_ref, jnp.where(even, last, first)), (send_b_ref, jnp.where(even, first, last))):
        ref[REACH * COLS : REACH * COLS + 16, 0:COLS] = chosen
        ref[REACH * COLS : REACH * COLS + 16, COLS : 2 * COLS] = chosen


def side_kernel(rows_ref, heads_ref, a_ref, side_ref, diag_ref):
    even = is_even("row")
    fill = jnp.zeros((8, HALF), F32)
    ends = rows_ref[FRAMES * ROWS : FRAMES * ROWS + ROWS, :]
    heads = in_groups([heads_ref[8 * i : 8 * i + 8] for i in range(ROWS)], ends)
    near = expanded(a_ref[...].astype(F32), 8)
    for group in range(3):
        lanes = slice(HALF * group, HALF * group + HALF)
        sent = [row[group] for row in heads + near] + [fill]
        side_ref[:, lanes] = jnp.concatenate(sent, axis=0).astype(BF16)
        chosen = [jnp.where(even, heads[i][group], heads[ROWS - REACH + i][group]) for i in range(REACH)]
        diag_ref[:, lanes] = jnp.concatenate(chosen + [fill], axis=0).astype(BF16)


def in_groups(tiles, ends):
    count = tiles[0].shape[0]
    final = lax.broadcasted_iota(jnp.int32, (count, HALF), 1) == HALF - 1
    ends = ends.T
    rows = []
    for i, tile in enumerate(tiles):
        late = jnp.where(final, ends[:count, i : i + 1], pltpu.roll(tile[:, :HALF], HALF - 1, 1))
        rows.append([tile[:, :HALF], tile[:, HALF:], late])
    return rows


def expanded(got, count):
    tiles = [got[COLS * i : COLS * i + count] for i in range(REACH)]
    return in_groups(tiles, got[REACH * COLS : REACH * COLS + 8, :COLS])


def make_band(filters_ref, band_ref, taps_ref):
    taps_ref[...] = jnp.zeros((16, 128), F32)
    for orient in range(ORIENT):
        for part in range(2):
            for i in range(TAPS):
                line = filters_ref[orient, i, part : part + 1, :]
                for cell in range(2):
                    row, lane = 8 * part + 4 * cell + orient, 64 * cell + 8 * i
                    taps_ref[row : row + 1, lane : lane + TAPS] = line
    taps = taps_ref[...]
    high = taps.astype(BF16)
    low = (taps - high.astype(F32)).astype(BF16)
    parts = jnp.concatenate([high, low], axis=0)
    tap = lax.broadcasted_iota(jnp.int32, (128, 128), 0)
    lane = lax.broadcasted_iota(jnp.int32, (128, 128), 1)
    column = ((lane >> 6) << 3) | (lane & 7)
    row_hit = ((lane >> 3) & 7) == ((tap >> 3) & 7)
    ahead = column - (tap & 7) - 1 - 4 * (tap >> 6)
    for j in range(4):
        select = jnp.where(row_hit & (ahead == j), 1.0, 0.0).astype(BF16)
        base = jnp.dot(parts, select, preferred_element_type=F32)
        for i in range(2):
            start = (4 * i + j) * 16
            rolled = (pltpu.roll(base, 8, 1) if i else base).astype(BF16)
            band_ref[start : start + 16, 0:128] = rolled[:16]
            band_ref[start : start + 16, 128:256] = rolled[16:]


def dot(a, b):
    return jnp.dot(a, b, precision=HIGHEST, preferred_element_type=F32)


def start_kernel(start_ref, basis_ref):
    basis_ref[...] = dot(start_ref[...], frame_order(0))


def frame_order(axis):
    frame = lax.broadcasted_iota(jnp.int32, (FRAMES, FRAMES), axis)
    lane = lax.broadcasted_iota(jnp.int32, (FRAMES, FRAMES), 1 - axis)
    return jnp.where(frame == 2 * (lane & (HALF - 1)) + (lane >> 7), 1.0, 0.0).astype(F32)


def place_rows(a_ref, b_ref, rows_ref, x_ref):
    even = is_even("row")
    got_a, got_b = a_ref[...], b_ref[...]
    above = expanded(jnp.where(even, got_b, got_a).astype(F32), COLS)
    below = expanded(jnp.where(even, got_a, got_b).astype(F32), COLS)
    x_ref[0] = jnp.zeros((112, 3 * HALF), BF16)
    for group in range(3):
        own = [turned(rows_ref, row, group) for row in range(ROWS)]
        tiles = [row[group] for row in above] + own + [row[group] for row in below]
        for pair in range(len(tiles) // 2):
            at = slice(16 * pair, 16 * pair + 16)
            x_ref[1:, at, HALF * group : HALF * group + HALF] = blocked(tiles[2 * pair], tiles[2 * pair + 1])


def block_feats(band_ref, left, right):
    pooled = []
    for cell in range(2):
        windows = []
        for half in range(2):
            at = 16 * (2 * cell + half)
            windows.append(jnp.concatenate([left[at : at + 64], right[at : at + 64]], axis=0))
        window = jnp.concatenate(
            [windows[0][:, :FRAMES], windows[1][:, :FRAMES], windows[0][:, FRAMES:], windows[1][:, FRAMES:]], axis=1
        )
        window = jnp.concatenate([window, window], axis=0)
        resp = jnp.dot(band_ref[...], window, preferred_element_type=F32)
        total = [None, None]
        for half in range(2):
            starts = (FRAMES * half, FRAMES * half + HALF, 2 * FRAMES + HALF * half)
            for pixel in range(8):
                at = 16 * pixel
                real = [resp[at : at + 8, s : s + HALF] for s in starts]
                imag = [resp[at + 8 : at + 16, s : s + HALF] for s in starts]
                for g in range(2):
                    prod_real = real[g + 1] * real[g] + imag[g + 1] * imag[g]
                    prod_imag = imag[g + 1] * real[g] - real[g + 1] * imag[g]
                    motion = prod_imag * lax.rsqrt(prod_real * prod_real + prod_imag * prod_imag + 1.0)
                    total[g] = motion if total[g] is None else total[g] + motion
        pooled.append(jnp.concatenate(total, axis=1) * (1.0 / 16.0))
    return jnp.concatenate(pooled, axis=0)


def second_cells():
    return (lax.broadcasted_iota(jnp.int32, (16, FRAMES), 0) & 4) == 4


def inner_kernel(a_ref, b_ref, rows_ref, filters_ref, feats_ref, x_ref, band_ref, taps_ref):
    make_band(filters_ref, band_ref, taps_ref)
    place_rows(a_ref, b_ref, rows_ref, x_ref)

    def body(step, carry):
        for i in range(UNROLL):
            block = UNROLL * step + i
            feats_ref[block] = block_feats(band_ref, x_ref[block], x_ref[block + 1]).astype(BF16)
        return carry

    lax.fori_loop(0, BLOCKS // UNROLL, body, 0)
    begins = lax.axis_index("col") == 0
    feats_ref[0] = jnp.where(second_cells() & begins, feats_ref[0].astype(F32), 0.0).astype(BF16)


def edge_kernel(band_ref, x_ref, side_ref, diag_ref, inner_ref, edge_ref, mine_ref, other_ref, passed_ref):
    even = is_even("row")
    side = side_ref[...].astype(F32)
    near, far = side[8 * ROWS : 8 * ROWS + 8 * REACH], diag_ref[...].astype(F32)[: 8 * REACH]
    rows = [jnp.where(even, far, near), side[: 8 * ROWS], jnp.where(even, near, far)]
    edge = block_feats(band_ref, x_ref[BLOCKS], jnp.concatenate(rows, axis=0).astype(BF16))
    ends = lax.axis_index("col") == lax.axis_size("col") - 1
    edge = jnp.where(second_cells() & ends, 0.0, edge).astype(BF16)
    edge_ref[...] = edge
    flat = jnp.concatenate([inner_ref[...].reshape(16 * BLOCKS, FRAMES), edge], axis=0)
    gram = lax.dot_general(flat, flat, (((0,), (0,)), ((), ())), preferred_element_type=F32)
    top, cross, low = gram[:HALF, :HALF], gram[:HALF, HALF:], gram[HALF:, HALF:]
    i = lax.broadcasted_iota(jnp.int32, (HALF, HALF), 0)
    j = lax.broadcasted_iota(jnp.int32, (HALF, HALF), 1)
    folded = jnp.where(i <= j, top, low)
    diagonal = jnp.sum(jnp.where(i == j, low, 0.0), axis=0, keepdims=True)
    first = is_even("row")
    spare = jnp.broadcast_to(diagonal, (8, HALF))
    mine_ref[0:HALF] = jnp.where(first, cross, folded)
    mine_ref[HALF:SUMMED] = spare
    other_ref[0:HALF] = jnp.where(first, folded, cross)
    other_ref[HALF:SUMMED] = spare
    edge = edge.astype(F32)
    passed = jnp.where(second_cells()[:8], edge[:8], pltpu.roll(edge[8:], 4, 0))
    passed_ref[0:8] = passed[:, :HALF]
    passed_ref[8:16] = passed[:, HALF:]


def inverse_factor(inner):
    count = MODES // 8
    shape = (8, 2 * MODES)
    i = lax.broadcasted_iota(jnp.int32, (MODES, MODES), 0)
    j = lax.broadcasted_iota(jnp.int32, (MODES, MODES), 1)
    work = jnp.concatenate([jnp.where(i == j, 1.0, 0.0), inner], axis=1)
    work = [work[8 * v : 8 * v + 8] for v in range(count)]
    sub = lax.broadcasted_iota(jnp.int32, shape, 0)

    def columns(b, first, last):
        lanes = [MODES + 8 * b + m for m in range(8)]
        return {v: [jnp.broadcast_to(work[v][:, k : k + 1], shape) for k in lanes] for v in range(first, last)}

    def spread(tile, row):
        return jnp.broadcast_to(tile[row : row + 1], shape)

    cols = columns(0, 0, count)
    done = []
    for b in range(count):
        near = min(count, b + 1 + AHEAD)
        ahead = columns(b + 1, b + 1, near)
        scale = jnp.ones(shape, F32)
        for m in range(8):
            lead = cols[b][m]
            pivot = spread(lead, m)
            inverse = 1.0 / pivot
            scale = jnp.where(sub == m, pivot, scale)
            row = spread(work[b], m) * inverse
            for q in range(m + 1, 8):
                times = spread(lead, q) * inverse
                for v in cols:
                    cols[v][q] = cols[v][q] - cols[v][m] * times
            for q in range(8 if ahead else 0):
                times = spread(cols[b + 1][m], q) * inverse
                for v in ahead:
                    ahead[v][q] = ahead[v][q] - cols[v][m] * times
            work[b] = work[b] - jnp.where(sub > m, lead, 0.0) * row
            for v in range(b + 1, count):
                work[v] = work[v] - cols[v][m] * row
        done.append(work[b] * lax.rsqrt(scale))
        cols = {**ahead, **columns(b + 1, near, count)}
    return jnp.concatenate(done, axis=0)[:, :MODES]


def basis_kernel(scale, mine_ref, other_ref, start_ref, inner_ref, edge_ref, before_ref, basis_ref, modes_ref, rows_ref, out_ref):
    first = is_even("row")
    mine, other = mine_ref[...], other_ref[...]
    cross = jnp.where(first, mine, other)[:HALF]
    second = jnp.where(first, other, mine)
    folded = second[:HALF]
    i = lax.broadcasted_iota(jnp.int32, (HALF, HALF), 0)
    j = lax.broadcasted_iota(jnp.int32, (HALF, HALF), 1)
    flipped = folded.T
    top = jnp.where(i <= j, folded, flipped)
    low = jnp.where(i > j, folded, jnp.where(i < j, flipped, second[HALF : HALF + 1]))
    gram = jnp.concatenate(
        [jnp.concatenate([top, cross], axis=1), jnp.concatenate([cross.T, low], axis=1)], axis=0
    )
    gram = gram * scale
    stacked = dot(start_ref[...], gram)
    for sweep in range(SWEEPS):
        inner = lax.dot_general(
            stacked, stacked, (((1,), (1,)), ((), ())), precision=HIGHEST, preferred_element_type=F32
        )
        if sweep < SWEEPS - 1:
            beside = dot(stacked, gram)
        else:
            beside = jnp.concatenate([stacked, dot(stacked, frame_order(1))], axis=1)
        stacked = dot(inverse_factor(inner), beside)
    basis = stacked[:, :FRAMES]
    basis_ref[...] = stacked[:, FRAMES:]
    twice = jnp.concatenate([basis, basis], axis=0)
    before = jnp.concatenate([before_ref[:8], before_ref[8:]], axis=1)
    before = jnp.concatenate([before, pltpu.roll(before, 4, 0)], axis=0)
    before = jnp.where(lax.axis_index("col") == 0, inner_ref[0].astype(F32), before)
    cell = jnp.where(second_cells(), before, edge_ref[...].astype(F32)).astype(BF16)
    flat = jnp.concatenate([inner_ref[1:].reshape(16 * BLOCKS - 16, FRAMES), cell], axis=0)
    rows_ref[...] = lax.dot_general(
        flat, twice.astype(BF16), (((1,), (1,)), ((), ())), preferred_element_type=F32
    )
    left = lax.broadcasted_iota(jnp.int32, (BLOCKS, 2 * MODES), 1) < MODES
    for row in range(2):
        for half in range(2):
            for cell in range(2):
                at = 8 * row + 4 * cell + 2 * half
                field = jnp.where(
                    left, rows_ref[pl.ds(at, BLOCKS, stride=16), :], rows_ref[pl.ds(at + 1, BLOCKS, stride=16), :]
                )
                if cell:
                    field = pltpu.roll(field, 1, 0)
                out_ref[pl.ds(64 * row + 32 * half + 1 - cell, BLOCKS, stride=2), :] = field
            modes_ref[row, :, 128 * half : 128 * half + 128] = out_ref[64 * row + 32 * half : 64 * row + 32 * half + 32]


def call(kernel, outs, n_in, scratch=()):
    return pl.pallas_call(
        kernel,
        out_shape=[jax.ShapeDtypeStruct(shape, dtype) for shape, dtype in outs],
        in_specs=[VMEM] * n_in,
        out_specs=[VMEM] * len(outs),
        scratch_shapes=list(scratch),
        compiler_params=PARAMS,
    )


def pairs(size, start):
    swaps = []
    for i in range(start, size - 1, 2):
        swaps += [(i, i + 1), (i + 1, i)]
    return swaps


def on_device(video, filters, start_basis):
    size_row, size_col = lax.axis_size("row"), lax.axis_size("col")
    near, far = pairs(size_row, 0), pairs(size_row, 1)
    to_left = [(i + 1, i) for i in range(size_col - 1)]

    across = [(a * size_col + i, b * size_col + j) for a, b in far for i, j in to_left]
    send = ((REACH * COLS + 16, FRAMES), BF16)
    tiles = ((BLOCKS + 1, 112, 3 * HALF), BF16)
    rows = (((FRAMES + 1) * ROWS, COLS), F32)
    rows, send_a, send_b, heads = call(send_kernel, [rows, send, send, ((8 * ROWS, FRAMES), F32)], 1)(video)
    got_a = lax.ppermute(send_a, "row", near)
    got_b = lax.ppermute(send_b, "row", far)
    outs = [((96, 3 * HALF), BF16), ((32, 3 * HALF), BF16)]
    side, diag = call(side_kernel, outs, 3)(rows, heads, got_a)
    side = lax.ppermute(side, "col", to_left)
    diag = lax.ppermute(diag, ("row", "col"), across)

    outs = [((BLOCKS, 16, FRAMES), BF16), tiles, ((128, 256), BF16)]
    inner, x, band = call(inner_kernel, outs, 4, [pltpu.VMEM((16, 128), F32)])(
        got_a, got_b, rows, jnp.transpose(filters, (0, 2, 1, 3))
    )
    part, passed = ((SUMMED, HALF), F32), ((16, HALF), F32)
    edge, mine, other, passed = call(edge_kernel, [((16, FRAMES), BF16), part, part, passed], 5)(
        band, x, side, diag, inner
    )

    mine = mine + lax.ppermute(other, "row", near)
    step = 2
    while step < size_row:
        mine = mine + lax.ppermute(mine, "row", [(i, i ^ step) for i in range(size_row)])
        step *= 2
    mine = jnp.concatenate([mine, passed], axis=0)
    summed = lax.broadcasted_iota(jnp.int32, mine.shape, 0) < SUMMED
    step = 1
    col = lax.axis_index("col")
    before = jnp.zeros((16, HALF), F32)
    start = start_basis.T
    while step < size_col:
        if 2 * step >= size_col:
            mine, start = lax.optimization_barrier((mine, start))
            (start,) = call(start_kernel, [((MODES, FRAMES), F32)], 1)(start)
        got = lax.ppermute(mine, "col", [(i, i ^ step) for i in range(size_col)])
        mine = jnp.where(summed, mine + got, got)
        before = jnp.where((col & (2 * step - 1)) == step, got[SUMMED:], before)
        step *= 2
    mine = mine[:SUMMED]
    other = lax.ppermute(mine, "row", near)

    features = ORIENT * (size_row * ROWS // 4) * (size_col * COLS // 4)
    kernel = functools.partial(basis_kernel, 1.0 / features)
    basis, modes = call(
        kernel,
        [((MODES, FRAMES), F32), ((ROWS // 4, COLS // 4, ORIENT * MODES), F32)],
        6,
        [pltpu.VMEM((FRAMES, 2 * MODES), F32), pltpu.VMEM((128, 128), F32)],
    )(mine, other, start, inner, edge, before)
    return basis.T, modes


def solution(mesh):
    return jax.shard_map(
        on_device,
        mesh=mesh,
        in_specs=(P("grp", "row", "col"), P(), P()),
        out_specs=(P("grp", None), P(("grp", "row"), "col", None)),
        check_vma=False,
    )
```

```python
import functools

import jax
import jax.numpy as jnp
from jax import lax
from jax.experimental import pallas as pl
from jax.experimental.pallas import tpu as pltpu
from jax.sharding import PartitionSpec as P

FRAMES = 256
HALF = FRAMES // 2
MODES = 64
ORIENT = 4
TAPS = 7
REACH = 3
SWEEPS = 2
ROWS = 8
COLS = 128
SUMMED = HALF + 8
BLOCKS = 16
UNROLL = 16
AHEAD = 3
F32 = jnp.float32
BF16 = jnp.bfloat16
HIGHEST = lax.Precision.HIGHEST
PARAMS = pltpu.CompilerParams(vmem_limit_bytes=24 * 1024 * 1024)
VMEM = pl.BlockSpec(memory_space=pltpu.VMEM)


def turned(rows_ref, row, group):
    return rows_ref[pl.ds(group * ROWS + row, HALF, stride=2 * ROWS), :].T


def blocked(upper, lower):
    both = [part.reshape(BLOCKS, 8, HALF) for part in (upper, lower)]
    return jnp.concatenate(both, axis=1).astype(BF16)


def is_even(axis):
    return (lax.axis_index(axis) & 1) == 0


def send_kernel(video_ref, rows_ref, send_a_ref, send_b_ref, heads_ref):
    even = is_even("row")
    rows_ref[...] = video_ref[...].astype(F32).reshape(rows_ref.shape)
    for group in range(2):
        lanes = slice(HALF * group, HALF * group + HALF)
        tiles = [turned(rows_ref, row, group) for row in range(ROWS)]
        heads_ref[:, lanes] = jnp.concatenate([tile[:8] for tile in tiles], axis=0)
        for i in range(REACH):
            first, last = tiles[i], tiles[ROWS - REACH + i]
            at = slice(COLS * i, COLS * i + COLS)
            send_a_ref[at, lanes] = jnp.where(even, last, first).astype(BF16)
            send_b_ref[at, lanes] = jnp.where(even, first, last).astype(BF16)
    fill = jnp.zeros((8, COLS), F32)
    final = rows_ref[FRAMES * ROWS : FRAMES * ROWS + ROWS, :]
    shifted = pltpu.roll(final, REACH, 0)
    first, last = (jnp.concatenate([part, fill], axis=0).astype(BF16) for part in (final, shifted))
    for ref, chosen in ((send_a_ref, jnp.where(even, last, first)), (send_b_ref, jnp.where(even, first, last))):
        ref[REACH * COLS : REACH * COLS + 16, 0:COLS] = chosen
        ref[REACH * COLS : REACH * COLS + 16, COLS : 2 * COLS] = chosen


def side_kernel(rows_ref, heads_ref, a_ref, side_ref, diag_ref):
    even = is_even("row")
    ends = rows_ref[FRAMES * ROWS : FRAMES * ROWS + ROWS, :]
    heads = in_groups([heads_ref[8 * i : 8 * i + 8] for i in range(ROWS)], ends)
    near = expanded(a_ref[...].astype(F32), 8)
    for group in range(3):
        lanes = slice(HALF * group, HALF * group + HALF)
        sent = [row[group] for row in heads + near]
        side_ref[:, lanes] = jnp.concatenate(sent, axis=0).astype(BF16)
        chosen = [jnp.where(even, heads[i][group], heads[ROWS - REACH + i][group]) for i in range(REACH)]
        diag_ref[:, lanes] = jnp.concatenate(chosen, axis=0).astype(BF16)


def in_groups(tiles, ends):
    count = tiles[0].shape[0]
    final = lax.broadcasted_iota(jnp.int32, (count, HALF), 1) == HALF - 1
    ends = ends.T
    rows = []
    for i, tile in enumerate(tiles):
        late = jnp.where(final, ends[:count, i : i + 1], pltpu.roll(tile[:, :HALF], HALF - 1, 1))
        rows.append([tile[:, :HALF], tile[:, HALF:], late])
    return rows


def expanded(got, count):
    tiles = [got[COLS * i : COLS * i + count] for i in range(REACH)]
    return in_groups(tiles, got[REACH * COLS : REACH * COLS + 8, :COLS])


def make_band(filters_ref, band_ref, taps_ref):
    taps_ref[...] = jnp.zeros((16, 128), F32)
    for orient in range(ORIENT):
        for part in range(2):
            for i in range(TAPS):
                line = filters_ref[orient, i, part : part + 1, :]
                for cell in range(2):
                    row, lane = 8 * part + 4 * cell + orient, 64 * cell + 8 * i
                    taps_ref[row : row + 1, lane : lane + TAPS] = line
    taps = taps_ref[...]
    high = taps.astype(BF16)
    low = (taps - high.astype(F32)).astype(BF16)
    parts = jnp.concatenate([high, low], axis=0)
    tap = lax.broadcasted_iota(jnp.int32, (128, 128), 0)
    lane = lax.broadcasted_iota(jnp.int32, (128, 128), 1)
    column = ((lane >> 6) << 3) | (lane & 7)
    row_hit = ((lane >> 3) & 7) == ((tap >> 3) & 7)
    ahead = column - (tap & 7) - 1 - 4 * (tap >> 6)
    for j in range(4):
        select = jnp.where(row_hit & (ahead == j), 1.0, 0.0).astype(BF16)
        base = jnp.dot(parts, select, preferred_element_type=F32)
        for i in range(2):
            start = (4 * i + j) * 16
            rolled = (pltpu.roll(base, 8, 1) if i else base).astype(BF16)
            band_ref[start : start + 16, 0:128] = rolled[:16]
            band_ref[start : start + 16, 128:256] = rolled[16:]


def dot(a, b):
    return jnp.dot(a, b, precision=HIGHEST, preferred_element_type=F32)


def start_kernel(start_ref, basis_ref):
    basis_ref[...] = dot(start_ref[...], frame_order(0))


def frame_order(axis):
    frame = lax.broadcasted_iota(jnp.int32, (FRAMES, FRAMES), axis)
    lane = lax.broadcasted_iota(jnp.int32, (FRAMES, FRAMES), 1 - axis)
    return jnp.where(frame == 2 * (lane & (HALF - 1)) + (lane >> 7), 1.0, 0.0).astype(F32)


def place_rows(a_ref, b_ref, rows_ref, x_ref):
    even = is_even("row")
    got_a, got_b = a_ref[...], b_ref[...]
    above = expanded(jnp.where(even, got_b, got_a).astype(F32), COLS)
    below = expanded(jnp.where(even, got_a, got_b).astype(F32), COLS)
    x_ref[0] = jnp.zeros((112, 3 * HALF), BF16)
    for group in range(3):
        own = [turned(rows_ref, row, group) for row in range(ROWS)]
        tiles = [row[group] for row in above] + own + [row[group] for row in below]
        for pair in range(len(tiles) // 2):
            at = slice(16 * pair, 16 * pair + 16)
            x_ref[1:, at, HALF * group : HALF * group + HALF] = blocked(tiles[2 * pair], tiles[2 * pair + 1])


def block_feats(band_ref, left, right):
    pooled = []
    for cell in range(2):
        windows = []
        for half in range(2):
            at = 16 * (2 * cell + half)
            windows.append(jnp.concatenate([left[at : at + 64], right[at : at + 64]], axis=0))
        window = jnp.concatenate(
            [windows[0][:, :FRAMES], windows[1][:, :FRAMES], windows[0][:, FRAMES:], windows[1][:, FRAMES:]], axis=1
        )
        window = jnp.concatenate([window, window], axis=0)
        resp = jnp.dot(band_ref[...], window, preferred_element_type=F32)
        total = [None, None]
        for half in range(2):
            starts = (FRAMES * half, FRAMES * half + HALF, 2 * FRAMES + HALF * half)
            for pixel in range(8):
                at = 16 * pixel
                real = [resp[at : at + 8, s : s + HALF] for s in starts]
                imag = [resp[at + 8 : at + 16, s : s + HALF] for s in starts]
                for g in range(2):
                    prod_real = real[g + 1] * real[g] + imag[g + 1] * imag[g]
                    prod_imag = imag[g + 1] * real[g] - real[g + 1] * imag[g]
                    motion = prod_imag * lax.rsqrt(prod_real * prod_real + prod_imag * prod_imag + 1.0)
                    total[g] = motion if total[g] is None else total[g] + motion
        pooled.append(jnp.concatenate(total, axis=1) * (1.0 / 16.0))
    return jnp.concatenate(pooled, axis=0)


def second_cells():
    return (lax.broadcasted_iota(jnp.int32, (16, FRAMES), 0) & 4) == 4


def inner_kernel(a_ref, b_ref, rows_ref, filters_ref, feats_ref, x_ref, band_ref, taps_ref):
    make_band(filters_ref, band_ref, taps_ref)
    place_rows(a_ref, b_ref, rows_ref, x_ref)

    def body(step, carry):
        for i in range(UNROLL):
            block = UNROLL * step + i
            feats_ref[block] = block_feats(band_ref, x_ref[block], x_ref[block + 1]).astype(BF16)
        return carry

    lax.fori_loop(0, BLOCKS // UNROLL, body, 0)
    begins = lax.axis_index("col") == 0
    feats_ref[0] = jnp.where(second_cells() & begins, feats_ref[0].astype(F32), 0.0).astype(BF16)


def edge_kernel(band_ref, x_ref, side_ref, diag_ref, inner_ref, edge_ref, mine_ref, other_ref, passed_ref):
    even = is_even("row")
    side = side_ref[...].astype(F32)
    near, far = side[8 * ROWS : 8 * ROWS + 8 * REACH], diag_ref[...].astype(F32)
    rows = [jnp.where(even, far, near), side[: 8 * ROWS], jnp.where(even, near, far)]
    edge = block_feats(band_ref, x_ref[BLOCKS], jnp.concatenate(rows, axis=0).astype(BF16))
    ends = lax.axis_index("col") == lax.axis_size("col") - 1
    edge = jnp.where(second_cells() & ends, 0.0, edge).astype(BF16)
    edge_ref[...] = edge
    flat = jnp.concatenate([inner_ref[...].reshape(16 * BLOCKS, FRAMES), edge], axis=0)
    gram = lax.dot_general(flat, flat, (((0,), (0,)), ((), ())), preferred_element_type=F32)
    top, cross, low = gram[:HALF, :HALF], gram[:HALF, HALF:], gram[HALF:, HALF:]
    i = lax.broadcasted_iota(jnp.int32, (HALF, HALF), 0)
    j = lax.broadcasted_iota(jnp.int32, (HALF, HALF), 1)
    folded = jnp.where(i <= j, top, low)
    diagonal = jnp.sum(jnp.where(i == j, low, 0.0), axis=0, keepdims=True)
    first = is_even("row")
    spare = jnp.broadcast_to(diagonal, (8, HALF))
    mine_ref[0:HALF] = jnp.where(first, cross, folded)
    mine_ref[HALF:SUMMED] = spare
    other_ref[0:HALF] = jnp.where(first, folded, cross)
    other_ref[HALF:SUMMED] = spare
    edge = edge.astype(F32)
    passed = jnp.where(second_cells()[:8], edge[:8], pltpu.roll(edge[8:], 4, 0))
    passed_ref[0:8] = passed[:, :HALF]
    passed_ref[8:16] = passed[:, HALF:]


def inverse_factor(inner):
    count = MODES // 8
    shape = (8, 2 * MODES)
    i = lax.broadcasted_iota(jnp.int32, (MODES, MODES), 0)
    j = lax.broadcasted_iota(jnp.int32, (MODES, MODES), 1)
    work = jnp.concatenate([jnp.where(i == j, 1.0, 0.0), inner], axis=1)
    work = [work[8 * v : 8 * v + 8] for v in range(count)]
    sub = lax.broadcasted_iota(jnp.int32, shape, 0)

    def columns(b, first, last):
        lanes = [MODES + 8 * b + m for m in range(8)]
        return {v: [jnp.broadcast_to(work[v][:, k : k + 1], shape) for k in lanes] for v in range(first, last)}

    def spread(tile, row):
        return jnp.broadcast_to(tile[row : row + 1], shape)

    cols = columns(0, 0, count)
    done = []
    for b in range(count):
        near = min(count, b + 1 + AHEAD)
        ahead = columns(b + 1, b + 1, near)
        scale = jnp.ones(shape, F32)
        for m in range(8):
            lead = cols[b][m]
            pivot = spread(lead, m)
            inverse = 1.0 / pivot
            scale = jnp.where(sub == m, pivot, scale)
            row = spread(work[b], m) * inverse
            for q in range(m + 1, 8):
                times = spread(lead, q) * inverse
                for v in cols:
                    cols[v][q] = cols[v][q] - cols[v][m] * times
            for q in range(8 if ahead else 0):
                times = spread(cols[b + 1][m], q) * inverse
                for v in ahead:
                    ahead[v][q] = ahead[v][q] - cols[v][m] * times
            work[b] = work[b] - jnp.where(sub > m, lead, 0.0) * row
            for v in range(b + 1, count):
                work[v] = work[v] - cols[v][m] * row
        done.append(work[b] * lax.rsqrt(scale))
        cols = {**ahead, **columns(b + 1, near, count)}
    return jnp.concatenate(done, axis=0)[:, :MODES]


def basis_kernel(scale, mine_ref, other_ref, start_ref, inner_ref, edge_ref, before_ref, basis_ref, modes_ref, rows_ref, out_ref):
    first = is_even("row")
    mine, other = mine_ref[...], other_ref[...]
    cross = jnp.where(first, mine, other)[:HALF]
    second = jnp.where(first, other, mine)
    folded = second[:HALF]
    i = lax.broadcasted_iota(jnp.int32, (HALF, HALF), 0)
    j = lax.broadcasted_iota(jnp.int32, (HALF, HALF), 1)
    flipped = folded.T
    top = jnp.where(i <= j, folded, flipped)
    low = jnp.where(i > j, folded, jnp.where(i < j, flipped, second[HALF : HALF + 1]))
    gram = jnp.concatenate(
        [jnp.concatenate([top, cross], axis=1), jnp.concatenate([cross.T, low], axis=1)], axis=0
    )
    gram = gram * scale
    stacked = dot(start_ref[...], gram)
    for sweep in range(SWEEPS):
        inner = lax.dot_general(
            stacked, stacked, (((1,), (1,)), ((), ())), precision=HIGHEST, preferred_element_type=F32
        )
        if sweep < SWEEPS - 1:
            beside = dot(stacked, gram)
        else:
            beside = jnp.concatenate([stacked, dot(stacked, frame_order(1))], axis=1)
        stacked = dot(inverse_factor(inner), beside)
    basis = stacked[:, :FRAMES]
    basis_ref[...] = stacked[:, FRAMES:]
    twice = jnp.concatenate([basis, basis], axis=0)
    before = jnp.concatenate([before_ref[:8], before_ref[8:]], axis=1)
    before = jnp.concatenate([before, pltpu.roll(before, 4, 0)], axis=0)
    before = jnp.where(lax.axis_index("col") == 0, inner_ref[0].astype(F32), before)
    cell = jnp.where(second_cells(), before, edge_ref[...].astype(F32)).astype(BF16)
    flat = jnp.concatenate([inner_ref[1:].reshape(16 * BLOCKS - 16, FRAMES), cell], axis=0)
    rows_ref[...] = lax.dot_general(
        flat, twice.astype(BF16), (((1,), (1,)), ((), ())), preferred_element_type=F32
    )
    left = lax.broadcasted_iota(jnp.int32, (BLOCKS, 2 * MODES), 1) < MODES
    for row in range(2):
        for half in range(2):
            for cell in range(2):
                at = 8 * row + 4 * cell + 2 * half
                field = jnp.where(
                    left, rows_ref[pl.ds(at, BLOCKS, stride=16), :], rows_ref[pl.ds(at + 1, BLOCKS, stride=16), :]
                )
                if cell:
                    field = pltpu.roll(field, 1, 0)
                out_ref[pl.ds(64 * row + 32 * half + 1 - cell, BLOCKS, stride=2), :] = field
            modes_ref[row, :, 128 * half : 128 * half + 128] = out_ref[64 * row + 32 * half : 64 * row + 32 * half + 32]


def call(kernel, outs, n_in, scratch=()):
    return pl.pallas_call(
        kernel,
        out_shape=[jax.ShapeDtypeStruct(shape, dtype) for shape, dtype in outs],
        in_specs=[VMEM] * n_in,
        out_specs=[VMEM] * len(outs),
        scratch_shapes=list(scratch),
        compiler_params=PARAMS,
    )


def pairs(size, start):
    swaps = []
    for i in range(start, size - 1, 2):
        swaps += [(i, i + 1), (i + 1, i)]
    return swaps


def on_device(video, filters, start_basis):
    size_row, size_col = lax.axis_size("row"), lax.axis_size("col")
    near, far = pairs(size_row, 0), pairs(size_row, 1)
    to_left = [(i + 1, i) for i in range(size_col - 1)]

    across = [(a * size_col + i, b * size_col + j) for a, b in far for i, j in to_left]
    send = ((REACH * COLS + 16, FRAMES), BF16)
    tiles = ((BLOCKS + 1, 112, 3 * HALF), BF16)
    rows = (((FRAMES + 1) * ROWS, COLS), F32)
    rows, send_a, send_b, heads = call(send_kernel, [rows, send, send, ((8 * ROWS, FRAMES), F32)], 1)(video)
    got_a = lax.ppermute(send_a, "row", near)
    got_b = lax.ppermute(send_b, "row", far)
    outs = [((8 * ROWS + 8 * REACH, 3 * HALF), BF16), ((8 * REACH, 3 * HALF), BF16)]
    side, diag = call(side_kernel, outs, 3)(rows, heads, got_a)
    side = lax.ppermute(side, "col", to_left)
    diag = lax.ppermute(diag, ("row", "col"), across)

    outs = [((BLOCKS, 16, FRAMES), BF16), tiles, ((128, 256), BF16)]
    inner, x, band = call(inner_kernel, outs, 4, [pltpu.VMEM((16, 128), F32)])(
        got_a, got_b, rows, jnp.transpose(filters, (0, 2, 1, 3))
    )
    part, passed = ((SUMMED, HALF), F32), ((16, HALF), F32)
    edge, mine, other, passed = call(edge_kernel, [((16, FRAMES), BF16), part, part, passed], 5)(
        band, x, side, diag, inner
    )

    mine = mine + lax.ppermute(other, "row", near)
    step = 2
    while step < size_row:
        mine = mine + lax.ppermute(mine, "row", [(i, i ^ step) for i in range(size_row)])
        step *= 2
    mine = jnp.concatenate([mine, passed], axis=0)
    summed = lax.broadcasted_iota(jnp.int32, mine.shape, 0) < SUMMED
    step = 1
    col = lax.axis_index("col")
    before = jnp.zeros((16, HALF), F32)
    start = start_basis.T
    while step < size_col:
        if 2 * step >= size_col:
            mine, start = lax.optimization_barrier((mine, start))
            (start,) = call(start_kernel, [((MODES, FRAMES), F32)], 1)(start)
        got = lax.ppermute(mine, "col", [(i, i ^ step) for i in range(size_col)])
        mine = jnp.where(summed, mine + got, got)
        before = jnp.where((col & (2 * step - 1)) == step, got[SUMMED:], before)
        step *= 2
    mine = mine[:SUMMED]
    other = lax.ppermute(mine, "row", near)

    features = ORIENT * (size_row * ROWS // 4) * (size_col * COLS // 4)
    kernel = functools.partial(basis_kernel, 1.0 / features)
    basis, modes = call(
        kernel,
        [((MODES, FRAMES), F32), ((ROWS // 4, COLS // 4, ORIENT * MODES), F32)],
        6,
        [pltpu.VMEM((FRAMES, 2 * MODES), F32), pltpu.VMEM((128, 128), F32)],
    )(mine, other, start, inner, edge, before)
    return basis.T, modes


def solution(mesh):
    return jax.shard_map(
        on_device,
        mesh=mesh,
        in_specs=(P("grp", "row", "col"), P(), P()),
        out_specs=(P("grp", None), P(("grp", "row"), "col", None)),
        check_vma=False,
    )
```

```python
import functools

import jax
import jax.numpy as jnp
from jax import lax
from jax.experimental import pallas as pl
from jax.experimental.pallas import tpu as pltpu
from jax.sharding import PartitionSpec as P

FRAMES = 256
HALF = FRAMES // 2
MODES = 64
ORIENT = 4
TAPS = 7
REACH = 3
SWEEPS = 2
ROWS = 8
COLS = 128
SUMMED = HALF + 8
BLOCKS = 16
UNROLL = 16
AHEAD = 3
F32 = jnp.float32
BF16 = jnp.bfloat16
HIGHEST = lax.Precision.HIGHEST
PARAMS = pltpu.CompilerParams(vmem_limit_bytes=24 * 1024 * 1024)
VMEM = pl.BlockSpec(memory_space=pltpu.VMEM)


def turned(rows_ref, row, group):
    return rows_ref[pl.ds(group * ROWS + row, HALF, stride=2 * ROWS), :].T


def blocked(upper, lower):
    both = [part.reshape(BLOCKS, 8, HALF) for part in (upper, lower)]
    return jnp.concatenate(both, axis=1).astype(BF16)


def is_even(axis):
    return (lax.axis_index(axis) & 1) == 0


def send_kernel(video_ref, rows_ref, send_a_ref, send_b_ref, heads_ref):
    even = is_even("row")
    rows_ref[...] = video_ref[...].astype(F32).reshape(rows_ref.shape)
    for group in range(2):
        lanes = slice(HALF * group, HALF * group + HALF)
        tiles = [turned(rows_ref, row, group) for row in range(ROWS)]
        heads_ref[:, lanes] = jnp.concatenate([tile[:8] for tile in tiles], axis=0)
        for i in range(REACH):
            first, last = tiles[i], tiles[ROWS - REACH + i]
            at = slice(COLS * i, COLS * i + COLS)
            send_a_ref[at, lanes] = jnp.where(even, last, first).astype(BF16)
            send_b_ref[at, lanes] = jnp.where(even, first, last).astype(BF16)
    fill = jnp.zeros((8, COLS), F32)
    final = rows_ref[FRAMES * ROWS : FRAMES * ROWS + ROWS, :]
    shifted = pltpu.roll(final, REACH, 0)
    first, last = (jnp.concatenate([part, fill], axis=0).astype(BF16) for part in (final, shifted))
    for ref, chosen in ((send_a_ref, jnp.where(even, last, first)), (send_b_ref, jnp.where(even, first, last))):
        ref[REACH * COLS : REACH * COLS + 16, 0:COLS] = chosen
        ref[REACH * COLS : REACH * COLS + 16, COLS : 2 * COLS] = chosen


def side_kernel(rows_ref, heads_ref, a_ref, side_ref, diag_ref):
    even = is_even("row")
    ends = rows_ref[FRAMES * ROWS : FRAMES * ROWS + ROWS, :]
    heads = in_groups([heads_ref[8 * i : 8 * i + 8] for i in range(ROWS)], ends)
    near = expanded(a_ref[...].astype(F32), 8)
    for group in range(3):
        lanes = slice(HALF * group, HALF * group + HALF)
        sent = [row[group] for row in heads + near]
        side_ref[:, lanes] = jnp.concatenate(sent, axis=0).astype(BF16)
        chosen = [jnp.where(even, heads[i][group], heads[ROWS - REACH + i][group]) for i in range(REACH)]
        diag_ref[:, lanes] = jnp.concatenate(chosen, axis=0).astype(BF16)


def in_groups(tiles, ends):
    count = tiles[0].shape[0]
    final = lax.broadcasted_iota(jnp.int32, (count, HALF), 1) == HALF - 1
    ends = ends.T
    rows = []
    for i, tile in enumerate(tiles):
        late = jnp.where(final, ends[:count, i : i + 1], pltpu.roll(tile[:, :HALF], HALF - 1, 1))
        rows.append([tile[:, :HALF], tile[:, HALF:], late])
    return rows


def expanded(got, count):
    tiles = [got[COLS * i : COLS * i + count] for i in range(REACH)]
    return in_groups(tiles, got[REACH * COLS : REACH * COLS + 8, :COLS])


def make_band(filters_ref, band_ref, taps_ref):
    taps_ref[...] = jnp.zeros((16, 128), F32)
    for orient in range(ORIENT):
        for part in range(2):
            for i in range(TAPS):
                line = filters_ref[orient, i, part : part + 1, :]
                for cell in range(2):
                    row, lane = 8 * part + 4 * cell + orient, 64 * cell + 8 * i
                    taps_ref[row : row + 1, lane : lane + TAPS] = line
    taps = taps_ref[...]
    high = taps.astype(BF16)
    low = (taps - high.astype(F32)).astype(BF16)
    parts = jnp.concatenate([high, low], axis=0)
    tap = lax.broadcasted_iota(jnp.int32, (128, 128), 0)
    lane = lax.broadcasted_iota(jnp.int32, (128, 128), 1)
    column = ((lane >> 6) << 3) | (lane & 7)
    row_hit = ((lane >> 3) & 7) == ((tap >> 3) & 7)
    ahead = column - (tap & 7) - 1 - 4 * (tap >> 6)
    for j in range(4):
        select = jnp.where(row_hit & (ahead == j), 1.0, 0.0).astype(BF16)
        base = jnp.dot(parts, select, preferred_element_type=F32)
        for i in range(2):
            start = (4 * i + j) * 16
            rolled = (pltpu.roll(base, 8, 1) if i else base).astype(BF16)
            band_ref[start : start + 16, 0:128] = rolled[:16]
            band_ref[start : start + 16, 128:256] = rolled[16:]


def dot(a, b):
    return jnp.dot(a, b, precision=HIGHEST, preferred_element_type=F32)


def start_kernel(start_ref, basis_ref):
    basis_ref[...] = dot(start_ref[...], frame_order(0))


def frame_order(axis):
    frame = lax.broadcasted_iota(jnp.int32, (FRAMES, FRAMES), axis)
    lane = lax.broadcasted_iota(jnp.int32, (FRAMES, FRAMES), 1 - axis)
    return jnp.where(frame == 2 * (lane & (HALF - 1)) + (lane >> 7), 1.0, 0.0).astype(F32)


def place_rows(a_ref, b_ref, rows_ref, x_ref):
    even = is_even("row")
    got_a, got_b = a_ref[...], b_ref[...]
    above = expanded(jnp.where(even, got_b, got_a).astype(F32), COLS)
    below = expanded(jnp.where(even, got_a, got_b).astype(F32), COLS)
    x_ref[0] = jnp.zeros((112, 3 * HALF), BF16)
    for group in range(3):
        own = [turned(rows_ref, row, group) for row in range(ROWS)]
        tiles = [row[group] for row in above] + own + [row[group] for row in below]
        for pair in range(len(tiles) // 2):
            at = slice(16 * pair, 16 * pair + 16)
            x_ref[1:, at, HALF * group : HALF * group + HALF] = blocked(tiles[2 * pair], tiles[2 * pair + 1])


def block_feats(band_ref, left, right):
    pooled = []
    for cell in range(2):
        windows = []
        for half in range(2):
            at = 16 * (2 * cell + half)
            windows.append(jnp.concatenate([left[at : at + 64], right[at : at + 64]], axis=0))
        window = jnp.concatenate(
            [windows[0][:, :FRAMES], windows[1][:, :FRAMES], windows[0][:, FRAMES:], windows[1][:, FRAMES:]], axis=1
        )
        window = jnp.concatenate([window, window], axis=0)
        resp = jnp.dot(band_ref[...], window, preferred_element_type=F32)
        total = [None, None]
        for half in range(2):
            starts = (FRAMES * half, FRAMES * half + HALF, 2 * FRAMES + HALF * half)
            for pixel in range(8):
                at = 16 * pixel
                real = [resp[at : at + 8, s : s + HALF] for s in starts]
                imag = [resp[at + 8 : at + 16, s : s + HALF] for s in starts]
                for g in range(2):
                    prod_real = real[g + 1] * real[g] + imag[g + 1] * imag[g]
                    prod_imag = imag[g + 1] * real[g] - real[g + 1] * imag[g]
                    motion = prod_imag * lax.rsqrt(prod_real * prod_real + prod_imag * prod_imag + 1.0)
                    total[g] = motion if total[g] is None else total[g] + motion
        pooled.append(jnp.concatenate(total, axis=1) * (1.0 / 16.0))
    return jnp.concatenate(pooled, axis=0)


def second_cells():
    return (lax.broadcasted_iota(jnp.int32, (16, FRAMES), 0) & 4) == 4


def inner_kernel(a_ref, b_ref, rows_ref, filters_ref, feats_ref, x_ref, band_ref, taps_ref):
    make_band(filters_ref, band_ref, taps_ref)
    place_rows(a_ref, b_ref, rows_ref, x_ref)

    def body(step, carry):
        for i in range(UNROLL):
            block = UNROLL * step + i
            feats_ref[block] = block_feats(band_ref, x_ref[block], x_ref[block + 1]).astype(BF16)
        return carry

    lax.fori_loop(0, BLOCKS // UNROLL, body, 0)
    begins = lax.axis_index("col") == 0
    feats_ref[0] = jnp.where(second_cells() & begins, feats_ref[0].astype(F32), 0.0).astype(BF16)


def frame_sums(flat):
    return lax.dot_general(flat, flat, (((0,), (0,)), ((), ())), preferred_element_type=F32)


def edge_kernel(band_ref, x_ref, side_ref, diag_ref, inner_ref, edge_ref, mine_ref, other_ref, passed_ref):
    even = is_even("row")
    side = side_ref[...].astype(F32)
    near, far = side[8 * ROWS : 8 * ROWS + 8 * REACH], diag_ref[...].astype(F32)
    rows = [jnp.where(even, far, near), side[: 8 * ROWS], jnp.where(even, near, far)]
    edge = block_feats(band_ref, x_ref[BLOCKS], jnp.concatenate(rows, axis=0).astype(BF16))
    ends = lax.axis_index("col") == lax.axis_size("col") - 1
    edge = jnp.where(second_cells() & ends, 0.0, edge).astype(BF16)
    edge_ref[...] = edge
    gram = frame_sums(inner_ref[...].reshape(16 * BLOCKS, FRAMES)) + frame_sums(edge)
    top, cross, low = gram[:HALF, :HALF], gram[:HALF, HALF:], gram[HALF:, HALF:]
    i = lax.broadcasted_iota(jnp.int32, (HALF, HALF), 0)
    j = lax.broadcasted_iota(jnp.int32, (HALF, HALF), 1)
    folded = jnp.where(i <= j, top, low)
    diagonal = jnp.sum(jnp.where(i == j, low, 0.0), axis=0, keepdims=True)
    first = is_even("row")
    spare = jnp.broadcast_to(diagonal, (8, HALF))
    mine_ref[0:HALF] = jnp.where(first, cross, folded)
    mine_ref[HALF:SUMMED] = spare
    other_ref[0:HALF] = jnp.where(first, folded, cross)
    other_ref[HALF:SUMMED] = spare
    edge = edge.astype(F32)
    passed = jnp.where(second_cells()[:8], edge[:8], pltpu.roll(edge[8:], 4, 0))
    passed_ref[0:8] = passed[:, :HALF]
    passed_ref[8:16] = passed[:, HALF:]


def inverse_factor(inner):
    count = MODES // 8
    shape = (8, 2 * MODES)
    i = lax.broadcasted_iota(jnp.int32, (MODES, MODES), 0)
    j = lax.broadcasted_iota(jnp.int32, (MODES, MODES), 1)
    work = jnp.concatenate([jnp.where(i == j, 1.0, 0.0), inner], axis=1)
    work = [work[8 * v : 8 * v + 8] for v in range(count)]
    sub = lax.broadcasted_iota(jnp.int32, shape, 0)

    def columns(b, first, last):
        lanes = [MODES + 8 * b + m for m in range(8)]
        return {v: [jnp.broadcast_to(work[v][:, k : k + 1], shape) for k in lanes] for v in range(first, last)}

    def spread(tile, row):
        return jnp.broadcast_to(tile[row : row + 1], shape)

    cols = columns(0, 0, count)
    done = []
    for b in range(count):
        near = min(count, b + 1 + AHEAD)
        ahead = columns(b + 1, b + 1, near)
        scale = jnp.ones(shape, F32)
        for m in range(8):
            lead = cols[b][m]
            pivot = spread(lead, m)
            inverse = 1.0 / pivot
            scale = jnp.where(sub == m, pivot, scale)
            row = spread(work[b], m) * inverse
            for q in range(m + 1, 8):
                times = spread(lead, q) * inverse
                for v in cols:
                    cols[v][q] = cols[v][q] - cols[v][m] * times
            for q in range(8 if ahead else 0):
                times = spread(cols[b + 1][m], q) * inverse
                for v in ahead:
                    ahead[v][q] = ahead[v][q] - cols[v][m] * times
            work[b] = work[b] - jnp.where(sub > m, lead, 0.0) * row
            for v in range(b + 1, count):
                work[v] = work[v] - cols[v][m] * row
        done.append(work[b] * lax.rsqrt(scale))
        cols = {**ahead, **columns(b + 1, near, count)}
    return jnp.concatenate(done, axis=0)[:, :MODES]


def basis_kernel(scale, mine_ref, other_ref, start_ref, inner_ref, edge_ref, before_ref, basis_ref, modes_ref, rows_ref, out_ref):
    first = is_even("row")
    mine, other = mine_ref[...], other_ref[...]
    cross = jnp.where(first, mine, other)[:HALF]
    second = jnp.where(first, other, mine)
    folded = second[:HALF]
    i = lax.broadcasted_iota(jnp.int32, (HALF, HALF), 0)
    j = lax.broadcasted_iota(jnp.int32, (HALF, HALF), 1)
    flipped = folded.T
    top = jnp.where(i <= j, folded, flipped)
    low = jnp.where(i > j, folded, jnp.where(i < j, flipped, second[HALF : HALF + 1]))
    gram = jnp.concatenate(
        [jnp.concatenate([top, cross], axis=1), jnp.concatenate([cross.T, low], axis=1)], axis=0
    )
    gram = gram * scale
    stacked = dot(start_ref[...], gram)
    for sweep in range(SWEEPS):
        inner = lax.dot_general(
            stacked, stacked, (((1,), (1,)), ((), ())), precision=HIGHEST, preferred_element_type=F32
        )
        if sweep < SWEEPS - 1:
            beside = dot(stacked, gram)
        else:
            beside = jnp.concatenate([stacked, dot(stacked, frame_order(1))], axis=1)
        stacked = dot(inverse_factor(inner), beside)
    basis = stacked[:, :FRAMES]
    basis_ref[...] = stacked[:, FRAMES:]
    twice = jnp.concatenate([basis, basis], axis=0)
    before = jnp.concatenate([before_ref[:8], before_ref[8:]], axis=1)
    before = jnp.concatenate([before, pltpu.roll(before, 4, 0)], axis=0)
    before = jnp.where(lax.axis_index("col") == 0, inner_ref[0].astype(F32), before)
    cell = jnp.where(second_cells(), before, edge_ref[...].astype(F32)).astype(BF16)
    flat = jnp.concatenate([inner_ref[1:].reshape(16 * BLOCKS - 16, FRAMES), cell], axis=0)
    rows_ref[...] = lax.dot_general(
        flat, twice.astype(BF16), (((1,), (1,)), ((), ())), preferred_element_type=F32
    )
    left = lax.broadcasted_iota(jnp.int32, (BLOCKS, 2 * MODES), 1) < MODES
    for row in range(2):
        for half in range(2):
            for cell in range(2):
                at = 8 * row + 4 * cell + 2 * half
                field = jnp.where(
                    left, rows_ref[pl.ds(at, BLOCKS, stride=16), :], rows_ref[pl.ds(at + 1, BLOCKS, stride=16), :]
                )
                if cell:
                    field = pltpu.roll(field, 1, 0)
                out_ref[pl.ds(64 * row + 32 * half + 1 - cell, BLOCKS, stride=2), :] = field
            modes_ref[row, :, 128 * half : 128 * half + 128] = out_ref[64 * row + 32 * half : 64 * row + 32 * half + 32]


def call(kernel, outs, n_in, scratch=()):
    return pl.pallas_call(
        kernel,
        out_shape=[jax.ShapeDtypeStruct(shape, dtype) for shape, dtype in outs],
        in_specs=[VMEM] * n_in,
        out_specs=[VMEM] * len(outs),
        scratch_shapes=list(scratch),
        compiler_params=PARAMS,
    )


def pairs(size, start):
    swaps = []
    for i in range(start, size - 1, 2):
        swaps += [(i, i + 1), (i + 1, i)]
    return swaps


def on_device(video, filters, start_basis):
    size_row, size_col = lax.axis_size("row"), lax.axis_size("col")
    near, far = pairs(size_row, 0), pairs(size_row, 1)
    to_left = [(i + 1, i) for i in range(size_col - 1)]

    across = [(a * size_col + i, b * size_col + j) for a, b in far for i, j in to_left]
    send = ((REACH * COLS + 16, FRAMES), BF16)
    tiles = ((BLOCKS + 1, 112, 3 * HALF), BF16)
    rows = (((FRAMES + 1) * ROWS, COLS), F32)
    rows, send_a, send_b, heads = call(send_kernel, [rows, send, send, ((8 * ROWS, FRAMES), F32)], 1)(video)
    got_a = lax.ppermute(send_a, "row", near)
    got_b = lax.ppermute(send_b, "row", far)
    outs = [((8 * ROWS + 8 * REACH, 3 * HALF), BF16), ((8 * REACH, 3 * HALF), BF16)]
    side, diag = call(side_kernel, outs, 3)(rows, heads, got_a)
    side = lax.ppermute(side, "col", to_left)
    diag = lax.ppermute(diag, ("row", "col"), across)

    outs = [((BLOCKS, 16, FRAMES), BF16), tiles, ((128, 256), BF16)]
    inner, x, band = call(inner_kernel, outs, 4, [pltpu.VMEM((16, 128), F32)])(
        got_a, got_b, rows, jnp.transpose(filters, (0, 2, 1, 3))
    )
    part, passed = ((SUMMED, HALF), F32), ((16, HALF), F32)
    edge, mine, other, passed = call(edge_kernel, [((16, FRAMES), BF16), part, part, passed], 5)(
        band, x, side, diag, inner
    )

    mine = mine + lax.ppermute(other, "row", near)
    step = 2
    while step < size_row:
        mine = mine + lax.ppermute(mine, "row", [(i, i ^ step) for i in range(size_row)])
        step *= 2
    mine = jnp.concatenate([mine, passed], axis=0)
    summed = lax.broadcasted_iota(jnp.int32, mine.shape, 0) < SUMMED
    step = 1
    col = lax.axis_index("col")
    before = jnp.zeros((16, HALF), F32)
    start = start_basis.T
    while step < size_col:
        if 2 * step >= size_col:
            mine, start = lax.optimization_barrier((mine, start))
            (start,) = call(start_kernel, [((MODES, FRAMES), F32)], 1)(start)
        got = lax.ppermute(mine, "col", [(i, i ^ step) for i in range(size_col)])
        mine = jnp.where(summed, mine + got, got)
        before = jnp.where((col & (2 * step - 1)) == step, got[SUMMED:], before)
        step *= 2
    mine = mine[:SUMMED]
    other = lax.ppermute(mine, "row", near)

    features = ORIENT * (size_row * ROWS // 4) * (size_col * COLS // 4)
    kernel = functools.partial(basis_kernel, 1.0 / features)
    basis, modes = call(
        kernel,
        [((MODES, FRAMES), F32), ((ROWS // 4, COLS // 4, ORIENT * MODES), F32)],
        6,
        [pltpu.VMEM((FRAMES, 2 * MODES), F32), pltpu.VMEM((128, 128), F32)],
    )(mine, other, start, inner, edge, before)
    return basis.T, modes


def solution(mesh):
    return jax.shard_map(
        on_device,
        mesh=mesh,
        in_specs=(P("grp", "row", "col"), P(), P()),
        out_specs=(P("grp", None), P(("grp", "row"), "col", None)),
        check_vma=False,
    )
```
